32 devices in a mesh: expert: 4 (over y, x), shard: 4 (over z), dp: 2 (over core).
Axes of the slice: x: 2, y: 2, z: 4, core: 2. Of those that a mesh axis runs over, the one named last changes fastest.
Arguments:
- tokens: bfloat16 [8, 2560, 1024], P(('expert', 'dp'), 'shard'), may hold values from -6 to 6
- teacher: bfloat16 [8, 2560, 1024], P(('expert', 'dp'), 'shard'), may hold values from -6 to 6
- seg_ids: int32 [8, 2560], P(('expert', 'dp')), may hold values from 0 to 12, as said below
- parents: int32 [8, 13], P(('expert', 'dp')), may hold values from 0 to 12, as said below
- depth: int32 [8, 2560], P(('expert', 'dp')), may hold values from 0 to 1279, as said below
- valid: int32 [8, 2560], P(('expert', 'dp')), may hold values from 0 to 1, as said below
- routes: int32 [8, 2560, 2], P(('expert', 'dp')), may hold values from 0 to 3, all different within a row; in each aligned block of 2560 rows (0 to 2559, 2560 to 5119, ..., all dimensions but the last counted through in order) at most 1600 rows name the same one
- norm1_gain: float32 [1024], replicated, may hold values from 0.5 to 1.5
- w_query: bfloat16 [1024, 1024], P(None, 'shard'), may hold values from -0.1875 to 0.1875
- w_key: bfloat16 [1024, 1024], P(None, 'shard'), may hold values from -0.1875 to 0.1875
- w_value: bfloat16 [1024, 1024], P(None, 'shard'), may hold values from -0.1875 to 0.1875
- w_out: bfloat16 [1024, 1024], P('shard'), may hold values from -3 to 3
- rel_bias: float32 [32, 16], P(None, 'shard'), may hold values from -4 to 4
- norm2_gain: float32 [1024], replicated, may hold values from 0.5 to 1.5
- router: float32 [1024, 4], replicated, may hold values from -0.12 to 0.12
- w_gate: bfloat16 [4, 1024, 2816], P('expert', None, 'shard'), may hold values from -0.1875 to 0.1875
- w_up: bfloat16 [4, 1024, 2816], P('expert', None, 'shard'), may hold values from -0.1875 to 0.1875
- w_down: bfloat16 [4, 2816, 1024], P('expert', 'shard'), may hold values from -0.21875 to 0.21875
Outputs:
- output: bfloat16 [8, 2560, 1024], P(('expert', 'dp'), 'shard')
- loss: float32 [], replicated
- grad_tokens: float32 [8, 2560, 1024], P(('expert', 'dp'), 'shard')
- grad_norm1: float32 [1024], replicated
- grad_query: float32 [1024, 1024], P(None, 'shard')
- grad_key: float32 [1024, 1024], P(None, 'shard')
- grad_value: float32 [1024, 1024], P(None, 'shard')
- grad_out: float32 [1024, 1024], P('shard')
- grad_bias: float32 [32, 16], P(None, 'shard')
- grad_norm2: float32 [1024], replicated
- grad_router: float32 [1024, 4], replicated
- grad_gate: float32 [4, 1024, 2816], P('expert', None, 'shard')
- grad_up: float32 [4, 1024, 2816], P('expert', None, 'shard')
- grad_down: float32 [4, 2816, 1024], P('expert', 'shard')
The draws below stay inside these ranges and needn't reach their ends.
Inputs may be any that keep to these rules, and one draw needn't show every extreme that they name: `seg_ids`: each tree is a trunk of 1024 positions, then 4 times a branch of 128 positions followed by its 2 leaves of 128 positions; each segment's positions form one run and carry one label. `parents`: for each segment label the label of the segment it grows from; the trunk names itself. Within a segment depth rises by one a position; a segment's first position has the number of valid positions of its ancestors. Each segment's valid positions come first and are 1 to all of its positions; the rest are padding. `routes`: among the 2560 tokens of one tree, no expert is named by more than 1600 tokens.
All inputs are finite; a program needn't handle non-finite values.
Results may differ from the reference program's by a relative error of at most 0.014.
Values may be sent and summed in bfloat16 or wider, within the bound.
A program may use at most 256 MiB of HBM per device.

```python
import math
import jax
import jax.numpy as jnp
import numpy as np
from jax import lax

D = 1024
HEADS = 16
HEAD_DIM = 64
FF = 2816
TOP = 2
BUCKETS = 32
MAX_DIST = 128
TRUNK = 1024
BRANCH = 128
LEAF = 128
NBRANCH = 4
NLEAF = 2
EXPERTS = 4
SEGS = 13
TREE_LEN = 2560
TREES = 8
TOKENS = 20480
CAP = 1600


def tree_layout(key):
    slot_sizes = [TRUNK]
    parent_slots = [0]
    leaf_flags = [0]
    for branch_number in range(NBRANCH):
        branch_slot = len(slot_sizes)
        slot_sizes.append(BRANCH)
        parent_slots.append(0)
        leaf_flags.append(0)
        for leaf_number in range(NLEAF):
            slot_sizes.append(LEAF)
            parent_slots.append(branch_slot)
            leaf_flags.append(1)
    slot_of_place = np.repeat(np.arange(SEGS), slot_sizes).astype(np.int32)
    offsets = np.concatenate([np.arange(size_value) for size_value in slot_sizes]).astype(np.int32)
    sizes_row = jnp.asarray(np.array(slot_sizes, np.int32))[None, :]
    tree_numbers = jnp.arange(TREES, dtype=jnp.int32)[:, None]
    lowest = jnp.maximum(sizes_row * (2 * (TREES - 1) + 8 * tree_numbers) // (10 * (TREES - 1)), 1)
    highest_len = jnp.minimum(lowest + sizes_row // 5, sizes_row)
    length_key, label_key = jax.random.split(key)
    lengths = jax.random.randint(length_key, (TREES, SEGS), lowest, highest_len + 1).astype(jnp.int32)
    parent_index = jnp.asarray(np.array(parent_slots, np.int32))
    leaf_mask = jnp.asarray(np.array(leaf_flags, np.int32))[None, :]
    trunk_mask = (jnp.arange(SEGS) == 0)[None, :]
    base_depth = jnp.where(trunk_mask, 0, lengths[:, parent_index] + leaf_mask * lengths[:, 0:1])
    place_slots = jnp.asarray(slot_of_place)
    place_offsets = jnp.asarray(offsets)[None, :]
    depth_values = (base_depth[:, place_slots] + place_offsets).astype(jnp.int32)
    valid_values = (place_offsets < lengths[:, place_slots]).astype(jnp.int32)

    def shuffle(label_seed):
        return jax.random.permutation(label_seed, SEGS)
    permutations = jax.vmap(shuffle)(jax.random.split(label_key, TREES)).astype(jnp.int32)
    segment_values = permutations[:, place_slots].astype(jnp.int32)
    inverse = jnp.argsort(permutations, axis=1)
    parent_values = jnp.take_along_axis(permutations, parent_index[inverse], axis=1).astype(jnp.int32)
    return (segment_values, parent_values, depth_values, valid_values)


def draw_seg_ids(key, part):
    return tree_layout(key)[0]


def draw_parents(key, part):
    return tree_layout(key)[1]


def draw_depth(key, part):
    return tree_layout(key)[2]


def draw_valid(key, part):
    return tree_layout(key)[3]


def shard_levels(rng, extent, cuts, least, high):
    def one(position, shards_of):
        heights = jax.random.uniform(jax.random.fold_in(jax.random.fold_in(rng, 6), position), (shards_of,), jnp.float32, least / len(cuts), high / len(cuts))
        return jnp.repeat(jnp.exp(heights), extent[position] // shards_of).reshape((-1,) + (1,) * (len(extent) - position - 1))

    level = one(*cuts[0])
    for cut in cuts[1:]:
        level = level * one(*cut)
    return level


def routed_block(stream_key, own, number, rows, number_of, top, limit, lean):
    ranking = jax.random.permutation(stream_key, number_of)
    crowded, ordinary = shares(number_of, rows * top, limit, lean, True), shares(number_of, rows * top, limit, lean, False)
    places = jnp.arange(number_of)

    def named(tallies, turn):
        used = int((tallies > 0).sum())
        fixed = max(1, used // 4)
        moved = fixed + (places - fixed + turn * (used - fixed)) % max(1, number_of - fixed)
        return jnp.zeros((number_of,), jnp.int32).at[ranking[jnp.where(places < fixed, places, moved)]].set(jnp.asarray(tallies, jnp.int32))

    tallies = jnp.where(number % 4 == 0, named(crowded, number // 4), named(ordinary, number - number // 4 - 1))
    mixed = jax.random.permutation(jax.random.fold_in(own, 3), number_of)
    donor, receiver = mixed[0:number_of // 2 * 2:2], mixed[1:number_of // 2 * 2:2]
    slack = jnp.minimum(tallies[donor] - 1, limit - tallies[receiver]) // 2
    slack = jnp.where((donor == ranking[0]) | (receiver == ranking[0]) | (tallies[receiver] == 0), 0, jnp.maximum(slack, 0))
    moved = jax.random.randint(jax.random.fold_in(own, 4), (number_of // 2,), 0, 1 << 20) % (slack + 1)
    tallies = tallies.at[donor].add(-moved).at[receiver].add(moved)
    labels = jnp.searchsorted(jnp.cumsum(tallies), jnp.arange(rows * top), side="right").astype(jnp.int32)
    listing = labels.reshape(top, rows).T
    listing = listing[jax.random.permutation(jax.random.fold_in(own, 1), rows)]
    turn = jax.random.randint(jax.random.fold_in(own, 2), (rows, 1), 0, top)
    return jnp.take_along_axis(listing, (jnp.arange(top)[None, :] + turn) % top, axis=1)


def shares(count, total, reach, skew, full):
    weights = [(1 << 20) // math.isqrt(rank ** skew) + 1 for rank in range(1, count + 1)]
    largest = reach if full else min(reach, max(-(-total // count), total * weights[0] // sum(weights)))
    least = 1 if total - largest >= count - 1 else 0
    holding, spare = [largest] + [least] * (count - 1), total - largest - least * (count - 1)
    while spare > 0:
        candidates = [i for i in range(1, count) if holding[i] < largest] or [i for i in range(1, count) if holding[i] < reach]
        pool, remaining = sum([weights[i] for i in candidates]), spare
        for i in candidates:
            addition = min(reach - holding[i], max(1, remaining * weights[i] // pool), spare)
            holding[i] = holding[i] + addition
            spare = spare - addition
    return np.array(holding)


def gaussian(own_key, shape, width, most, cuts=(), kind=jnp.bfloat16):
    values = jax.random.normal(own_key, shape, jnp.float32) * width
    if len(cuts) > 0:
        values = shard_levels(own_key, shape, cuts, -0.22, 0.18) * values
    return jnp.clip(values, min=-most, max=most).astype(kind)


def setup_inputs(seed: int = 0) -> dict:
    arg_keys = jax.random.split(jax.random.key(seed), 19)
    tokens = gaussian(arg_keys[0], (TREES, TREE_LEN, D), 1.0, 6.0, ((0, 8), (1, 4)))
    teacher = gaussian(arg_keys[1], (TREES, TREE_LEN, D), 1.0, 6.0, ((0, 8), (1, 4)))
    seg_ids = draw_seg_ids(jax.random.fold_in(arg_keys[18], 71), 0)
    parents = draw_parents(jax.random.fold_in(arg_keys[18], 71), 0)
    depth = draw_depth(jax.random.fold_in(arg_keys[18], 71), 0)
    valid = draw_valid(jax.random.fold_in(arg_keys[18], 71), 0)
    routes_keys = jax.random.split(jax.random.fold_in(arg_keys[6], 1), TREES * TREE_LEN // TREE_LEN)
    routes_turns = jax.random.permutation(jax.random.fold_in(arg_keys[6], 3), TREES * TREE_LEN // TREE_LEN)
    routes = jax.vmap(lambda own, number: routed_block(jax.random.fold_in(arg_keys[6], 2), own, number, TREE_LEN, EXPERTS, TOP, CAP, 1))(routes_keys, routes_turns).reshape((TREES, TREE_LEN, TOP))
    norm1_gain = jnp.clip(1.0 + 0.1 * jax.random.normal(arg_keys[7], (D,), jnp.float32), 0.5, 1.5)
    w_query = gaussian(arg_keys[8], (D, HEADS * HEAD_DIM), D ** -0.5, 0.1875, ((1, 4),))
    w_key = gaussian(arg_keys[9], (D, HEADS * HEAD_DIM), D ** -0.5, 0.1875, ((1, 4),))
    w_value = gaussian(arg_keys[10], (D, HEADS * HEAD_DIM), D ** -0.5, 0.1875, ((1, 4),))
    w_out = gaussian(arg_keys[11], (HEADS * HEAD_DIM, D), 4 ** -0.5, 3.0, ((0, 4),))
    rel_bias = gaussian(arg_keys[12], (BUCKETS, HEADS), 1.0, 4.0, ((1, 4),), jnp.float32)
    norm2_gain = jnp.clip(1.0 + 0.1 * jax.random.normal(arg_keys[13], (D,), jnp.float32), 0.5, 1.5)
    router = gaussian(arg_keys[14], (D, EXPERTS), 0.02, 0.12, (), jnp.float32)
    w_gate = gaussian(arg_keys[15], (EXPERTS, D, FF), D ** -0.5, 0.1875, ((0, 4), (2, 4)))
    w_up = gaussian(arg_keys[16], (EXPERTS, D, FF), D ** -0.5, 0.1875, ((0, 4), (2, 4)))
    w_down = gaussian(arg_keys[17], (EXPERTS, FF, D), (FF // 4) ** -0.5, 0.21875, ((0, 4), (1, 4)))
    return {"tokens": tokens, "teacher": teacher, "seg_ids": seg_ids, "parents": parents, "depth": depth, "valid": valid, "routes": routes, "norm1_gain": norm1_gain, "w_query": w_query, "w_key": w_key, "w_value": w_value, "w_out": w_out, "rel_bias": rel_bias, "norm2_gain": norm2_gain, "router": router, "w_gate": w_gate, "w_up": w_up, "w_down": w_down}


EPSILON = 1e-06
MASKED_SCORE = -1e+30
SCORE_SCALE = 0.125
HIGHEST_PRECISION = lax.Precision.HIGHEST

@jax.custom_vjp
def low(v):
    return lax.optimization_barrier(v.astype(jnp.bfloat16)).astype(jnp.float32)

@jax.custom_vjp
def low_back(v):
    return v

def low_keep(v):
    return (low(v), None)

def low_pass(kept, grad):
    return (grad,)

def back_keep(v):
    return (v, None)

def back_low(kept, grad):
    return (low(grad),)
low.defvjp(low_keep, low_pass)
low_back.defvjp(back_keep, back_low)

def bucket_index(distance):
    half_count = BUCKETS // 2
    counted = jnp.zeros_like(distance)
    for number in range(1, BUCKETS - half_count):
        border = math.ceil(half_count * (MAX_DIST / half_count) ** (number / (BUCKETS - half_count)))
        counted = counted + (distance >= border).astype(jnp.int32)
    return jnp.where(distance < half_count, distance, half_count + counted).astype(jnp.int32)

def routing_tables(route_rows):
    length = route_rows.shape[0]
    flat_routes = route_rows.reshape(-1).astype(jnp.int32)
    onehot_rows = (flat_routes[:, None] == jnp.arange(EXPERTS, dtype=jnp.int32)[None, :]).astype(jnp.int32)
    earlier = (jnp.cumsum(onehot_rows, axis=0) - onehot_rows).astype(jnp.int32)
    slots = lax.optimization_barrier(jnp.sum(earlier * onehot_rows, axis=1)).astype(jnp.int32)
    target = (flat_routes * CAP + slots).astype(jnp.int32)
    source = jnp.zeros((EXPERTS * CAP,), jnp.int32).at[target].set(jnp.arange(length * TOP, dtype=jnp.int32) + 1)
    return (target, source)

def tree_forward(weights, inputs, segment, parent_table, depths, validity, route_rows, target, source):
    norm1_gain, w_query, w_key, w_value, w_out, rel_bias, norm2_gain, router, w_gate, w_up, w_down = weights
    length = inputs.shape[0]
    scale_one = lax.rsqrt(lax.optimization_barrier(jnp.mean(inputs * inputs, axis=1, keepdims=True)) + EPSILON)
    normed_one = low(inputs * scale_one * norm1_gain)

    def project(matrix):
        projected = jnp.dot(normed_one, matrix, precision=HIGHEST_PRECISION)
        return low(low_back(projected)).reshape(length, HEADS, HEAD_DIM)
    query_rows = project(w_query)
    key_rows = project(w_key)
    value_rows = project(w_value)
    first_up = parent_table[segment]
    second_up = parent_table[first_up]
    block_rows = min(512, length)
    blocks = length // block_rows

    def attend(pieces):
        query_block, query_depth, query_seg, query_up, query_top = pieces
        raw_scores = jnp.einsum('qhd,khd->hqk', query_block, key_rows, precision=HIGHEST_PRECISION) * SCORE_SCALE
        distance = jnp.maximum(query_depth[:, None] - depths[None, :], 0)
        raw_scores = raw_scores + jnp.transpose(rel_bias[bucket_index(distance)], (2, 0, 1))
        allowed = (validity[None, :] > 0) & (depths[None, :] <= query_depth[:, None]) & ((segment[None, :] == query_seg[:, None]) | (segment[None, :] == query_up[:, None]) | (segment[None, :] == query_top[:, None]))
        scores = jnp.where(allowed[None], low_back(raw_scores), MASKED_SCORE)
        highest = lax.optimization_barrier(jnp.max(scores, axis=2, keepdims=True))
        shifted = jnp.exp(scores - highest)
        probs = shifted / lax.optimization_barrier(jnp.sum(shifted, axis=2, keepdims=True))
        return jnp.einsum('hqk,khd->qhd', low(probs), value_rows, precision=HIGHEST_PRECISION)
    attended = lax.map(jax.checkpoint(attend), (query_rows.reshape(blocks, block_rows, HEADS, HEAD_DIM), depths.reshape(blocks, block_rows), segment.reshape(blocks, block_rows), first_up.reshape(blocks, block_rows), second_up.reshape(blocks, block_rows)))
    attended = low(low_back(attended.reshape(length, HEADS * HEAD_DIM)))
    hidden = inputs + low_back(jnp.dot(attended, w_out, precision=HIGHEST_PRECISION))
    scale_two = lax.rsqrt(lax.optimization_barrier(jnp.mean(hidden * hidden, axis=1, keepdims=True)) + EPSILON)
    normed_two = low(hidden * scale_two * norm2_gain)
    logits = jnp.dot(normed_two, router, precision=HIGHEST_PRECISION)
    chosen = jnp.take_along_axis(logits, route_rows, axis=1)
    gates = jax.nn.softmax(chosen, axis=1)
    filled = (source > 0).astype(jnp.float32)
    slot_token = jnp.maximum(source - 1, 0) // TOP
    send_rows = (normed_two[slot_token] * filled[:, None]).reshape(EXPERTS, CAP, D)
    gate_pre = low_back(jnp.einsum('ecd,edf->ecf', send_rows, w_gate, precision=HIGHEST_PRECISION))
    up_pre = low_back(jnp.einsum('ecd,edf->ecf', send_rows, w_up, precision=HIGHEST_PRECISION))
    inner_low = low(jax.nn.gelu(gate_pre, approximate=True) * up_pre)
    expert_rows = low_back(jnp.einsum('ecf,efd->ecd', inner_low, w_down, precision=HIGHEST_PRECISION))
    picked = expert_rows.reshape(EXPERTS * CAP, D)[target].reshape(length, TOP, D)
    return hidden + lax.optimization_barrier(jnp.sum(gates[:, :, None] * picked, axis=1))

def reference(tokens, teacher, seg_ids, parents, depth, valid, routes, norm1_gain, w_query, w_key, w_value, w_out, rel_bias, norm2_gain, router, w_gate, w_up, w_down):
    params = tuple((weight_array.astype(jnp.float32) for weight_array in (norm1_gain, w_query, w_key, w_value, w_out, rel_bias, norm2_gain, router, w_gate, w_up, w_down)))
    valid_count = jnp.sum(valid).astype(jnp.float32)
    factor = TOKENS / valid_count

    def per_tree(running, pieces):
        grads_total, error_total = running
        tree_tokens, tree_teacher, tree_seg, tree_parents, tree_depth, tree_valid, tree_routes = pieces
        target, source = routing_tables(tree_routes)
        valid_float = tree_valid.astype(jnp.float32)

        def objective(weights, inputs):
            result = tree_forward(weights, inputs, tree_seg, tree_parents, tree_depth, tree_valid, tree_routes, target, source)
            error = result - tree_teacher.astype(jnp.float32)
            squares = jnp.sum(valid_float[:, None] * error * error)
            return (0.5 * factor * squares, (result, squares))
        objective_value, pullback, (result, squares) = jax.vjp(objective, params, tree_tokens.astype(jnp.float32), has_aux=True)
        weight_grads, input_grad = pullback(jnp.ones_like(objective_value))
        grads_total = jax.tree.map(jnp.add, grads_total, weight_grads)
        return ((grads_total, error_total + squares), (result.astype(jnp.bfloat16), input_grad))
    zero_grads = jax.tree.map(jnp.zeros_like, params)
    (grads, error_total), (outputs, input_grads) = lax.scan(per_tree, (zero_grads, jnp.zeros((), jnp.float32)), (tokens, teacher, seg_ids, parents, depth, valid, routes))
    loss = error_total / (D * valid_count)
    return (outputs, loss, input_grads, grads[0], grads[1], grads[2], grads[3], grads[4], grads[5], grads[6], grads[7], grads[8], grads[9], grads[10])
```

```python
import functools
import math

import jax
import jax.numpy as jnp
from jax import lax
from jax.experimental import pallas as pl
from jax.experimental.pallas import tpu as pltpu
from jax.sharding import PartitionSpec as P

TRUNK, SEGMENT, NBRANCH, NLEAF = 1024, 128, 4, 2
TILE = 128
TRUNK_TILES = TRUNK // TILE
HEAD_DIM = 64
MASKED = -1e30
DIAG, SUB, FAR, NONE, BRANCH_NEAR, LEAF_NEAR, LEAF_BRANCH = 0, 1, 2, 3, 4, 6, 14
CLASSES = 18
LIMIT_AT, OFFSET_AT = 0, 32


def head_rows(block, heads):
    lane = lax.broadcasted_iota(jnp.int32, block.shape, 1) // HEAD_DIM
    return jnp.concatenate(
        [jnp.where(lane == h, block, jnp.zeros((), block.dtype)) for h in range(heads)], axis=0
    )


def fill_bias(info, table, bias, heads):
    rows = lax.broadcasted_iota(jnp.int32, (TILE, TILE), 0)
    lanes = lax.broadcasted_iota(jnp.int32, (TILE, TILE), 1)

    def one(number, carry):
        place = jnp.clip(info[OFFSET_AT + number] + lanes - rows, 0, TILE - 1)
        hidden = ((number == DIAG) & (rows > lanes)) | (number == NONE)
        for h in range(heads):
            line = jnp.broadcast_to(table[h : h + 1, :], (TILE, TILE))
            values = jnp.take_along_axis(line, place, axis=1)
            bias[number, :, h * TILE : (h + 1) * TILE] = jnp.where(hidden, MASKED, values)
        return carry

    lax.fori_loop(0, CLASSES, one, 0)


def tile_plan(i, info):
    last = info[LIMIT_AT + 20]
    trunk = i < TRUNK_TILES
    place = jnp.maximum(i - TRUNK_TILES, 0)
    branch = place // (1 + NLEAF)
    leaf = (place % (1 + NLEAF)) > 0
    branch_tile = TRUNK_TILES + branch * (1 + NLEAF)
    near = jnp.where(trunk, i, last)
    tiles = jnp.minimum(near, last) + 1
    near_class = jnp.where(trunk, DIAG, jnp.where(leaf, LEAF_NEAR + branch, BRANCH_NEAR))
    next_class = jnp.where(trunk, SUB, jnp.where(leaf, LEAF_NEAR + NBRANCH + branch, BRANCH_NEAR + 1))
    trunk_steps = (tiles + 1) // 2
    steps = trunk_steps + jnp.where(trunk, 0, 1)
    tail = (
        (jnp.where(leaf, branch_tile, i), jnp.where(leaf, LEAF_BRANCH + branch, DIAG)),
        (i, jnp.where(leaf, DIAG, NONE)),
    )

    def tile_of(step, half):
        kt = step * 2 + half
        in_trunk = step < trunk_steps
        kind = jnp.where(
            kt == near, near_class, jnp.where(kt == near - 1, next_class, jnp.where(kt < near, FAR, NONE))
        )
        return jnp.where(in_trunk, kt, tail[half][0]), jnp.where(in_trunk, kind, tail[half][1])

    return steps, tile_of


def masked_scores(scores, half, tile, kind, info, bias, heads):
    rows = lax.broadcasted_iota(jnp.int32, (TILE, TILE), 0)
    shade = jnp.where(rows < info[LIMIT_AT + tile], 0.0, MASKED)
    shade = jnp.concatenate([shade] * heads, axis=1)
    return scores[half * TILE : (half + 1) * TILE] + bias[kind] + shade


def rows_at(ref, tile):
    return ref[pl.ds(pl.multiple_of(tile * TILE, TILE), TILE), :]


def lanes_at(ref, first, count, tile):
    return ref[first : first + count, pl.ds(pl.multiple_of(tile * TILE, TILE), TILE)]


def forward_kernel(info, table, q, k, v_t, out, log_total, bias, score, total_out, *, heads):
    i = pl.program_id(0)

    @pl.when(i == 0)
    def _():
        fill_bias(info, table, bias, heads)

    steps, tile_of = tile_plan(i, info)
    queries = head_rows(q[...] * jnp.bfloat16(0.125), heads)
    width = heads * TILE

    def first(step, highest):
        (ta, ka), (tb, kb) = tile_of(step, 0), tile_of(step, 1)
        keys = jnp.concatenate([rows_at(k, ta), rows_at(k, tb)], axis=0)
        raw = lax.dot_general(keys, queries, (((1,), (1,)), ((), ())), preferred_element_type=jnp.float32)
        both = jnp.concatenate(
            [masked_scores(raw, 0, ta, ka, info, bias, heads), masked_scores(raw, 1, tb, kb, info, bias, heads)],
            axis=0,
        )
        score[pl.ds(pl.multiple_of(step * 2 * TILE, 2 * TILE), 2 * TILE), :] = both
        return jnp.maximum(highest, jnp.max(both.reshape(2 * TILE // 8, 8, width), axis=0))

    highest = lax.fori_loop(0, steps, first, jnp.full((8, width), MASKED, jnp.float32))
    highest = jnp.max(highest, axis=0, keepdims=True)
    total_out[...] = jnp.zeros_like(total_out)
    pairs = heads // 2

    def second(step, total):
        (ta, _), (tb, _) = tile_of(step, 0), tile_of(step, 1)
        part = jnp.exp(score[pl.ds(pl.multiple_of(step * 2 * TILE, 2 * TILE), 2 * TILE), :] - highest)
        low = part.astype(jnp.bfloat16)
        for p in range(pairs):
            values = jnp.concatenate(
                [lanes_at(v_t, p * TILE, TILE, ta), lanes_at(v_t, p * TILE, TILE, tb)], axis=1
            )
            total_out[p] += jnp.dot(
                values, low[:, p * 2 * TILE : (p + 1) * 2 * TILE], preferred_element_type=jnp.float32
            )
        return total + jnp.sum(part.reshape(2 * TILE // 8, 8, width), axis=0)

    total = lax.fori_loop(0, steps, second, jnp.zeros((8, width), jnp.float32))
    total = jnp.sum(total, axis=0, keepdims=True)
    inverse = 1.0 / total
    for h in range(heads):
        p, odd = h // 2, h % 2
        block = total_out[p, odd * HEAD_DIM : (odd + 1) * HEAD_DIM, odd * TILE : (odd + 1) * TILE]
        out[h * HEAD_DIM : (h + 1) * HEAD_DIM, :] = (
            block * inverse[:, h * TILE : (h + 1) * TILE]
        ).astype(jnp.bfloat16)
    log_total[0] = highest + jnp.log(total)


def attention_forward(info, table, q, k, v_t):
    length, columns = q.shape
    heads = columns // HEAD_DIM
    tiles = length // TILE
    width = heads * TILE
    whole = lambda shape: pl.BlockSpec(shape, lambda i, info: (0,) * len(shape))
    return pl.pallas_call(
        functools.partial(forward_kernel, heads=heads),
        grid_spec=pltpu.PrefetchScalarGridSpec(
            num_scalar_prefetch=1,
            grid=(tiles,),
            in_specs=[
                whole(table.shape),
                pl.BlockSpec((TILE, columns), lambda i, info: (i, 0)),
                whole(k.shape),
                whole(v_t.shape),
            ],
            out_specs=[
                pl.BlockSpec((columns, TILE), lambda i, info: (0, i)),
                pl.BlockSpec((1, 1, width), lambda i, info: (i, 0, 0)),
            ],
            scratch_shapes=[
                pltpu.VMEM((CLASSES, TILE, width), jnp.float32),
                pltpu.VMEM((10 * TILE, width), jnp.float32),
                pltpu.VMEM((heads // 2, TILE, 2 * TILE), jnp.float32),
            ],
        ),
        out_shape=[
            jax.ShapeDtypeStruct((columns, length), jnp.bfloat16),
            jax.ShapeDtypeStruct((tiles, 1, width), jnp.float32),
        ],
        compiler_params=pltpu.CompilerParams(
            dimension_semantics=("arbitrary",), vmem_limit_bytes=50 << 20
        ),
        name="attention_forward",
    )(info, table, q, k, v_t)


def backward_kernel(
    info, table, q, k, k_t, v, grad, attended_t, log_total,
    grad_q, grad_k, grad_v, ahead, behind,
    bias, by_class, total_q, total_k, total_v, *, heads, tiles,
):
    i = pl.program_id(0)
    width = heads * TILE

    @pl.when(i == 0)
    def _():
        fill_bias(info, table, bias, heads)
        by_class[...] = jnp.zeros_like(by_class)
        total_k[...] = jnp.zeros_like(total_k)
        total_v[...] = jnp.zeros_like(total_v)

    steps, tile_of = tile_plan(i, info)
    queries = head_rows(q[...] * jnp.bfloat16(0.125), heads)
    grads = head_rows(grad[...], heads)
    product = jnp.transpose(grad[...].astype(jnp.float32)) * attended_t[...].astype(jnp.float32)
    centre = jnp.concatenate(
        [
            jnp.sum(product[h * HEAD_DIM : (h + 1) * HEAD_DIM], axis=0, keepdims=True)
            for h in range(heads)
        ],
        axis=1,
    )
    logs = log_total[0]
    total_q[...] = jnp.zeros_like(total_q)
    pairs = heads // 2

    def one(step, carry):
        (ta, ka), (tb, kb) = tile_of(step, 0), tile_of(step, 1)
        keys = jnp.concatenate([rows_at(k, ta), rows_at(k, tb)], axis=0)
        values = jnp.concatenate([rows_at(v, ta), rows_at(v, tb)], axis=0)
        raw = lax.dot_general(keys, queries, (((1,), (1,)), ((), ())), preferred_element_type=jnp.float32)
        both = jnp.concatenate(
            [masked_scores(raw, 0, ta, ka, info, bias, heads), masked_scores(raw, 1, tb, kb, info, bias, heads)],
            axis=0,
        )
        probs = jnp.exp(both - logs)
        grad_probs = lax.dot_general(
            values, grads, (((1,), (1,)), ((), ())), preferred_element_type=jnp.float32
        )
        grad_scores = probs * (grad_probs - centre)
        by_class[ka] += grad_scores[:TILE]
        by_class[kb] += grad_scores[TILE:]
        low = grad_scores.astype(jnp.bfloat16)
        value_part = jnp.dot(probs.astype(jnp.bfloat16), grads, preferred_element_type=jnp.float32)
        key_part = jnp.dot(low, queries, preferred_element_type=jnp.float32)
        for half, tile in ((0, ta), (1, tb)):
            at = pl.ds(pl.multiple_of(tile * TILE, TILE), TILE)
            total_v[at, :] += value_part[half * TILE : (half + 1) * TILE]
            total_k[at, :] += key_part[half * TILE : (half + 1) * TILE]
        for p in range(pairs):
            keys_t = jnp.concatenate(
                [lanes_at(k_t, p * TILE, TILE, ta), lanes_at(k_t, p * TILE, TILE, tb)], axis=1
            )
            total_q[p] += jnp.dot(
                keys_t, low[:, p * 2 * TILE : (p + 1) * 2 * TILE], preferred_element_type=jnp.float32
            )
        return carry

    lax.fori_loop(0, steps, one, 0)
    for h in range(heads):
        p, odd = h // 2, h % 2
        block = total_q[p, odd * HEAD_DIM : (odd + 1) * HEAD_DIM, odd * TILE : (odd + 1) * TILE]
        grad_q[h * HEAD_DIM : (h + 1) * HEAD_DIM, :] = (block * 0.125).astype(jnp.bfloat16)

    @pl.when(i == tiles - 1)
    def _():
        grad_k[...] = total_k[...].astype(jnp.bfloat16)
        grad_v[...] = total_v[...].astype(jnp.bfloat16)
        rows = lax.broadcasted_iota(jnp.int32, (TILE, TILE), 0)
        lanes = lax.broadcasted_iota(jnp.int32, (TILE, TILE), 1)

        def reduce(number, carry):
            for h in range(heads):
                block = by_class[number, :, h * TILE : (h + 1) * TILE]
                turned = jnp.take_along_axis(block, (rows + lanes) % TILE, axis=1)
                forward = jnp.sum(jnp.where(rows + lanes < TILE, turned, 0.0), axis=0, keepdims=True)
                wrapped = jnp.sum(jnp.where(rows + lanes < TILE, 0.0, turned), axis=0, keepdims=True)
                ahead[number, :, h * TILE : (h + 1) * TILE] = forward
                behind[number, :, h * TILE : (h + 1) * TILE] = wrapped
            return carry

        lax.fori_loop(0, CLASSES, reduce, 0)


def attention_backward(info, table, q, k, k_t, v, grad, attended_t, log_total):
    length, columns = q.shape
    heads = columns // HEAD_DIM
    tiles = length // TILE
    width = heads * TILE
    whole = lambda shape: pl.BlockSpec(shape, lambda i, info: (0,) * len(shape))
    rows = pl.BlockSpec((TILE, columns), lambda i, info: (i, 0))
    lanes = pl.BlockSpec((columns, TILE), lambda i, info: (0, i))
    return pl.pallas_call(
        functools.partial(backward_kernel, heads=heads, tiles=tiles),
        grid_spec=pltpu.PrefetchScalarGridSpec(
            num_scalar_prefetch=1,
            grid=(tiles,),
            in_specs=[
                whole(table.shape), rows, whole(k.shape), whole(k_t.shape), whole(v.shape), rows, lanes,
                pl.BlockSpec((1, 1, width), lambda i, info: (i, 0, 0)),
            ],
            out_specs=[
                lanes, whole(k.shape), whole(v.shape),
                whole((CLASSES, 1, width)), whole((CLASSES, 1, width)),
            ],
            scratch_shapes=[
                pltpu.VMEM((CLASSES, TILE, width), jnp.float32),
                pltpu.VMEM((CLASSES, TILE, width), jnp.float32),
                pltpu.VMEM((heads // 2, TILE, 2 * TILE), jnp.float32),
                pltpu.VMEM((length, columns), jnp.float32),
                pltpu.VMEM((length, columns), jnp.float32),
            ],
        ),
        out_shape=[
            jax.ShapeDtypeStruct((columns, length), jnp.bfloat16),
            jax.ShapeDtypeStruct((length, columns), jnp.bfloat16),
            jax.ShapeDtypeStruct((length, columns), jnp.bfloat16),
            jax.ShapeDtypeStruct((CLASSES, 1, width), jnp.float32),
            jax.ShapeDtypeStruct((CLASSES, 1, width), jnp.float32),
        ],
        compiler_params=pltpu.CompilerParams(
            dimension_semantics=("arbitrary",), vmem_limit_bytes=56 << 20
        ),
        name="attention_backward",
    )(info, table, q, k, k_t, v, grad, attended_t, log_total)


def bucket_index(distance, bucket_count, max_dist=128):
    half_count = bucket_count // 2
    counted = jnp.zeros_like(distance)
    for number in range(1, bucket_count - half_count):
        border = math.ceil(half_count * (max_dist / half_count) ** (number / (bucket_count - half_count)))
        counted = counted + (distance >= border).astype(jnp.int32)
    return jnp.where(distance < half_count, distance, half_count + counted)


def attention_info(validity):
    trunk = jnp.sum(validity[:TRUNK])
    lengths = jnp.sum(validity[TRUNK:].reshape(NBRANCH, 1 + NLEAF, SEGMENT), axis=2)
    last = (trunk - 1) // TILE
    limits = jnp.concatenate([trunk - TILE * jnp.arange(TRUNK_TILES), lengths.reshape(-1)])
    left = trunk - last * TILE
    branch = lengths[:, 0]
    offsets = jnp.concatenate(
        [
            jnp.array([0, TILE, 4096, 0]),
            jnp.stack([left, left + TILE]),
            left + branch,
            left + branch + TILE,
            branch,
        ]
    )
    info = jnp.zeros((64,), jnp.int32)
    info = info.at[:20].set(limits).at[20].set(last).at[OFFSET_AT : OFFSET_AT + CLASSES].set(offsets)
    return info, offsets


def bias_table(rel_bias):
    places = bucket_index(jnp.arange(TILE, dtype=jnp.int32), rel_bias.shape[0])
    pick = (places[:, None] == jnp.arange(rel_bias.shape[0])[None, :]).astype(jnp.float32)
    shifted = rel_bias - rel_bias[-1:]
    return jnp.einsum("db,bh->hd", pick, shifted, precision=lax.Precision.HIGHEST)


def bias_gradient(ahead, behind, offsets, bucket_count):
    heads = ahead.shape[2] // TILE
    lane = jnp.arange(TILE, dtype=jnp.int32)[None, :]
    distance = jnp.stack([offsets[:, None] + lane, offsets[:, None] + lane - TILE], axis=0)
    bucket = bucket_index(jnp.maximum(distance, 0), bucket_count)
    pick = (bucket[..., None] == jnp.arange(bucket_count)).astype(jnp.float32)
    sums = jnp.stack([ahead, behind], axis=0).reshape(2, CLASSES, heads, TILE)
    return jnp.einsum("sclb,schl->bh", pick, sums, precision=lax.Precision.HIGHEST)


EPSILON = 1e-06
SLOT_TILE = 256


def compact_kernel(bounds, slots, scale, rows, out):
    block = pl.program_id(0)

    @pl.when(block == 0)
    def _():
        out[...] = jnp.zeros_like(out)

    values = rows[0]
    if scale is not None:
        values = (scale[0] * values.astype(jnp.float32)).astype(jnp.bfloat16)
    count = values.shape[0]
    places = lax.broadcasted_iota(jnp.int32, (SLOT_TILE, count), 0)

    def one(tile, carry):
        pick = (slots[0] - tile * SLOT_TILE == places).astype(jnp.float32).astype(jnp.bfloat16)
        at = pl.ds(pl.multiple_of(tile * SLOT_TILE, SLOT_TILE), SLOT_TILE)
        part = jnp.dot(pick, values, preferred_element_type=jnp.float32)
        out[at, :] += part.astype(jnp.bfloat16)
        return carry

    lax.fori_loop(bounds[block] // SLOT_TILE, pl.cdiv(bounds[block + 1], SLOT_TILE), one, 0)


def compact(bounds, slots, rows, scale=None):
    blocks, count, width = rows.shape
    padded = pl.cdiv(blocks * count, SLOT_TILE) * SLOT_TILE
    specs = [
        pl.BlockSpec((1, 1, count), lambda b, bounds: (b, 0, 0)),
        pl.BlockSpec((1, count, 1), lambda b, bounds: (b, 0, 0)),
        pl.BlockSpec((1, count, width), lambda b, bounds: (b, 0, 0)),
    ]
    body = compact_kernel
    operands = (slots.reshape(blocks, 1, count), scale, rows)
    if scale is None:
        body = lambda bounds, slots, rows, out: compact_kernel(bounds, slots, None, rows, out)
        specs = [specs[0], specs[2]]
        operands = (operands[0], rows)
    return pl.pallas_call(
        body,
        grid_spec=pltpu.PrefetchScalarGridSpec(
            num_scalar_prefetch=1,
            grid=(blocks,),
            in_specs=specs,
            out_specs=pl.BlockSpec(
                (padded, width), lambda b, bounds: (0, 0), pipeline_mode=pl.Buffered(1)
            ),
        ),
        out_shape=jax.ShapeDtypeStruct((padded, width), jnp.bfloat16),
        compiler_params=pltpu.CompilerParams(vmem_limit_bytes=48 << 20),
        name="compact",
    )(bounds, *operands)


def expand_kernel(bounds, slots, rows, out):
    block = pl.program_id(0)
    count = out.shape[1]
    out[0] = jnp.zeros(out.shape[1:], out.dtype)
    places = lax.broadcasted_iota(jnp.int32, (count, SLOT_TILE), 1)

    def one(tile, carry):
        pick = (slots[0] - tile * SLOT_TILE == places).astype(jnp.float32).astype(jnp.bfloat16)
        at = pl.ds(pl.multiple_of(tile * SLOT_TILE, SLOT_TILE), SLOT_TILE)
        part = jnp.dot(pick, rows[at, :].astype(jnp.bfloat16), preferred_element_type=jnp.float32)
        out[0] += part.astype(jnp.bfloat16)
        return carry

    lax.fori_loop(bounds[block] // SLOT_TILE, pl.cdiv(bounds[block + 1], SLOT_TILE), one, 0)


def expand(bounds, slots, rows):
    blocks, count = slots.shape
    padded, width = rows.shape
    return pl.pallas_call(
        expand_kernel,
        grid_spec=pltpu.PrefetchScalarGridSpec(
            num_scalar_prefetch=1,
            grid=(blocks,),
            in_specs=[
                pl.BlockSpec((1, count, 1), lambda b, bounds: (b, 0, 0)),
                pl.BlockSpec((padded, width), lambda b, bounds: (0, 0), pipeline_mode=pl.Buffered(1)),
            ],
            out_specs=pl.BlockSpec((1, count, width), lambda b, bounds: (b, 0, 0)),
        ),
        out_shape=jax.ShapeDtypeStruct((blocks, count, width), jnp.bfloat16),
        compiler_params=pltpu.CompilerParams(vmem_limit_bytes=48 << 20),
        name="expand",
    )(bounds, slots.reshape(blocks, count, 1), rows)


GELU_IN = math.sqrt(2.0 / math.pi)
GELU_CUBE = 0.044715


def gelu_parts(pre):
    square = pre * pre
    bent = jnp.tanh(GELU_IN * pre * (1.0 + GELU_CUBE * square))
    half = 0.5 * (1.0 + bent)
    return pre * half, half, bent, square


def expert_forward_kernel(bounds, rows, gate_w, up_w, down_w, total):
    step = pl.program_id(0)
    columns = gate_w.shape[-1]
    width = rows.shape[1]

    def one(tile, carry):
        at = pl.ds(pl.multiple_of(tile * SLOT_TILE, SLOT_TILE), SLOT_TILE)
        values = rows[at, :]
        gate_pre = jnp.dot(values, gate_w[...].reshape(width, columns), preferred_element_type=jnp.float32)
        up_pre = jnp.dot(values, up_w[...].reshape(width, columns), preferred_element_type=jnp.float32)
        inner = (gelu_parts(gate_pre)[0] * up_pre).astype(jnp.bfloat16)
        part = jnp.dot(inner, down_w[...].reshape(columns, width), preferred_element_type=jnp.float32)

        @pl.when(step == 0)
        def _():
            total[at, :] = part

        @pl.when(step > 0)
        def _():
            total[at, :] += part

        return carry

    lax.fori_loop(0, pl.cdiv(bounds[bounds.shape[0] - 1], SLOT_TILE), one, 0)


def weight_spec(array):
    halves, shards, rows, columns = array.shape
    return pl.BlockSpec((halves, 1, rows, columns), lambda s, bounds: (0, s, 0, 0))


def expert_forward(bounds, rows, gate_w, up_w, down_w):
    padded, width = rows.shape
    whole = pl.BlockSpec((padded, width), lambda s, bounds: (0, 0), pipeline_mode=pl.Buffered(1))
    return pl.pallas_call(
        expert_forward_kernel,
        grid_spec=pltpu.PrefetchScalarGridSpec(
            num_scalar_prefetch=1,
            grid=(gate_w.shape[1],),
            in_specs=[whole, weight_spec(gate_w), weight_spec(up_w), weight_spec(down_w)],
            out_specs=whole,
        ),
        out_shape=jax.ShapeDtypeStruct((padded, width), jnp.float32),
        compiler_params=pltpu.CompilerParams(vmem_limit_bytes=56 << 20),
        name="expert_forward",
    )(bounds, rows, gate_w, up_w, down_w)


def expert_backward_kernel(
    bounds, rows, grads, gate_w, up_w, down_w,
    gate_out, up_out, down_out, total,
    gate_total, up_total, down_total,
):
    step = pl.program_id(0)
    columns = gate_w.shape[-1]
    width = rows.shape[1]
    gate_total[...] = jnp.zeros_like(gate_total)
    up_total[...] = jnp.zeros_like(up_total)
    down_total[...] = jnp.zeros_like(down_total)
    first = (((0,), (0,)), ((), ()))
    last = (((1,), (1,)), ((), ()))

    def one(tile, carry):
        at = pl.ds(pl.multiple_of(tile * SLOT_TILE, SLOT_TILE), SLOT_TILE)
        values, upstream = rows[at, :], grads[at, :]
        gate_m = gate_w[...].reshape(width, columns)
        up_m = up_w[...].reshape(width, columns)
        down_m = down_w[...].reshape(columns, width)
        gate_pre = jnp.dot(values, gate_m, preferred_element_type=jnp.float32)
        up_pre = jnp.dot(values, up_m, preferred_element_type=jnp.float32)
        grad_inner = lax.dot_general(upstream, down_m, last, preferred_element_type=jnp.float32)
        active, half, bent, square = gelu_parts(gate_pre)
        slope = half + (0.5 * GELU_IN) * gate_pre * (1.0 - bent * bent) * (1.0 + 3.0 * GELU_CUBE * square)
        inner = (active * up_pre).astype(jnp.bfloat16)
        grad_gate = (grad_inner * up_pre * slope).astype(jnp.bfloat16)
        grad_up = (grad_inner * active).astype(jnp.bfloat16)
        down_total[...] += lax.dot_general(inner, upstream, first, preferred_element_type=jnp.float32)
        gate_total[...] += lax.dot_general(values, grad_gate, first, preferred_element_type=jnp.float32)
        up_total[...] += lax.dot_general(values, grad_up, first, preferred_element_type=jnp.float32)
        part = lax.dot_general(grad_gate, gate_m, last, preferred_element_type=jnp.float32)
        part = part + lax.dot_general(grad_up, up_m, last, preferred_element_type=jnp.float32)

        @pl.when(step == 0)
        def _():
            total[at, :] = part

        @pl.when(step > 0)
        def _():
            total[at, :] += part

        return carry

    lax.fori_loop(0, pl.cdiv(bounds[bounds.shape[0] - 1], SLOT_TILE), one, 0)
    gate_out[0] = gate_total[...].astype(jnp.bfloat16)
    up_out[0] = up_total[...].astype(jnp.bfloat16)
    down_out[0] = down_total[...].astype(jnp.bfloat16)


def expert_backward(bounds, rows, grads, gate_w, up_w, down_w):
    padded, width = rows.shape
    shards, columns = gate_w.shape[1], gate_w.shape[3]
    whole = pl.BlockSpec((padded, width), lambda s, bounds: (0, 0), pipeline_mode=pl.Buffered(1))
    wide = pl.BlockSpec((1, width, columns), lambda s, bounds: (s, 0, 0))
    tall = pl.BlockSpec((1, columns, width), lambda s, bounds: (s, 0, 0))
    return pl.pallas_call(
        expert_backward_kernel,
        grid_spec=pltpu.PrefetchScalarGridSpec(
            num_scalar_prefetch=1,
            grid=(shards,),
            in_specs=[whole, whole, weight_spec(gate_w), weight_spec(up_w), weight_spec(down_w)],
            out_specs=[wide, wide, tall, whole],
            scratch_shapes=[
                pltpu.VMEM((width, columns), jnp.float32),
                pltpu.VMEM((width, columns), jnp.float32),
                pltpu.VMEM((columns, width), jnp.float32),
            ],
        ),
        out_shape=[
            jax.ShapeDtypeStruct((shards, width, columns), jnp.bfloat16),
            jax.ShapeDtypeStruct((shards, width, columns), jnp.bfloat16),
            jax.ShapeDtypeStruct((shards, columns, width), jnp.bfloat16),
            jax.ShapeDtypeStruct((padded, width), jnp.float32),
        ],
        compiler_params=pltpu.CompilerParams(vmem_limit_bytes=60 << 20),
        name="expert_backward",
    )(bounds, rows, grads, gate_w, up_w, down_w)


def split_float(values):
    high = values.astype(jnp.bfloat16)
    rest = values - high.astype(jnp.float32)
    middle = rest.astype(jnp.bfloat16)
    low = (rest - middle.astype(jnp.float32)).astype(jnp.bfloat16)
    return jnp.concatenate([high, middle, low], axis=1)


def join_float(products, count):
    return products[:, 2 * count :] + products[:, count : 2 * count] + products[:, :count]


def gather_weight(weight):
    cores = lax.axis_size("dp")
    half = weight.shape[0] // cores
    mine = lax.dynamic_slice_in_dim(weight, lax.axis_index("dp") * half, half, 0)
    return lax.all_gather(lax.all_gather(mine, "shard", axis=0), "dp", axis=0)


def scatter_weight_grad(parts):
    cores = lax.axis_size("dp")
    shards, rows, columns = parts.shape
    parts = parts.reshape(shards, cores, rows // cores, columns)
    mine = lax.psum_scatter(parts, "dp", scatter_dimension=1, tiled=False)
    mine = lax.psum_scatter(mine, "shard", scatter_dimension=0, tiled=False)
    return lax.all_gather(mine, "dp", axis=0, tiled=True).astype(jnp.float32)


def on_device(
    tokens, teacher, seg_ids, parents, depth, valid, routes, norm1_gain, w_query, w_key, w_value,
    w_out, rel_bias, norm2_gain, router, w_gate, w_up, w_down,
):
    shard_index = lax.axis_index("shard")
    expert_index = lax.axis_index("expert")
    shards = lax.axis_size("shard")
    columns = lax.axis_size("expert")
    experts = columns * w_gate.shape[0]
    token_rows = tokens[0].astype(jnp.float32)
    local_rows, width = token_rows.shape
    length = seg_ids.shape[1]
    heads_here = rel_bias.shape[1]
    bucket_count = rel_bias.shape[0]
    validity = valid[0]
    route_rows = routes[0]
    head_columns = w_query.shape[1]

    row_start = shard_index * local_rows
    valid_local = lax.dynamic_slice_in_dim(validity, row_start, local_rows, 0).astype(jnp.float32)
    route_local = lax.dynamic_slice_in_dim(route_rows, row_start, local_rows, 0)

    scale_one = lax.rsqrt(jnp.mean(token_rows * token_rows, axis=1, keepdims=True) + EPSILON)
    base_one = token_rows * scale_one
    normed_one = (base_one * norm1_gain).astype(jnp.bfloat16)
    normed_all = lax.all_gather(normed_one, "shard", axis=0, tiled=True)
    out_all = lax.all_gather(w_out, "shard", axis=0, tiled=True)
    gate_all = gather_weight(w_gate[0])
    up_all = gather_weight(w_up[0])
    down_all = gather_weight(w_down[0])
    valid_total = lax.psum(jnp.sum(validity), ("expert", "dp")).astype(jnp.float32)

    route_all = lax.all_gather(route_local, "expert", axis=0)
    taken = jnp.any(route_all == expert_index, axis=2)
    order = jnp.cumsum(taken.reshape(-1).astype(jnp.int32))
    slots = jnp.where(taken, order.reshape(taken.shape) - 1, -1)
    bounds = jnp.concatenate([jnp.zeros((1,), jnp.int32), order[local_rows - 1 :: local_rows]])

    info, offsets = attention_info(validity)
    table = bias_table(rel_bias)
    weights = jnp.concatenate([w_query, w_key, w_value], axis=1)
    projected = jnp.dot(normed_all, weights, preferred_element_type=jnp.float32).astype(jnp.bfloat16)
    query_rows, key_rows, value_rows = jnp.split(projected, 3, axis=1)
    attended_t, log_totals = attention_forward(info, table, query_rows, key_rows, value_rows.T)

    pieces = attended_t.reshape(head_columns, shards, local_rows).transpose(1, 0, 2)
    pieces = lax.all_to_all(pieces, "shard", split_axis=0, concat_axis=0, tiled=True)
    attended_here = pieces.reshape(shards * head_columns, local_rows)
    update = lax.dot_general(
        attended_here, out_all, (((0,), (0,)), ((), ())), preferred_element_type=jnp.float32
    )
    hidden = token_rows + update
    scale_two = lax.rsqrt(jnp.mean(hidden * hidden, axis=1, keepdims=True) + EPSILON)
    base_two = hidden * scale_two
    normed_two = (base_two * norm2_gain).astype(jnp.bfloat16)

    expert_ids = jnp.arange(experts, dtype=jnp.int32)
    router_pieces = split_float(router)

    def gates_of(rows, named):
        logits = join_float(jnp.dot(rows, router_pieces, preferred_element_type=jnp.float32), experts)
        match = named[:, :, None] == expert_ids[None, None, :]
        chosen = jnp.sum(jnp.where(match, logits[:, None, :], 0.0), axis=2)
        return jax.nn.softmax(chosen, axis=1), match

    gates, route_match = gates_of(normed_two, route_local)
    normed_layer = lax.all_gather(normed_two, "expert", axis=0)
    route_flat = route_all.reshape(columns * local_rows, -1)
    gates_layer, _ = gates_of(normed_layer.reshape(columns * local_rows, width), route_flat)
    gate_here = jnp.sum(jnp.where(route_flat == expert_index, gates_layer, 0.0), axis=1)
    gate_here = gate_here.reshape(columns, local_rows, 1)
    expert_rows = compact(bounds, slots, normed_layer)
    produced = expert_forward(bounds, expert_rows, gate_all, up_all, down_all)
    produced_layer = expand(bounds, slots, produced)
    shares = (gate_here * produced_layer.astype(jnp.float32)).astype(jnp.bfloat16)
    combined = lax.psum_scatter(shares, "expert", scatter_dimension=0, tiled=False).astype(jnp.float32)

    output_rows = hidden + combined
    factor = length * columns * lax.axis_size("dp") / valid_total
    error = output_rows - teacher[0].astype(jnp.float32)
    error_sum = jnp.sum(valid_local[:, None] * error * error)
    grad_output = valid_local[:, None] * error * factor
    grad_layer = lax.all_gather(grad_output.astype(jnp.bfloat16), "expert", axis=0)
    gate_grads = jnp.sum(grad_layer.astype(jnp.float32) * produced_layer.astype(jnp.float32), axis=2)
    gate_grads = lax.all_to_all(gate_grads, "expert", split_axis=0, concat_axis=0, tiled=True)
    grad_rows = compact(bounds, slots, grad_layer, gate_here)
    gate_part, up_part, down_part, rows_grad = expert_backward(
        bounds, expert_rows, grad_rows, gate_all, up_all, down_all
    )
    expert_back = lax.psum_scatter(
        expand(bounds, slots, rows_grad), "expert", scatter_dimension=0, tiled=False
    ).astype(jnp.float32)
    gate_grad = scatter_weight_grad(gate_part)
    up_grad = scatter_weight_grad(up_part)
    down_grad = scatter_weight_grad(down_part)

    grad_gates = jnp.sum(jnp.where(route_match, gate_grads.T[:, None, :], 0.0), axis=2)
    weighted = jnp.sum(gates * grad_gates, axis=1, keepdims=True)
    grad_chosen = gates * (grad_gates - weighted)
    grad_logits = jnp.sum(jnp.where(route_match, grad_chosen[:, :, None], 0.0), axis=1)
    router_grad = join_float(
        lax.dot_general(
            normed_two, split_float(grad_logits), (((0,), (0,)), ((), ())),
            preferred_element_type=jnp.float32,
        ),
        experts,
    )
    grad_normed_two = expert_back
    for number in range(experts):
        grad_normed_two = grad_normed_two + grad_logits[:, number : number + 1] * router[:, number][None]
    grad_base_two = grad_normed_two * norm2_gain
    norm2_grad = jnp.sum(grad_normed_two * base_two, axis=0)
    grad_hidden = grad_output + scale_two * (
        grad_base_two - base_two * jnp.mean(grad_base_two * base_two, axis=1, keepdims=True)
    )
    grad_update = grad_hidden.astype(jnp.bfloat16)
    out_grad = jnp.dot(attended_here, grad_update, preferred_element_type=jnp.float32)
    grad_heads = lax.dot_general(
        grad_update, out_all, (((1,), (1,)), ((), ())), preferred_element_type=jnp.float32
    ).astype(jnp.bfloat16)
    grad_heads = grad_heads.reshape(local_rows, shards, head_columns).transpose(1, 0, 2)
    grad_attended = lax.all_to_all(
        grad_heads, "shard", split_axis=0, concat_axis=0, tiled=True
    ).reshape(length, head_columns)

    grad_queries_t, grad_keys, grad_values, ahead, behind = attention_backward(
        info, table, query_rows, key_rows, key_rows.T, value_rows, grad_attended, attended_t, log_totals
    )
    bias_grad = bias_gradient(ahead, behind, offsets, bucket_count)
    across = (((0,), (0,)), ((), ()))
    grad_three = jnp.concatenate([grad_queries_t.T, grad_keys, grad_values], axis=1)
    three_wgrad = lax.dot_general(normed_all, grad_three, across, preferred_element_type=jnp.float32)
    grad_normed_all = lax.dot_general(
        grad_three, weights, (((1,), (1,)), ((), ())), preferred_element_type=jnp.float32
    )
    grad_normed_one = lax.psum_scatter(
        grad_normed_all.astype(jnp.bfloat16), "shard", scatter_dimension=0, tiled=True
    ).astype(jnp.float32)
    grad_base_one = grad_normed_one * norm1_gain
    norm1_grad = jnp.sum(grad_normed_one * base_one, axis=0)
    grad_tokens = grad_hidden + scale_one * (
        grad_base_one - base_one * jnp.mean(grad_base_one * base_one, axis=1, keepdims=True)
    )
    out_grad = lax.psum_scatter(
        out_grad.astype(jnp.bfloat16), "shard", scatter_dimension=0, tiled=True
    )
    three_wgrad, out_grad, bias_grad = lax.psum(
        (three_wgrad.astype(jnp.bfloat16), out_grad, bias_grad.astype(jnp.bfloat16)), ("expert", "dp")
    )
    three_wgrad, out_grad, bias_grad = (
        value.astype(jnp.float32) for value in (three_wgrad, out_grad, bias_grad)
    )
    query_wgrad, key_wgrad, value_wgrad = jnp.split(three_wgrad, 3, axis=1)
    router_grad, norm1_grad, norm2_grad, error_total = lax.psum(
        (router_grad, norm1_grad, norm2_grad, error_sum), ("expert", "shard", "dp")
    )
    loss = error_total / (width * valid_total)
    return (
        output_rows.astype(jnp.bfloat16)[None],
        loss,
        grad_tokens[None],
        norm1_grad,
        query_wgrad,
        key_wgrad,
        value_wgrad,
        out_grad,
        bias_grad,
        norm2_grad,
        router_grad,
        gate_grad[None],
        up_grad[None],
        down_grad[None],
    )


def solution(mesh):
    in_specs = (
        P(("expert", "dp"), "shard", None),
        P(("expert", "dp"), "shard", None),
        P(("expert", "dp"), None),
        P(("expert", "dp"), None),
        P(("expert", "dp"), None),
        P(("expert", "dp"), None),
        P(("expert", "dp"), None, None),
        P(),
        P(None, "shard"),
        P(None, "shard"),
        P(None, "shard"),
        P("shard", None),
        P(None, "shard"),
        P(),
        P(),
        P("expert", None, "shard"),
        P("expert", None, "shard"),
        P("expert", "shard", None),
    )
    out_specs = (
        P(("expert", "dp"), "shard", None),
        P(),
        P(("expert", "dp"), "shard", None),
        P(),
        P(None, "shard"),
        P(None, "shard"),
        P(None, "shard"),
        P("shard", None),
        P(None, "shard"),
        P(),
        P(),
        P("expert", None, "shard"),
        P("expert", None, "shard"),
        P("expert", "shard", None),
    )
    return jax.shard_map(
        on_device, mesh=mesh, in_specs=in_specs, out_specs=out_specs, check_vma=False
    )
```

```python
import functools
import math

import jax
import jax.numpy as jnp
from jax import lax
from jax.experimental import pallas as pl
from jax.experimental.pallas import tpu as pltpu
from jax.sharding import PartitionSpec as P

TRUNK, SEGMENT, NBRANCH, NLEAF = 1024, 128, 4, 2
TILE = 128
TRUNK_TILES = TRUNK // TILE
HEAD_DIM = 64
MASKED = -1e30
DIAG, SUB, FAR, NONE, BRANCH_NEAR, LEAF_NEAR, LEAF_BRANCH = 0, 1, 2, 3, 4, 6, 14
CLASSES = 18
LIMIT_AT, OFFSET_AT = 0, 32


def head_rows(block, heads):
    lane = lax.broadcasted_iota(jnp.int32, block.shape, 1) // HEAD_DIM
    return jnp.concatenate(
        [jnp.where(lane == h, block, jnp.zeros((), block.dtype)) for h in range(heads)], axis=0
    )


def fill_bias(info, table, bias, heads):
    rows = lax.broadcasted_iota(jnp.int32, (TILE, TILE), 0)
    lanes = lax.broadcasted_iota(jnp.int32, (TILE, TILE), 1)

    def one(number, carry):
        place = jnp.clip(info[OFFSET_AT + number] + lanes - rows, 0, TILE - 1)
        hidden = ((number == DIAG) & (rows > lanes)) | (number == NONE)
        for h in range(heads):
            line = jnp.broadcast_to(table[h : h + 1, :], (TILE, TILE))
            values = jnp.take_along_axis(line, place, axis=1)
            bias[number, :, h * TILE : (h + 1) * TILE] = jnp.where(hidden, MASKED, values)
        return carry

    lax.fori_loop(0, CLASSES, one, 0)


def tile_plan(i, info):
    last = info[LIMIT_AT + 20]
    trunk = i < TRUNK_TILES
    place = jnp.maximum(i - TRUNK_TILES, 0)
    branch = place // (1 + NLEAF)
    leaf = (place % (1 + NLEAF)) > 0
    branch_tile = TRUNK_TILES + branch * (1 + NLEAF)
    near = jnp.where(trunk, i, last)
    near_class = jnp.where(trunk, DIAG, jnp.where(leaf, LEAF_NEAR + branch, BRANCH_NEAR))
    next_class = jnp.where(trunk, SUB, jnp.where(leaf, LEAF_NEAR + NBRANCH + branch, BRANCH_NEAR + 1))
    trunk_steps = TRUNK_TILES // 2
    tail = (
        (jnp.where(leaf, branch_tile, i), jnp.where(leaf, LEAF_BRANCH + branch, DIAG)),
        (i, jnp.where(leaf, DIAG, NONE)),
    )

    def tile_of(step, half):
        kt = step * 2 + half
        in_trunk = trunk | (step < trunk_steps)
        kind = jnp.where(
            kt == near, near_class, jnp.where(kt == near - 1, next_class, jnp.where(kt < near, FAR, NONE))
        )
        return jnp.where(in_trunk, kt, tail[half][0]), jnp.where(in_trunk, kind, tail[half][1])

    return tile_of


def by_steps(i, run):
    for count in range(1, TRUNK_TILES // 2 + 1):

        @pl.when((i < TRUNK_TILES) & (i // 2 == count - 1))
        def _(count=count):
            run(count)

    @pl.when(i >= TRUNK_TILES)
    def _():
        run(TRUNK_TILES // 2 + 1)


def masked_scores(scores, half, tile, kind, info, bias, heads):
    rows = lax.broadcasted_iota(jnp.int32, (TILE, TILE), 0)
    shade = jnp.where(rows < info[LIMIT_AT + tile], 0.0, MASKED)
    shade = jnp.concatenate([shade] * heads, axis=1)
    return scores[half * TILE : (half + 1) * TILE] + bias[kind] + shade


def rows_at(ref, tile):
    return ref[pl.ds(pl.multiple_of(tile * TILE, TILE), TILE), :]


def lanes_at(ref, first, count, tile):
    return ref[first : first + count, pl.ds(pl.multiple_of(tile * TILE, TILE), TILE)]


def forward_kernel(info, table, q, k, v_t, out, log_total, bias, score, total_out, *, heads):
    i = pl.program_id(0)

    @pl.when(i == 0)
    def _():
        fill_bias(info, table, bias, heads)

    tile_of = tile_plan(i, info)
    queries = head_rows(q[...] * jnp.bfloat16(0.125), heads)
    width = heads * TILE

    def first(step, highest):
        (ta, ka), (tb, kb) = tile_of(step, 0), tile_of(step, 1)
        keys = jnp.concatenate([rows_at(k, ta), rows_at(k, tb)], axis=0)
        raw = lax.dot_general(keys, queries, (((1,), (1,)), ((), ())), preferred_element_type=jnp.float32)
        both = jnp.concatenate(
            [masked_scores(raw, 0, ta, ka, info, bias, heads), masked_scores(raw, 1, tb, kb, info, bias, heads)],
            axis=0,
        )
        score[step * 2 * TILE : (step + 1) * 2 * TILE, :] = both
        return jnp.maximum(highest, jnp.max(both.reshape(2 * TILE // 8, 8, width), axis=0))

    pairs = heads // 2

    def run(steps):
        highest = jnp.full((8, width), MASKED, jnp.float32)
        for step in range(steps):
            highest = first(step, highest)
        highest = jnp.max(highest, axis=0, keepdims=True)
        total = jnp.zeros((8, width), jnp.float32)
        for step in range(steps):
            (ta, _), (tb, _) = tile_of(step, 0), tile_of(step, 1)
            part = jnp.exp(score[step * 2 * TILE : (step + 1) * 2 * TILE, :] - highest)
            low = part.astype(jnp.bfloat16)
            for p in range(pairs):
                values = jnp.concatenate(
                    [lanes_at(v_t, p * TILE, TILE, ta), lanes_at(v_t, p * TILE, TILE, tb)], axis=1
                )
                product = jnp.dot(
                    values, low[:, p * 2 * TILE : (p + 1) * 2 * TILE], preferred_element_type=jnp.float32
                )
                if step == 0:
                    total_out[p] = product
                else:
                    total_out[p] += product
            total = total + jnp.sum(part.reshape(2 * TILE // 8, 8, width), axis=0)
        total = jnp.sum(total, axis=0, keepdims=True)
        inverse = 1.0 / total
        for h in range(heads):
            p, odd = h // 2, h % 2
            block = total_out[p, odd * HEAD_DIM : (odd + 1) * HEAD_DIM, odd * TILE : (odd + 1) * TILE]
            out[h * HEAD_DIM : (h + 1) * HEAD_DIM, :] = (
                block * inverse[:, h * TILE : (h + 1) * TILE]
            ).astype(jnp.bfloat16)
        log_total[0] = highest + jnp.log(total)

    by_steps(i, run)


def attention_forward(info, table, q, k, v_t):
    length, columns = q.shape
    heads = columns // HEAD_DIM
    tiles = length // TILE
    width = heads * TILE
    whole = lambda shape: pl.BlockSpec(shape, lambda i, info: (0,) * len(shape))
    return pl.pallas_call(
        functools.partial(forward_kernel, heads=heads),
        grid_spec=pltpu.PrefetchScalarGridSpec(
            num_scalar_prefetch=1,
            grid=(tiles,),
            in_specs=[
                whole(table.shape),
                pl.BlockSpec((TILE, columns), lambda i, info: (i, 0)),
                whole(k.shape),
                whole(v_t.shape),
            ],
            out_specs=[
                pl.BlockSpec((columns, TILE), lambda i, info: (0, i)),
                pl.BlockSpec((1, 1, width), lambda i, info: (i, 0, 0)),
            ],
            scratch_shapes=[
                pltpu.VMEM((CLASSES, TILE, width), jnp.float32),
                pltpu.VMEM((10 * TILE, width), jnp.float32),
                pltpu.VMEM((heads // 2, TILE, 2 * TILE), jnp.float32),
            ],
        ),
        out_shape=[
            jax.ShapeDtypeStruct((columns, length), jnp.bfloat16),
            jax.ShapeDtypeStruct((tiles, 1, width), jnp.float32),
        ],
        compiler_params=pltpu.CompilerParams(
            dimension_semantics=("arbitrary",), vmem_limit_bytes=50 << 20
        ),
        cost_estimate=pl.CostEstimate(flops=4 * 10**10, bytes_accessed=10**7, transcendentals=0),
        name="attention_forward",
    )(info, table, q, k, v_t)


def backward_kernel(
    info, table, q, k, k_t, v, grad, attended_t, log_total,
    grad_q, grad_k, grad_v, ahead, behind,
    bias, by_class, total_q, total_k, total_v, *, heads, tiles,
):
    i = pl.program_id(0)
    width = heads * TILE

    @pl.when(i == 0)
    def _():
        fill_bias(info, table, bias, heads)
        by_class[...] = jnp.zeros_like(by_class)
        total_k[...] = jnp.zeros_like(total_k)
        total_v[...] = jnp.zeros_like(total_v)

    tile_of = tile_plan(i, info)
    queries = head_rows(q[...] * jnp.bfloat16(0.125), heads)
    grads = head_rows(grad[...], heads)
    product = jnp.transpose(grad[...].astype(jnp.float32)) * attended_t[...].astype(jnp.float32)
    centre = jnp.concatenate(
        [
            jnp.sum(product[h * HEAD_DIM : (h + 1) * HEAD_DIM], axis=0, keepdims=True)
            for h in range(heads)
        ],
        axis=1,
    )
    logs = log_total[0]
    total_q[...] = jnp.zeros_like(total_q)
    pairs = heads // 2

    def one(step):
        (ta, ka), (tb, kb) = tile_of(step, 0), tile_of(step, 1)
        keys = jnp.concatenate([rows_at(k, ta), rows_at(k, tb)], axis=0)
        values = jnp.concatenate([rows_at(v, ta), rows_at(v, tb)], axis=0)
        raw = lax.dot_general(keys, queries, (((1,), (1,)), ((), ())), preferred_element_type=jnp.float32)
        both = jnp.concatenate(
            [masked_scores(raw, 0, ta, ka, info, bias, heads), masked_scores(raw, 1, tb, kb, info, bias, heads)],
            axis=0,
        )
        probs = jnp.exp(both - logs)
        grad_probs = lax.dot_general(
            values, grads, (((1,), (1,)), ((), ())), preferred_element_type=jnp.float32
        )
        grad_scores = probs * (grad_probs - centre)
        by_class[ka] += grad_scores[:TILE]
        by_class[kb] += grad_scores[TILE:]
        low = grad_scores.astype(jnp.bfloat16)
        value_part = jnp.dot(probs.astype(jnp.bfloat16), grads, preferred_element_type=jnp.float32)
        key_part = jnp.dot(low, queries, preferred_element_type=jnp.float32)
        for half, tile in ((0, ta), (1, tb)):
            at = pl.ds(pl.multiple_of(tile * TILE, TILE), TILE)
            total_v[at, :] += value_part[half * TILE : (half + 1) * TILE]
            total_k[at, :] += key_part[half * TILE : (half + 1) * TILE]
        for p in range(pairs):
            keys_t = jnp.concatenate(
                [lanes_at(k_t, p * TILE, TILE, ta), lanes_at(k_t, p * TILE, TILE, tb)], axis=1
            )
            total_q[p] += jnp.dot(
                keys_t, low[:, p * 2 * TILE : (p + 1) * 2 * TILE], preferred_element_type=jnp.float32
            )

    def run(steps):
        for step in range(steps):
            one(step)

    by_steps(i, run)
    for h in range(heads):
        p, odd = h // 2, h % 2
        block = total_q[p, odd * HEAD_DIM : (odd + 1) * HEAD_DIM, odd * TILE : (odd + 1) * TILE]
        grad_q[h * HEAD_DIM : (h + 1) * HEAD_DIM, :] = (block * 0.125).astype(jnp.bfloat16)

    @pl.when(i == tiles - 1)
    def _():
        grad_k[...] = total_k[...].astype(jnp.bfloat16)
        grad_v[...] = total_v[...].astype(jnp.bfloat16)
        rows = lax.broadcasted_iota(jnp.int32, (TILE, TILE), 0)
        lanes = lax.broadcasted_iota(jnp.int32, (TILE, TILE), 1)

        def reduce(number, carry):
            for h in range(heads):
                block = by_class[number, :, h * TILE : (h + 1) * TILE]
                turned = jnp.take_along_axis(block, (rows + lanes) % TILE, axis=1)
                forward = jnp.sum(jnp.where(rows + lanes < TILE, turned, 0.0), axis=0, keepdims=True)
                wrapped = jnp.sum(jnp.where(rows + lanes < TILE, 0.0, turned), axis=0, keepdims=True)
                ahead[number, :, h * TILE : (h + 1) * TILE] = forward
                behind[number, :, h * TILE : (h + 1) * TILE] = wrapped
            return carry

        lax.fori_loop(0, CLASSES, reduce, 0)


def attention_backward(info, table, q, k, k_t, v, grad, attended_t, log_total):
    length, columns = q.shape
    heads = columns // HEAD_DIM
    tiles = length // TILE
    width = heads * TILE
    whole = lambda shape: pl.BlockSpec(shape, lambda i, info: (0,) * len(shape))
    rows = pl.BlockSpec((TILE, columns), lambda i, info: (i, 0))
    lanes = pl.BlockSpec((columns, TILE), lambda i, info: (0, i))
    return pl.pallas_call(
        functools.partial(backward_kernel, heads=heads, tiles=tiles),
        grid_spec=pltpu.PrefetchScalarGridSpec(
            num_scalar_prefetch=1,
            grid=(tiles,),
            in_specs=[
                whole(table.shape), rows, whole(k.shape), whole(k_t.shape), whole(v.shape), rows, lanes,
                pl.BlockSpec((1, 1, width), lambda i, info: (i, 0, 0)),
            ],
            out_specs=[
                lanes, whole(k.shape), whole(v.shape),
                whole((CLASSES, 1, width)), whole((CLASSES, 1, width)),
            ],
            scratch_shapes=[
                pltpu.VMEM((CLASSES, TILE, width), jnp.float32),
                pltpu.VMEM((CLASSES, TILE, width), jnp.float32),
                pltpu.VMEM((heads // 2, TILE, 2 * TILE), jnp.float32),
                pltpu.VMEM((length, columns), jnp.float32),
                pltpu.VMEM((length, columns), jnp.float32),
            ],
        ),
        out_shape=[
            jax.ShapeDtypeStruct((columns, length), jnp.bfloat16),
            jax.ShapeDtypeStruct((length, columns), jnp.bfloat16),
            jax.ShapeDtypeStruct((length, columns), jnp.bfloat16),
            jax.ShapeDtypeStruct((CLASSES, 1, width), jnp.float32),
            jax.ShapeDtypeStruct((CLASSES, 1, width), jnp.float32),
        ],
        compiler_params=pltpu.CompilerParams(
            dimension_semantics=("arbitrary",), vmem_limit_bytes=56 << 20
        ),
        cost_estimate=pl.CostEstimate(flops=6 * 10**10, bytes_accessed=10**7, transcendentals=0),
        name="attention_backward",
    )(info, table, q, k, k_t, v, grad, attended_t, log_total)


def bucket_index(distance, bucket_count, max_dist=128):
    half_count = bucket_count // 2
    counted = jnp.zeros_like(distance)
    for number in range(1, bucket_count - half_count):
        border = math.ceil(half_count * (max_dist / half_count) ** (number / (bucket_count - half_count)))
        counted = counted + (distance >= border).astype(jnp.int32)
    return jnp.where(distance < half_count, distance, half_count + counted)


def attention_info(validity):
    trunk = jnp.sum(validity[:TRUNK])
    lengths = jnp.sum(validity[TRUNK:].reshape(NBRANCH, 1 + NLEAF, SEGMENT), axis=2)
    last = (trunk - 1) // TILE
    limits = jnp.concatenate([trunk - TILE * jnp.arange(TRUNK_TILES), lengths.reshape(-1)])
    left = trunk - last * TILE
    branch = lengths[:, 0]
    offsets = jnp.concatenate(
        [
            jnp.array([0, TILE, 4096, 0]),
            jnp.stack([left, left + TILE]),
            left + branch,
            left + branch + TILE,
            branch,
        ]
    )
    info = jnp.zeros((64,), jnp.int32)
    info = info.at[:20].set(limits).at[20].set(last).at[OFFSET_AT : OFFSET_AT + CLASSES].set(offsets)
    return info


def bias_table(rel_bias):
    places = bucket_index(jnp.arange(TILE, dtype=jnp.int32), rel_bias.shape[0])
    pick = (places[:, None] == jnp.arange(rel_bias.shape[0])[None, :]).astype(jnp.float32)
    shifted = rel_bias - rel_bias[-1:]
    return jnp.einsum("db,bh->hd", pick, shifted, precision=lax.Precision.HIGHEST)


def bias_gradient(ahead, behind, offsets, bucket_count):
    heads = ahead.shape[2] // TILE
    lane = jnp.arange(TILE, dtype=jnp.int32)[None, :]
    distance = jnp.stack([offsets[:, None] + lane, offsets[:, None] + lane - TILE], axis=0)
    bucket = bucket_index(jnp.maximum(distance, 0), bucket_count)
    pick = (bucket[..., None] == jnp.arange(bucket_count)).astype(jnp.float32)
    sums = jnp.stack([ahead, behind], axis=0).reshape(2, CLASSES, heads, TILE)
    return jnp.einsum("sclb,schl->bh", pick, sums, precision=lax.Precision.HIGHEST)


EPSILON = 1e-06
SLOT_TILE = 256


def slot_pick(slots, tile, count, axis):
    shape = (SLOT_TILE, count) if axis == 0 else (count, SLOT_TILE)
    places = lax.broadcasted_iota(jnp.int32, shape, axis)
    return (slots - tile * SLOT_TILE == places).astype(jnp.float32).astype(jnp.bfloat16)


def fill_slots(scalars, block, slots, values, out):
    def one(tile, carry):
        at = pl.ds(pl.multiple_of(tile * SLOT_TILE, SLOT_TILE), SLOT_TILE)
        pick = slot_pick(slots, tile, values.shape[0], 0)
        out[at, :] += jnp.dot(pick, values, preferred_element_type=jnp.float32).astype(jnp.bfloat16)
        return carry

    lax.fori_loop(scalars[block] // SLOT_TILE, pl.cdiv(scalars[block + 1], SLOT_TILE), one, 0)


def compact_rows_kernel(scalars, router, slots, named, *refs, blocks, experts):
    stacks, (out, gate) = refs[:-2], refs[-2:]
    rows = [(stack, number) for stack in stacks for number in range(stack.shape[0])]
    out[...] = jnp.zeros_like(out)
    me = scalars[blocks + 1]
    for b, (stack, number) in enumerate(rows):
        values = stack[number]
        fill_slots(scalars, b, slots[b], values, out)
        products = jnp.dot(values, router[...], preferred_element_type=jnp.float32)
        lane = lax.broadcasted_iota(jnp.int32, products.shape, 1)
        lane = jnp.where(lane < 3 * experts, lane % experts, -1)
        choices = [named[b, :, k : k + 1] for k in range(named.shape[2])]
        logits = [
            jnp.sum(jnp.where(lane == choice, products, 0.0), axis=1, keepdims=True) for choice in choices
        ]
        highest = functools.reduce(jnp.maximum, logits)
        powers = [jnp.exp(logit - highest) for logit in logits]
        mine = sum(jnp.where(choice == me, power, 0.0) for choice, power in zip(choices, powers))
        gate[b] = mine / sum(powers)


def whole_calls(kernel, operands, out_shape, name, limit):
    specs = [pl.BlockSpec(memory_space=pltpu.SMEM)]
    specs += [pl.BlockSpec(memory_space=pltpu.VMEM) for _ in operands[1:]]
    return pl.pallas_call(
        kernel,
        in_specs=specs,
        out_specs=jax.tree.map(lambda _: pl.BlockSpec(memory_space=pltpu.VMEM), out_shape),
        out_shape=out_shape,
        compiler_params=pltpu.CompilerParams(vmem_limit_bytes=limit << 20),
        cost_estimate=pl.CostEstimate(flops=10**10, bytes_accessed=3 * 10**7, transcendentals=0),
        name=name,
    )(*operands)


def slot_room(rows):
    return pl.cdiv(rows, SLOT_TILE) * SLOT_TILE


def compact_rows(scalars, router, slots, named, rows, experts):
    (blocks, count), width = slots.shape, rows[0].shape[2]
    return whole_calls(
        functools.partial(compact_rows_kernel, blocks=blocks, experts=experts),
        (scalars, router, slots.reshape(blocks, 1, count), named, *rows),
        [
            jax.ShapeDtypeStruct((slot_room(blocks * count), width), jnp.bfloat16),
            jax.ShapeDtypeStruct((blocks, count, 1), jnp.float32),
        ],
        "compact_rows",
        48,
    )


def compact_grads_kernel(scalars, slots, gate, produced, *refs, blocks):
    stacks, (out, gate_grad) = refs[:-2], refs[-2:]
    rows = [(stack, number) for stack in stacks for number in range(stack.shape[0])]
    out[...] = jnp.zeros_like(out)
    for b, (stack, number) in enumerate(rows):
        wide = stack[number].astype(jnp.float32)
        gate_grad[b] = jnp.sum(wide * produced[b].astype(jnp.float32), axis=1, keepdims=True)
        fill_slots(scalars, b, slots[b], (gate[b] * wide).astype(jnp.bfloat16), out)


def compact_grads(scalars, slots, gate, produced, rows):
    (blocks, count), width = slots.shape, rows[0].shape[2]
    return whole_calls(
        functools.partial(compact_grads_kernel, blocks=blocks),
        (scalars, slots.reshape(blocks, 1, count), gate, produced, *rows),
        [
            jax.ShapeDtypeStruct((slot_room(blocks * count), width), jnp.bfloat16),
            jax.ShapeDtypeStruct((blocks, count, 1), jnp.float32),
        ],
        "compact_grads",
        56,
    )


def expand_kernel(scalars, slots, *refs, blocks, gated):
    gate = refs[0] if gated else None
    rows, outs = (refs[1], refs[2:]) if gated else (refs[0], refs[1:])
    for b in range(blocks):
        out = outs[b]
        count = out.shape[0]
        out[...] = jnp.zeros_like(out)

        def one(tile, carry):
            at = pl.ds(pl.multiple_of(tile * SLOT_TILE, SLOT_TILE), SLOT_TILE)
            pick = slot_pick(slots[b], tile, count, 1)
            part = jnp.dot(pick, rows[at, :].astype(jnp.bfloat16), preferred_element_type=jnp.float32)
            out[...] += part.astype(jnp.bfloat16)
            return carry

        lax.fori_loop(scalars[b] // SLOT_TILE, pl.cdiv(scalars[b + 1], SLOT_TILE), one, 0)
        if gated:
            outs[blocks][b] = out[...]
            out[...] = (gate[b] * out[...].astype(jnp.float32)).astype(jnp.bfloat16)


def expand(scalars, slots, rows, gate=None):
    blocks, count = slots.shape
    width = rows.shape[1]
    shapes = [jax.ShapeDtypeStruct((count, width), jnp.bfloat16)] * blocks
    if gate is not None:
        shapes = shapes + [jax.ShapeDtypeStruct((blocks, count, width), jnp.bfloat16)]
    operands = (scalars, slots.reshape(blocks, count, 1)) + (() if gate is None else (gate,)) + (rows,)
    outs = whole_calls(
        functools.partial(expand_kernel, blocks=blocks, gated=gate is not None),
        operands, shapes, "expand", 56,
    )
    return outs if gate is None else (outs[:blocks], outs[blocks])


GELU_IN = math.sqrt(2.0 / math.pi)
GELU_CUBE = 0.044715


def gelu_parts(pre):
    square = pre * pre
    bent = jnp.tanh(GELU_IN * pre * (1.0 + GELU_CUBE * square))
    half = 0.5 * (1.0 + bent)
    return pre * half, half, bent, square


LAST = (((1,), (1,)), ((), ()))
FIRST = (((0,), (0,)), ((), ()))


def weight_sources(sources, z):
    if len(sources) == 1:
        return [[(None, sources[0].at[number])] for number in range(sources[0].shape[0])]
    own, up_one, down_one, up_two, down_two, far = sources
    low, high = z == 0, z == 3
    return [
        [(None, own)],
        [(z < 3, down_one), (high, up_one)],
        [(low, down_two), ((z == 1) | (z == 2), up_one), (high, up_two)],
        [(low | high, far), (z == 1, down_two), (z == 2, up_two)],
    ]


def weight_copies(step, sources, theirs, room, sem, act):
    def copy(slot, half, view):
        rows = view.shape[1]
        for matrix in range(3):
            act(
                pltpu.make_async_copy(
                    view.at[matrix],
                    room.at[slot, matrix, pl.ds(half * rows, rows)],
                    sem.at[slot, half * 3 + matrix],
                )
            )

    for number, choices in enumerate(sources):
        for condition, view in choices:
            here = step == number if condition is None else (step == number) & condition
            pl.when(here)(functools.partial(copy, number % 2, 0, view))
        pl.when(step == number)(functools.partial(copy, number % 2, 1, theirs.at[number]))


def next_weights(sources, theirs, room, sem):
    step, steps = pl.program_id(0), len(sources)

    @pl.when(step == 0)
    def _():
        weight_copies(step, sources, theirs, room, sem, lambda copy: copy.start())

    @pl.when(step + 1 < steps)
    def _():
        weight_copies(step + 1, sources, theirs, room, sem, lambda copy: copy.start())

    weight_copies(step, sources, theirs, room, sem, lambda copy: copy.wait())
    return step % 2


def expert_forward_kernel(scalars, rows, theirs, *refs):
    mine, (total, room, sem) = refs[:-3], refs[-3:]
    step = pl.program_id(0)
    slot = next_weights(weight_sources(mine, scalars[1]), theirs, room, sem)

    def one(tile, carry):
        at = pl.ds(pl.multiple_of(tile * SLOT_TILE, SLOT_TILE), SLOT_TILE)
        values = rows[at, :]
        gate_pre = lax.dot_general(values, room[slot, 0], LAST, preferred_element_type=jnp.float32)
        up_pre = lax.dot_general(values, room[slot, 1], LAST, preferred_element_type=jnp.float32)
        inner = (gelu_parts(gate_pre)[0] * up_pre).astype(jnp.bfloat16)
        part = jnp.dot(inner, room[slot, 2], preferred_element_type=jnp.float32)

        @pl.when(step == 0)
        def _():
            total[at, :] = part

        @pl.when(step > 0)
        def _():
            total[at, :] += part

        return carry

    lax.fori_loop(0, pl.cdiv(scalars[0], SLOT_TILE), one, 0)


def expert_cost(rows, weights, shards, units):
    return pl.CostEstimate(
        flops=2 * units * rows * shards * weights.shape[-2] * 2 * weights.shape[-1],
        bytes_accessed=4 * weights.size,
        transcendentals=0,
    )


def expert_scratch(weights):
    half, width = weights.shape[-2:]
    return [pltpu.VMEM((2, 3, 2 * half, width), jnp.bfloat16), pltpu.SemaphoreType.DMA((2, 6))]


def expert_forward(scalars, rows, mine, theirs):
    padded, width = rows.shape
    shards = theirs.shape[0]
    whole = pl.BlockSpec((padded, width), lambda s, scalars: (0, 0), pipeline_mode=pl.Buffered(1))
    return pl.pallas_call(
        expert_forward_kernel,
        grid_spec=pltpu.PrefetchScalarGridSpec(
            num_scalar_prefetch=1,
            grid=(shards,),
            in_specs=[whole] + [pl.BlockSpec(memory_space=pl.ANY)] * (1 + len(mine)),
            out_specs=whole,
            scratch_shapes=expert_scratch(theirs),
        ),
        out_shape=jax.ShapeDtypeStruct((padded, width), jnp.float32),
        compiler_params=pltpu.CompilerParams(vmem_limit_bytes=56 << 20),
        cost_estimate=expert_cost(padded, theirs, shards, 3),
        name="expert_forward",
    )(scalars, rows, theirs, *mine)


def expert_backward_kernel(scalars, rows, grads, theirs, *refs):
    mine, rest = refs[:-8], refs[-8:]
    mine_out, theirs_out, total, gate_total, up_total, down_total, room, sem = rest
    step = pl.program_id(0)
    slot = next_weights(weight_sources(mine, scalars[1]), theirs, room, sem)
    gate_total[...] = jnp.zeros_like(gate_total)
    up_total[...] = jnp.zeros_like(up_total)
    down_total[...] = jnp.zeros_like(down_total)

    def one(tile, carry):
        at = pl.ds(pl.multiple_of(tile * SLOT_TILE, SLOT_TILE), SLOT_TILE)
        values, upstream = rows[at, :], grads[at, :]
        gate_pre = lax.dot_general(values, room[slot, 0], LAST, preferred_element_type=jnp.float32)
        up_pre = lax.dot_general(values, room[slot, 1], LAST, preferred_element_type=jnp.float32)
        grad_inner = lax.dot_general(upstream, room[slot, 2], LAST, preferred_element_type=jnp.float32)
        active, half, bent, square = gelu_parts(gate_pre)
        slope = half + (0.5 * GELU_IN) * gate_pre * (1.0 - bent * bent) * (1.0 + 3.0 * GELU_CUBE * square)
        inner = (active * up_pre).astype(jnp.bfloat16)
        grad_gate = (grad_inner * up_pre * slope).astype(jnp.bfloat16)
        grad_up = (grad_inner * active).astype(jnp.bfloat16)
        down_total[...] += lax.dot_general(inner, upstream, FIRST, preferred_element_type=jnp.float32)
        gate_total[...] += lax.dot_general(grad_gate, values, FIRST, preferred_element_type=jnp.float32)
        up_total[...] += lax.dot_general(grad_up, values, FIRST, preferred_element_type=jnp.float32)
        part = jnp.dot(grad_gate, room[slot, 0], preferred_element_type=jnp.float32)
        part = part + jnp.dot(grad_up, room[slot, 1], preferred_element_type=jnp.float32)

        @pl.when(step == 0)
        def _():
            total[at, :] = part

        @pl.when(step > 0)
        def _():
            total[at, :] += part

        return carry

    lax.fori_loop(0, pl.cdiv(scalars[0], SLOT_TILE), one, 0)
    half = mine_out.shape[2]
    for number, sums in enumerate((gate_total, up_total, down_total)):
        mine_out[0, number] = sums[:half].astype(jnp.bfloat16)
        theirs_out[0, number] = sums[half:].astype(jnp.bfloat16)


def expert_backward(scalars, rows, grads, mine, theirs):
    padded, width = rows.shape
    shards, _, half, _ = theirs.shape
    whole = pl.BlockSpec((padded, width), lambda s, scalars: (0, 0), pipeline_mode=pl.Buffered(1))
    out = pl.BlockSpec((1, 3, half, width), lambda s, scalars: (scalars[2 + s], 0, 0, 0))
    shape = jax.ShapeDtypeStruct((shards, 3, half, width), jnp.bfloat16)
    return pl.pallas_call(
        expert_backward_kernel,
        grid_spec=pltpu.PrefetchScalarGridSpec(
            num_scalar_prefetch=1,
            grid=(shards,),
            in_specs=[whole, whole] + [pl.BlockSpec(memory_space=pl.ANY)] * (1 + len(mine)),
            out_specs=[out, out, whole],
            scratch_shapes=[pltpu.VMEM((2 * half, width), jnp.float32)] * 3 + expert_scratch(theirs),
        ),
        out_shape=[shape, shape, jax.ShapeDtypeStruct((padded, width), jnp.float32)],
        compiler_params=pltpu.CompilerParams(vmem_limit_bytes=60 << 20),
        cost_estimate=expert_cost(padded, theirs, shards, 8),
        name="expert_backward",
    )(scalars, rows, grads, theirs, *mine)


def project_kernel(scalars, weights, *refs, parts):
    mine, others = refs[:parts], refs[parts : 2 * parts]
    rows_out, q, k, k_t, v, v_t = refs[2 * parts :]
    count = mine[0].shape[0]
    columns = q.shape[1]
    active = scalars[parts] > 0
    for part in range(parts):
        at = pl.ds(pl.multiple_of(scalars[part] * count, count), count)
        rows = jnp.where(active, mine[part][...], others[part][...])
        rows_out[at, :] = rows
        low = jnp.dot(rows, weights[...], preferred_element_type=jnp.float32).astype(jnp.bfloat16)
        q[at, :] = low[:, :columns]
        k[at, :] = low[:, columns : 2 * columns]
        v[at, :] = low[:, 2 * columns :]
        k_t[:, at] = jnp.transpose(low[:, columns : 2 * columns])
        v_t[:, at] = jnp.transpose(low[:, 2 * columns :])


def project(scalars, weights, mine, others):
    parts, (count, width) = len(mine), mine[0].shape
    length, columns = parts * count, weights.shape[1] // 3
    tall = jax.ShapeDtypeStruct((length, columns), jnp.bfloat16)
    wide = jax.ShapeDtypeStruct((columns, length), jnp.bfloat16)
    return whole_calls(
        functools.partial(project_kernel, parts=parts),
        (scalars, weights, *mine, *others),
        [jax.ShapeDtypeStruct((length, width), jnp.bfloat16), tall, tall, wide, tall, wide],
        "project",
        56,
    )


def split_float(values):
    high = values.astype(jnp.bfloat16)
    rest = values - high.astype(jnp.float32)
    middle = rest.astype(jnp.bfloat16)
    low = (rest - middle.astype(jnp.float32)).astype(jnp.bfloat16)
    return jnp.concatenate([high, middle, low], axis=1)


def join_float(products, count):
    return products[:, 2 * count :] + products[:, count : 2 * count] + products[:, :count]


def swap(array, axis, bit):
    size = lax.axis_size(axis)
    return lax.ppermute(array, axis, [(i, i ^ bit) for i in range(size)])


def sum_over(array, axes):
    for axis in axes:
        bit = 1
        while bit < lax.axis_size(axis):
            array = array + swap(array, axis, bit)
            bit *= 2
    return array


def ring_layer():
    return lax.axis_size("expert") == 4


def layer_member(number):
    return lax.axis_index("expert") ^ number if ring_layer() else number


def layer_gather(rows):
    columns = lax.axis_size("expert")
    if not ring_layer():
        stacked = lax.all_gather(rows, "expert", axis=0)
        return [stacked[number] for number in range(columns)]
    half = rows.shape[0] // 2
    top, bottom = rows[:half], rows[half:]
    x_top, y_bottom = swap(top, "expert", 1), swap(bottom, "expert", 2)
    x_bottom, y_top = swap(bottom, "expert", 1), swap(top, "expert", 2)
    far_top, far_bottom = swap(x_top, "expert", 2), swap(y_bottom, "expert", 1)
    return [top, bottom, x_top, x_bottom, y_top, y_bottom, far_top, far_bottom]


def layer_scatter(parts):
    if not ring_layer():
        return lax.psum_scatter(
            jnp.stack(parts), "expert", scatter_dimension=0, tiled=False
        ).astype(jnp.float32)
    top, bottom, x_top, x_bottom, y_top, y_bottom, far_top, far_bottom = parts
    far_top, far_bottom = swap(far_top, "expert", 1), swap(far_bottom, "expert", 2)
    x_top, y_bottom = swap(x_top, "expert", 1), swap(y_bottom, "expert", 2)
    y_top = swap(y_top + far_top, "expert", 2)
    x_bottom = swap(x_bottom + far_bottom, "expert", 1)
    wide = lambda array: array.astype(jnp.float32)
    return jnp.concatenate(
        [wide(top) + wide(x_top) + wide(y_top), wide(bottom) + wide(x_bottom) + wide(y_bottom)], axis=0
    )


def layer_small(array):
    columns = lax.axis_size("expert")
    if not ring_layer():
        return lax.all_gather(array, "expert", axis=0)
    return jnp.stack([array] + [swap(array, "expert", number) for number in range(1, columns)])


def layer_trade(array):
    if not ring_layer():
        return lax.all_to_all(array, "expert", split_axis=0, concat_axis=0, tiled=True)
    return jnp.stack([array[0]] + [swap(array[n], "expert", n) for n in range(1, array.shape[0])])


def layer_blocks(array, rows):
    half = rows // 2
    return [
        lax.dynamic_slice_in_dim(array, layer_member(number) * rows + side * half, half, 0)
        for number in range(array.shape[0] // rows)
        for side in range(2)
    ]


def layer_place(pieces):
    if not ring_layer():
        return jnp.concatenate(pieces, axis=0)
    half = pieces[0].shape[0]
    out = jnp.zeros((half * len(pieces),) + pieces[0].shape[1:], pieces[0].dtype)
    for place, piece in enumerate(pieces):
        at = layer_member(place // 2) * 2 * half + (place % 2) * half
        out = lax.dynamic_update_slice_in_dim(out, piece, at, 0)
    return out


PLACE = ("shard", "dp")


def split_trees():
    return lax.axis_size("shard") == 4 and lax.axis_size("dp") == 2 and ring_layer()


def move(array, pairs):
    index = lambda place: place[0] * 2 + place[1]
    return lax.ppermute(array, PLACE, [(index(a), index(b)) for a, b in pairs])


def mirrored(pairs):
    flip = lambda place: (3 - place[0], 1 - place[1])
    return pairs + [(flip(a), flip(b)) for a, b in pairs]


def heads_place(group, tree):
    return (2 * tree + group // 2, group % 2)


def my_place():
    z, core = lax.axis_index("shard"), lax.axis_index("dp")
    return z, core, z // 2, 2 * (z % 2) + core


WEIGHT_PAIRS = [((group, tree), heads_place(group, tree)) for group in range(4) for tree in range(2)]


def weights_to_groups(array):
    return move(array, WEIGHT_PAIRS)


def groups_to_weights(array):
    return move(array, [(b, a) for a, b in WEIGHT_PAIRS])


def of_tree(array):
    z, core, tree, group = my_place()
    return jnp.where(core == tree, array, swap(array, "dp", 1))


def tree_gather(own):
    z, core, tree, group = my_place()
    first = move(own, mirrored([((1, 0), (0, 0)), ((2, 0), (1, 0)), ((3, 0), (2, 0))]))
    back = move(own, mirrored([((0, 0), (1, 0))]))
    second = move(first, mirrored([((1, 0), (0, 0)), ((2, 0), (1, 0))]))
    third = move(second, mirrored([((1, 0), (0, 0))]))
    end = (z == 0) | (z == 3)
    step = jnp.where(tree == 0, 1, -1)
    blocks = [own, first, second, jnp.where(end, third, back)]
    places = [z, z + step, z + 2 * step, jnp.where(end, z + 3 * step, z - step)]
    scalars = jnp.stack(places + [core == tree]).astype(jnp.int32)
    return scalars, blocks, [swap(block, "dp", 1) for block in blocks]


def tree_scatter(rows_of):
    z, core, tree, group = my_place()
    active, end = core == tree, (z == 0) | (z == 3)

    def chip_sum(place):
        part = rows_of(jnp.where(tree == 0, place, 3 - place))
        return part + swap(part, "dp", 1)

    far, next_far, next_near, near = chip_sum(3), chip_sum(2), chip_sum(1), chip_sum(0)
    one = move(jnp.where(end, far, near), mirrored([((0, 0), (1, 0)), ((1, 0), (0, 0))]))
    two = move(
        jnp.where(end, next_far, far + one), mirrored([((0, 0), (1, 0)), ((1, 0), (2, 0))])
    )
    three = move(
        jnp.where(active, jnp.where(end, next_near, next_far + two), two),
        mirrored([((0, 0), (1, 0)), ((1, 0), (2, 0)), ((2, 0), (3, 0))]),
    )
    wide = lambda array: array.astype(jnp.float32)
    at_end, in_middle = wide(near) + wide(one), wide(next_near) + wide(three)
    return jnp.where(active, jnp.where(end, at_end, in_middle), wide(three))


def gather_out_weight(weight):
    if not (split_trees()):
        return lax.all_gather(weight, "shard", axis=0, tiled=True)
    z = lax.axis_index("shard")
    rows, width = weight.shape
    quarter = rows // 4
    mine = lax.dynamic_slice_in_dim(weight, lax.axis_index("expert") * quarter, quarter, 0)
    stack = jnp.zeros((rows, width), weight.dtype)
    for number in range(4):
        piece = swap(mine, "shard", number) if number else mine
        stack = lax.dynamic_update_slice_in_dim(stack, piece, (z ^ number) * quarter, 0)
    stack = layer_place(layer_gather(stack)).reshape(4, 4, quarter, width)
    return stack.transpose(1, 0, 2, 3).reshape(4 * rows, width)


def hop(array, pairs):
    return lax.ppermute(array, "shard", pairs)


def weight_hop_one(own):
    if not split_trees():
        return (lax.all_gather(own, "shard", axis=0),)
    return hop(own, [(0, 1), (1, 2), (2, 3)]), hop(own, [(1, 0), (2, 1), (3, 2)])


def weight_hop_two(arrays):
    if not split_trees():
        return arrays
    return hop(arrays[0], [(1, 2), (2, 3)]), hop(arrays[1], [(2, 1), (1, 0)])


def weight_shards():
    z = lax.axis_index("shard")
    if not split_trees():
        return jnp.arange(lax.axis_size("shard"), dtype=jnp.int32)
    places = [
        z,
        jnp.where(z == 3, 2, z + 1),
        jnp.where(z == 0, 2, jnp.where(z == 3, 1, z - 1)),
        jnp.where(z < 2, 3, 0),
    ]
    return jnp.stack(places).astype(jnp.int32)


def greet(devices):
    barrier = pltpu.get_barrier_semaphore()
    for device in devices:
        pl.semaphore_signal(barrier, inc=1, device_id=device, device_id_type=pl.DeviceIdType.MESH)
    pl.semaphore_wait(barrier, len(devices))


def send_to(source, target, sems, number, device):
    return pltpu.make_async_remote_copy(
        src_ref=source,
        dst_ref=target,
        send_sem=sems.at[0, number],
        recv_sem=sems.at[1, number],
        device_id=device,
        device_id_type=pl.DeviceIdType.MESH,
    )


def meet_kernel(rows, own, up_one, down_one, up_two, down_two, layer, theirs, far, sems):
    column, z = lax.axis_index("expert"), lax.axis_index("shard")
    beside, above = {"expert": column ^ 1}, {"expert": column ^ 2}
    next_z, twin = {"shard": z ^ 1}, {"dp": lax.axis_index("dp") ^ 1}
    greet([beside, above, next_z, twin])
    x_top = send_to(rows.at[0], layer.at[0], sems, 0, beside)
    y_bottom = send_to(rows.at[1], layer.at[3], sems, 1, above)
    x_bottom = send_to(rows.at[1], layer.at[1], sems, 2, beside)
    y_top = send_to(rows.at[0], layer.at[2], sems, 3, above)
    for copy in (x_top, y_bottom, x_bottom, y_top):
        copy.start()

    hop_down = send_to(down_two, far, sems, 6, next_z)
    hop_up = send_to(up_two, far, sems, 6, next_z)
    pl.when(z == 1)(hop_down.start)
    pl.when(z == 2)(hop_up.start)
    places = weight_sources((own, up_one, down_one, up_two, down_two, far), z)
    ends = (z == 0) | (z == 3)
    for place, choices in enumerate(places):
        for condition, view in choices:
            if view is far:
                continue
            copy = send_to(view, theirs.at[place], sems, 7 + place, twin)
            if condition is None:
                copy.start()
            else:
                pl.when(condition)(copy.start)

    x_top.wait_recv()
    far_top = send_to(layer.at[0], layer.at[4], sems, 4, above)
    far_top.start()
    y_bottom.wait_recv()
    far_bottom = send_to(layer.at[3], layer.at[5], sems, 5, beside)
    far_bottom.start()
    last = send_to(far, theirs.at[3], sems, 10, twin)

    @pl.when(ends)
    def _():
        hop_down.wait_recv()
        last.start()

    @pl.when(jnp.logical_not(ends))
    def _():
        hop_down.wait_send()

    for copy in (x_top, y_bottom):
        copy.wait_send()
    for copy in (x_bottom, y_top, far_top, far_bottom):
        copy.wait()
    for place in range(4):
        send_to(own, theirs.at[place], sems, 7 + place, twin).wait()


def meet(rows, own, one, two):
    half = rows.shape[0] // 2
    halves = rows.reshape(2, half, rows.shape[1])
    anywhere = pl.BlockSpec(memory_space=pl.ANY)
    layer, theirs, far = pl.pallas_call(
        meet_kernel,
        in_specs=[anywhere] * 6,
        out_specs=[anywhere] * 3,
        out_shape=[
            jax.ShapeDtypeStruct((6,) + halves.shape[1:], rows.dtype),
            jax.ShapeDtypeStruct((4,) + own.shape, own.dtype),
            jax.ShapeDtypeStruct(own.shape, own.dtype),
        ],
        scratch_shapes=[pltpu.SemaphoreType.DMA((2, 11))],
        compiler_params=pltpu.CompilerParams(collective_id=1, has_side_effects=True),
        cost_estimate=pl.CostEstimate(flops=5 * 10**10, bytes_accessed=10**7, transcendentals=0),
        name="meet",
    )(halves, own, *one, *two)
    return [halves, layer], theirs, (own, *one, *two, far)


def reduce_attention_grads(three, out):
    width = out.shape[1]
    if not (split_trees()):
        if split_trees():
            three = groups_to_weights(three)
        out = lax.psum_scatter(out, "shard", scatter_dimension=0, tiled=True)
        three = lax.psum(three, ("expert", "dp"))
        return three.astype(jnp.float32), lax.psum(out, ("expert", "dp")).astype(jnp.float32)
    z = lax.axis_index("shard")
    quarter = width // 4
    part = quarter // 4
    columns = three.shape[1]
    out = out.reshape(4, 4, part, width).transpose(1, 0, 2, 3).reshape(width, width)
    both = jnp.concatenate([three, out], axis=1)
    both = layer_scatter(layer_blocks(both, quarter)).astype(jnp.bfloat16)
    three = groups_to_weights(both[:, :columns])
    out = both[:, columns:]
    pieces = [lax.dynamic_slice_in_dim(out, (z ^ number) * part, part, 0) for number in range(4)]
    pieces = [pieces[0]] + [swap(pieces[number], "shard", number) for number in range(1, 4)]
    out = sum(piece.astype(jnp.float32) for piece in pieces).astype(jnp.bfloat16)
    both = jnp.concatenate([three, out.reshape(quarter, width // 4)], axis=1)
    both = both + swap(both, "dp", 1)
    both = layer_place(layer_gather(both))
    out = both[:, columns:].reshape(4 * part, width)
    return both[:, :columns].astype(jnp.float32), out.astype(jnp.float32)


def trade_pairs(turn):
    return [
        (heads_place(group, tree), ((group + turn) % 4, tree)) for group in range(4) for tree in range(2)
    ]


def heads_to_rows(attended_t, shards):
    columns, length = attended_t.shape
    rows = length // shards
    if not split_trees():
        pieces = attended_t.reshape(columns, shards, rows).transpose(1, 0, 2)
        pieces = lax.all_to_all(pieces, "shard", split_axis=0, concat_axis=0, tiled=True)
        return pieces.reshape(shards * columns, rows)
    z, core, tree, group = my_place()
    out = jnp.zeros((shards * columns, rows), attended_t.dtype)
    for turn in range(4):
        piece = lax.dynamic_slice_in_dim(attended_t, (group + turn) % 4 * rows, rows, 1)
        piece = move(piece, trade_pairs(turn))
        out = lax.dynamic_update_slice_in_dim(out, piece, (z - turn) % 4 * columns, 0)
    return out


def rows_to_heads(grads, shards):
    rows, width = grads.shape
    columns = width // shards
    if not split_trees():
        pieces = grads.reshape(rows, shards, columns).transpose(1, 0, 2)
        pieces = lax.all_to_all(pieces, "shard", split_axis=0, concat_axis=0, tiled=True)
        return pieces.reshape(shards * rows, columns)
    z, core, tree, group = my_place()
    out = jnp.zeros((shards * rows, columns), grads.dtype)
    for turn in range(4):
        piece = lax.dynamic_slice_in_dim(grads, (z - turn) % 4 * columns, columns, 1)
        piece = move(piece, [(b, a) for a, b in trade_pairs(turn)])
        out = lax.dynamic_update_slice_in_dim(out, piece, (group + turn) % 4 * rows, 0)
    return out


def on_device(
    tokens, teacher, seg_ids, parents, depth, valid, routes, norm1_gain, w_query, w_key, w_value,
    w_out, rel_bias, norm2_gain, router, w_gate, w_up, w_down,
):
    shard_index = lax.axis_index("shard")
    expert_index = lax.axis_index("expert")
    shards = lax.axis_size("shard")
    columns = lax.axis_size("expert")
    experts = columns * w_gate.shape[0]
    token_rows = tokens[0].astype(jnp.float32)
    local_rows, width = token_rows.shape
    length = seg_ids.shape[1]
    bucket_count = rel_bias.shape[0]
    validity = valid[0]
    route_rows = routes[0]

    row_start = shard_index * local_rows
    valid_local = lax.dynamic_slice_in_dim(validity, row_start, local_rows, 0).astype(jnp.float32)
    route_local = lax.dynamic_slice_in_dim(route_rows, row_start, local_rows, 0)

    scale_one = lax.rsqrt(jnp.mean(token_rows * token_rows, axis=1, keepdims=True) + EPSILON)
    base_one = token_rows * scale_one
    normed_one = (base_one * norm1_gain).astype(jnp.bfloat16)
    expert_w = jnp.stack([w_gate[0].T, w_up[0].T, w_down[0]])
    half = expert_w.shape[1] // lax.axis_size("dp")
    expert_w = lax.dynamic_slice_in_dim(expert_w, lax.axis_index("dp") * half, half, 1)
    out_all = gather_out_weight(w_out)
    info = attention_info(validity)
    weights = jnp.concatenate([w_query, w_key, w_value], axis=1)
    bias_here = rel_bias
    if split_trees():
        info, bias_here = of_tree(info), weights_to_groups(rel_bias)
        if ring_layer():
            quarter = width // columns
            mine = lax.dynamic_slice_in_dim(weights, expert_index * quarter, quarter, 0)
            mine, normed_one = lax.optimization_barrier((weights_to_groups(mine), normed_one))
            weights = layer_place(layer_gather(mine))
        else:
            weights = weights_to_groups(weights)
        places, mine, others = tree_gather(normed_one)
        mine[3], expert_w = lax.optimization_barrier((mine[3], expert_w))
        weights_one = weight_hop_one(expert_w)
        weights, out_all = lax.optimization_barrier((weights, out_all))
        normed_all, query_rows, key_rows, key_t, value_rows, value_t = project(
            places, weights, mine, others
        )
    else:
        normed_all = lax.all_gather(normed_one, "shard", axis=0, tiled=True)
        projected = jnp.dot(normed_all, weights, preferred_element_type=jnp.float32).astype(jnp.bfloat16)
        query_rows, key_rows, value_rows = jnp.split(projected, 3, axis=1)
        key_t, value_t = key_rows.T, value_rows.T
        weights_one = weight_hop_one(expert_w)
    tree_count = sum_over(jnp.broadcast_to(jnp.sum(validity), (8, 128)), ("dp", "expert"))
    valid_total = tree_count[0, 0].astype(jnp.float32)

    top_count = route_local.shape[1]
    route_layer = layer_small(route_local.T)
    taken = jnp.any(route_layer == expert_index, axis=1)
    order = jnp.cumsum(taken.reshape(-1).astype(jnp.int32))
    slots = jnp.where(taken, order.reshape(taken.shape) - 1, -1)
    half_blocks = 2 * columns if ring_layer() else columns
    block_rows = columns * local_rows // half_blocks
    slots = slots.reshape(half_blocks, block_rows)
    named = route_layer.transpose(0, 2, 1).reshape(half_blocks, block_rows, top_count)
    scalars = jnp.concatenate(
        [jnp.zeros((1,), jnp.int32), order[block_rows - 1 :: block_rows], expert_index[None].astype(jnp.int32)]
    )

    table = bias_table(bias_here)
    attended_t, log_totals = attention_forward(info, table, query_rows, key_rows, value_t)

    attended_t, *weights_one = lax.optimization_barrier((attended_t, *weights_one))
    attended_here = heads_to_rows(attended_t, shards)
    weights_two = weight_hop_two(weights_one)
    update = lax.dot_general(
        attended_here, out_all, (((0,), (0,)), ((), ())), preferred_element_type=jnp.float32
    )
    hidden = token_rows + update

    scale_two = lax.rsqrt(jnp.mean(hidden * hidden, axis=1, keepdims=True) + EPSILON)
    base_two = hidden * scale_two
    normed_two = (base_two * norm2_gain).astype(jnp.bfloat16)

    expert_ids = jnp.arange(experts, dtype=jnp.int32)
    router_pieces = split_float(router)

    def gates_of(rows, named):
        logits = join_float(jnp.dot(rows, router_pieces, preferred_element_type=jnp.float32), experts)
        match = named[:, :, None] == expert_ids[None, None, :]
        chosen = jnp.sum(jnp.where(match, logits[:, None, :], 0.0), axis=2)
        return jax.nn.softmax(chosen, axis=1), match

    gates, route_match = gates_of(normed_two, route_local)
    if split_trees():
        normed_layer, theirs_w, mine_w = meet(normed_two, expert_w, weights_one, weights_two)
    else:
        normed_layer = [block[None] for block in layer_gather(normed_two)]
        mine_w = weights_one
        theirs_w = swap(weights_one[0], "dp", 1)
    expert_scalars = jnp.concatenate(
        [order[-1:], shard_index[None].astype(jnp.int32), weight_shards()]
    )
    router_wide = jnp.pad(router_pieces, ((0, 0), (0, TILE - router_pieces.shape[1])))
    expert_rows, gate_here = compact_rows(scalars, router_wide, slots, named, normed_layer, experts)
    produced = expert_forward(expert_scalars, expert_rows, mine_w, theirs_w)
    shares, produced_layer = expand(scalars, slots, produced, gate_here)
    combined = layer_scatter(shares)

    output_rows = hidden + combined
    factor = length * columns * lax.axis_size("dp") / valid_total
    error = output_rows - teacher[0].astype(jnp.float32)
    error_sum = jnp.sum(valid_local[:, None] * error * error)
    grad_output = valid_local[:, None] * error * factor
    grad_layer = [block[None] for block in layer_gather(grad_output.astype(jnp.bfloat16))]
    grad_rows, gate_grads = compact_grads(scalars, slots, gate_here, produced_layer, grad_layer)
    gate_grads = layer_trade(gate_grads.reshape(columns, local_rows))
    mine_part, theirs_part, rows_grad = expert_backward(
        expert_scalars, expert_rows, grad_rows, mine_w, theirs_w
    )
    expanded = expand(scalars, slots, rows_grad)
    *expanded, mine_part, theirs_part = lax.optimization_barrier((*expanded, mine_part, theirs_part))
    expert_back = layer_scatter(expanded)
    weight_part = mine_part + swap(theirs_part, "dp", 1)
    weight_part = lax.psum_scatter(weight_part, "shard", scatter_dimension=0, tiled=False)

    members = jnp.stack([jnp.asarray(layer_member(number), jnp.int32) for number in range(columns)])
    grad_gates = jnp.sum(
        jnp.where(route_local[:, :, None] == members[None, None, :], gate_grads.T[:, None, :], 0.0), axis=2
    )
    weighted = jnp.sum(gates * grad_gates, axis=1, keepdims=True)
    grad_chosen = gates * (grad_gates - weighted)
    grad_logits = jnp.sum(jnp.where(route_match, grad_chosen[:, :, None], 0.0), axis=1)
    router_grad = join_float(
        lax.dot_general(
            normed_two, split_float(grad_logits), (((0,), (0,)), ((), ())),
            preferred_element_type=jnp.float32,
        ),
        experts,
    )
    grad_normed_two = expert_back
    for number in range(experts):
        grad_normed_two = grad_normed_two + grad_logits[:, number : number + 1] * router[:, number][None]
    grad_base_two = grad_normed_two * norm2_gain
    norm2_grad = jnp.sum(grad_normed_two * base_two, axis=0)
    grad_hidden = grad_output + scale_two * (
        grad_base_two - base_two * jnp.mean(grad_base_two * base_two, axis=1, keepdims=True)
    )
    grad_update = grad_hidden.astype(jnp.bfloat16)
    out_grad = jnp.dot(attended_here, grad_update, preferred_element_type=jnp.float32)
    grad_heads = lax.dot_general(
        grad_update, out_all, (((1,), (1,)), ((), ())), preferred_element_type=jnp.float32
    ).astype(jnp.bfloat16)
    grad_attended = rows_to_heads(grad_heads, shards)

    grad_queries_t, grad_keys, grad_values, ahead, behind = attention_backward(
        info, table, query_rows, key_rows, key_t, value_rows, grad_attended, attended_t, log_totals
    )
    bias_grad = bias_gradient(ahead, behind, info[OFFSET_AT : OFFSET_AT + CLASSES], bucket_count)
    across = (((0,), (0,)), ((), ()))
    grad_three = jnp.concatenate([grad_queries_t.T, grad_keys, grad_values], axis=1)
    three_wgrad = lax.dot_general(normed_all, grad_three, across, preferred_element_type=jnp.float32)
    norm1_grad = jnp.sum(three_wgrad * weights.astype(jnp.float32), axis=1) / norm1_gain
    def normed_part(block):
        part = lax.dynamic_slice_in_dim(grad_three, block * local_rows, local_rows, 0)
        part = lax.dot_general(
            part, weights, (((1,), (1,)), ((), ())), preferred_element_type=jnp.float32
        )
        return part.astype(jnp.bfloat16)

    if split_trees():
        grad_normed_one = tree_scatter(normed_part)
    else:
        grad_normed_all = jnp.concatenate([normed_part(block) for block in range(shards)], axis=0)
        grad_normed_one = lax.psum_scatter(
            grad_normed_all, "shard", scatter_dimension=0, tiled=True
        ).astype(jnp.float32)
    grad_base_one = grad_normed_one * norm1_gain
    grad_tokens = grad_hidden + scale_one * (
        grad_base_one - base_one * jnp.mean(grad_base_one * base_one, axis=1, keepdims=True)
    )
    three_wgrad, out_grad = reduce_attention_grads(
        three_wgrad.astype(jnp.bfloat16), out_grad.astype(jnp.bfloat16)
    )
    query_wgrad, key_wgrad, value_wgrad = jnp.split(three_wgrad, 3, axis=1)
    heads_here = bias_grad.shape[1]
    group = my_place()[3] if split_trees() else shard_index
    bias_all = lax.dynamic_update_slice_in_dim(
        jnp.zeros((bucket_count, heads_here * shards), jnp.float32), bias_grad, group * heads_here, 1
    )
    bias_line = jnp.pad(bias_all.reshape(-1), (0, width - bias_all.size))
    small = jnp.concatenate(
        [router_grad.T, norm2_grad[None], norm1_grad[None], bias_line[None], jnp.full((1, width), error_sum)],
        axis=0,
    )
    small = sum_over(small, ("dp", "expert", "shard"))
    router_grad, norm2_grad, norm1_grad = small[:experts].T, small[experts], small[experts + 1]
    bias_all = small[experts + 2, : bias_all.size].reshape(bias_all.shape)
    bias_grad = lax.dynamic_slice_in_dim(bias_all, shard_index * heads_here, heads_here, 1)
    error_total = small[experts + 3, 0]
    loss = error_total / (width * valid_total)

    other_part = swap(weight_part, "dp", 1)
    first_core = lax.axis_index("dp") == 0
    weight_grad = jnp.concatenate(
        [jnp.where(first_core, weight_part, other_part), jnp.where(first_core, other_part, weight_part)],
        axis=1,
    ).astype(jnp.float32)
    gate_grad, up_grad, down_grad = weight_grad[0].T[None], weight_grad[1].T[None], weight_grad[2][None]
    return (
        output_rows.astype(jnp.bfloat16)[None],
        loss,
        grad_tokens[None],
        norm1_grad,
        query_wgrad,
        key_wgrad,
        value_wgrad,
        out_grad,
        bias_grad,
        norm2_grad,
        router_grad,
        gate_grad,
        up_grad,
        down_grad,
    )


def solution(mesh):
    in_specs = (
        P(("expert", "dp"), "shard", None),
        P(("expert", "dp"), "shard", None),
        P(("expert", "dp"), None),
        P(("expert", "dp"), None),
        P(("expert", "dp"), None),
        P(("expert", "dp"), None),
        P(("expert", "dp"), None, None),
        P(),
        P(None, "shard"),
        P(None, "shard"),
        P(None, "shard"),
        P("shard", None),
        P(None, "shard"),
        P(),
        P(),
        P("expert", None, "shard"),
        P("expert", None, "shard"),
        P("expert", "shard", None),
    )
    out_specs = (
        P(("expert", "dp"), "shard", None),
        P(),
        P(("expert", "dp"), "shard", None),
        P(),
        P(None, "shard"),
        P(None, "shard"),
        P(None, "shard"),
        P("shard", None),
        P(None, "shard"),
        P(),
        P(),
        P("expert", None, "shard"),
        P("expert", None, "shard"),
        P("expert", "shard", None),
    )
    return jax.shard_map(
        on_device, mesh=mesh, in_specs=in_specs, out_specs=out_specs, check_vma=False
    )
```

```python
import functools
import math

import jax
import jax.numpy as jnp
from jax import lax
from jax.experimental import pallas as pl
from jax.experimental.pallas import tpu as pltpu
from jax.sharding import PartitionSpec as P

TRUNK, SEGMENT, NBRANCH, NLEAF = 1024, 128, 4, 2
TILE = 128
TRUNK_TILES = TRUNK // TILE
HEAD_DIM = 64
MASKED = -1e30
DIAG, SUB, FAR, NONE, BRANCH_NEAR, LEAF_NEAR, LEAF_BRANCH = 0, 1, 2, 3, 4, 6, 14
CLASSES = 18
LIMIT_AT, OFFSET_AT, INFO_SIZE = 0, 32, 64


def head_rows(block, heads):
    lane = lax.broadcasted_iota(jnp.int32, block.shape, 1) // HEAD_DIM
    return jnp.concatenate(
        [jnp.where(lane == h, block, jnp.zeros((), block.dtype)) for h in range(heads)], axis=0
    )


def fill_bias(info, table, bias, heads):
    rows = lax.broadcasted_iota(jnp.int32, (TILE, TILE), 0)
    lanes = lax.broadcasted_iota(jnp.int32, (TILE, TILE), 1)

    def one(number, carry):
        place = jnp.clip(info[OFFSET_AT + number] + lanes - rows, 0, TILE - 1)
        hidden = ((number == DIAG) & (rows > lanes)) | (number == NONE)
        for h in range(heads):
            line = jnp.broadcast_to(table[h : h + 1, :], (TILE, TILE))
            values = jnp.take_along_axis(line, place, axis=1)
            bias[number, :, h * TILE : (h + 1) * TILE] = jnp.where(hidden, MASKED, values)
        return carry

    lax.fori_loop(0, CLASSES, one, 0)


def tile_plan(i, info):
    last = info[LIMIT_AT + 20]
    trunk = i < TRUNK_TILES
    place = jnp.maximum(i - TRUNK_TILES, 0)
    branch = place // (1 + NLEAF)
    leaf = (place % (1 + NLEAF)) > 0
    branch_tile = TRUNK_TILES + branch * (1 + NLEAF)
    near = jnp.where(trunk, i, last)
    near_class = jnp.where(trunk, DIAG, jnp.where(leaf, LEAF_NEAR + branch, BRANCH_NEAR))
    next_class = jnp.where(trunk, SUB, jnp.where(leaf, LEAF_NEAR + NBRANCH + branch, BRANCH_NEAR + 1))
    trunk_steps = TRUNK_TILES // 2
    tail = (
        (jnp.where(leaf, branch_tile, i), jnp.where(leaf, LEAF_BRANCH + branch, DIAG)),
        (i, jnp.where(leaf, DIAG, NONE)),
    )

    def tile_of(step, half):
        kt = step * 2 + half
        in_trunk = trunk | (step < trunk_steps)
        kind = jnp.where(
            kt == near, near_class, jnp.where(kt == near - 1, next_class, jnp.where(kt < near, FAR, NONE))
        )
        return jnp.where(in_trunk, kt, tail[half][0]), jnp.where(in_trunk, kind, tail[half][1])

    return tile_of


def by_steps(i, run):
    for count in range(1, TRUNK_TILES // 2 + 1):

        @pl.when((i < TRUNK_TILES) & (i // 2 == count - 1))
        def _(count=count):
            run(count)

    @pl.when(i >= TRUNK_TILES)
    def _():
        run(TRUNK_TILES // 2 + 1)


def masked_scores(scores, half, tile, kind, info, bias, heads):
    rows = lax.broadcasted_iota(jnp.int32, (TILE, TILE), 0)
    shade = jnp.where(rows < info[LIMIT_AT + tile], 0.0, MASKED)
    shade = jnp.concatenate([shade] * heads, axis=1)
    return scores[half * TILE : (half + 1) * TILE] + bias[kind] + shade


def rows_at(ref, tile):
    return ref[pl.ds(pl.multiple_of(tile * TILE, TILE), TILE), :]


def lanes_at(ref, first, count, tile):
    return ref[first : first + count, pl.ds(pl.multiple_of(tile * TILE, TILE), TILE)]


def forward_kernel(info, table, q, k, v_t, out, log_total, bias, score, total_out, *, heads):
    i = pl.program_id(0)

    @pl.when(i == 0)
    def _():
        fill_bias(info, table, bias, heads)

    tile_of = tile_plan(i, info)
    queries = head_rows(q[...] * jnp.bfloat16(0.125), heads)
    width = heads * TILE

    def first(step, highest):
        (ta, ka), (tb, kb) = tile_of(step, 0), tile_of(step, 1)
        keys = jnp.concatenate([rows_at(k, ta), rows_at(k, tb)], axis=0)
        raw = lax.dot_general(keys, queries, (((1,), (1,)), ((), ())), preferred_element_type=jnp.float32)
        both = jnp.concatenate(
            [masked_scores(raw, 0, ta, ka, info, bias, heads), masked_scores(raw, 1, tb, kb, info, bias, heads)],
            axis=0,
        )
        score[step * 2 * TILE : (step + 1) * 2 * TILE, :] = both
        return jnp.maximum(highest, jnp.max(both.reshape(2 * TILE // 8, 8, width), axis=0))

    pairs = heads // 2

    def run(steps):
        highest = jnp.full((8, width), MASKED, jnp.float32)
        for step in range(steps):
            highest = first(step, highest)
        highest = jnp.max(highest, axis=0, keepdims=True)
        total = jnp.zeros((8, width), jnp.float32)
        for step in range(steps):
            (ta, _), (tb, _) = tile_of(step, 0), tile_of(step, 1)
            part = jnp.exp(score[step * 2 * TILE : (step + 1) * 2 * TILE, :] - highest)
            low = part.astype(jnp.bfloat16)
            for p in range(pairs):
                values = jnp.concatenate(
                    [lanes_at(v_t, p * TILE, TILE, ta), lanes_at(v_t, p * TILE, TILE, tb)], axis=1
                )
                product = jnp.dot(
                    values, low[:, p * 2 * TILE : (p + 1) * 2 * TILE], preferred_element_type=jnp.float32
                )
                if step == 0:
                    total_out[p] = product
                else:
                    total_out[p] += product
            total = total + jnp.sum(part.reshape(2 * TILE // 8, 8, width), axis=0)
        total = jnp.sum(total, axis=0, keepdims=True)
        inverse = 1.0 / total
        for h in range(heads):
            p, odd = h // 2, h % 2
            block = total_out[p, odd * HEAD_DIM : (odd + 1) * HEAD_DIM, odd * TILE : (odd + 1) * TILE]
            out[h * HEAD_DIM : (h + 1) * HEAD_DIM, :] = (
                block * inverse[:, h * TILE : (h + 1) * TILE]
            ).astype(jnp.bfloat16)
        log_total[0] = highest + jnp.log(total)

    by_steps(i, run)


def attention_forward(info, table, q, k, v_t):
    length, columns = q.shape
    heads = columns // HEAD_DIM
    tiles = length // TILE
    width = heads * TILE
    whole = lambda shape: pl.BlockSpec(shape, lambda i, info: (0,) * len(shape))
    return pl.pallas_call(
        functools.partial(forward_kernel, heads=heads),
        grid_spec=pltpu.PrefetchScalarGridSpec(
            num_scalar_prefetch=1,
            grid=(tiles,),
            in_specs=[
                whole(table.shape),
                pl.BlockSpec((TILE, columns), lambda i, info: (i, 0)),
                whole(k.shape),
                whole(v_t.shape),
            ],
            out_specs=[
                pl.BlockSpec((columns, TILE), lambda i, info: (0, i)),
                pl.BlockSpec((1, 1, width), lambda i, info: (i, 0, 0)),
            ],
            scratch_shapes=[
                pltpu.VMEM((CLASSES, TILE, width), jnp.float32),
                pltpu.VMEM((10 * TILE, width), jnp.float32),
                pltpu.VMEM((heads // 2, TILE, 2 * TILE), jnp.float32),
            ],
        ),
        out_shape=[
            jax.ShapeDtypeStruct((columns, length), jnp.bfloat16),
            jax.ShapeDtypeStruct((tiles, 1, width), jnp.float32),
        ],
        compiler_params=pltpu.CompilerParams(
            dimension_semantics=("arbitrary",), vmem_limit_bytes=50 << 20
        ),
        cost_estimate=pl.CostEstimate(flops=4 * 10**10, bytes_accessed=10**7, transcendentals=0),
        name="attention_forward",
    )(info, table, q, k, v_t)


def backward_kernel(
    info, table, q, k, k_t, v, grad, attended_t, log_total,
    grad_q, grad_k, grad_v, ahead, behind,
    bias, by_class, total_q, total_k, total_v, *, heads, tiles,
):
    i = pl.program_id(0)
    width = heads * TILE

    @pl.when(i == 0)
    def _():
        fill_bias(info, table, bias, heads)
        by_class[...] = jnp.zeros_like(by_class)
        total_k[...] = jnp.zeros_like(total_k)
        total_v[...] = jnp.zeros_like(total_v)

    tile_of = tile_plan(i, info)
    queries = head_rows(q[...] * jnp.bfloat16(0.125), heads)
    grads = head_rows(grad[...], heads)
    product = jnp.transpose(grad[...].astype(jnp.float32)) * attended_t[...].astype(jnp.float32)
    centre = jnp.concatenate(
        [
            jnp.sum(product[h * HEAD_DIM : (h + 1) * HEAD_DIM], axis=0, keepdims=True)
            for h in range(heads)
        ],
        axis=1,
    )
    logs = log_total[0]
    total_q[...] = jnp.zeros_like(total_q)
    pairs = heads // 2

    def one(step):
        (ta, ka), (tb, kb) = tile_of(step, 0), tile_of(step, 1)
        keys = jnp.concatenate([rows_at(k, ta), rows_at(k, tb)], axis=0)
        values = jnp.concatenate([rows_at(v, ta), rows_at(v, tb)], axis=0)
        raw = lax.dot_general(keys, queries, (((1,), (1,)), ((), ())), preferred_element_type=jnp.float32)
        both = jnp.concatenate(
            [masked_scores(raw, 0, ta, ka, info, bias, heads), masked_scores(raw, 1, tb, kb, info, bias, heads)],
            axis=0,
        )
        probs = jnp.exp(both - logs)
        grad_probs = lax.dot_general(
            values, grads, (((1,), (1,)), ((), ())), preferred_element_type=jnp.float32
        )
        grad_scores = probs * (grad_probs - centre)
        by_class[ka] += grad_scores[:TILE]
        by_class[kb] += grad_scores[TILE:]
        low = grad_scores.astype(jnp.bfloat16)
        value_part = jnp.dot(probs.astype(jnp.bfloat16), grads, preferred_element_type=jnp.float32)
        key_part = jnp.dot(low, queries, preferred_element_type=jnp.float32)
        for half, tile in ((0, ta), (1, tb)):
            at = pl.ds(pl.multiple_of(tile * TILE, TILE), TILE)
            total_v[at, :] += value_part[half * TILE : (half + 1) * TILE]
            total_k[at, :] += key_part[half * TILE : (half + 1) * TILE]
        for p in range(pairs):
            keys_t = jnp.concatenate(
                [lanes_at(k_t, p * TILE, TILE, ta), lanes_at(k_t, p * TILE, TILE, tb)], axis=1
            )
            total_q[p] += jnp.dot(
                keys_t, low[:, p * 2 * TILE : (p + 1) * 2 * TILE], preferred_element_type=jnp.float32
            )

    def run(steps):
        for step in range(steps):
            one(step)

    by_steps(i, run)
    for h in range(heads):
        p, odd = h // 2, h % 2
        block = total_q[p, odd * HEAD_DIM : (odd + 1) * HEAD_DIM, odd * TILE : (odd + 1) * TILE]
        grad_q[h * HEAD_DIM : (h + 1) * HEAD_DIM, :] = (block * 0.125).astype(jnp.bfloat16)

    @pl.when(i == tiles - 1)
    def _():
        grad_k[...] = total_k[...].astype(jnp.bfloat16)
        grad_v[...] = total_v[...].astype(jnp.bfloat16)
        rows = lax.broadcasted_iota(jnp.int32, (TILE, TILE), 0)
        lanes = lax.broadcasted_iota(jnp.int32, (TILE, TILE), 1)

        def reduce(number, carry):
            for h in range(heads):
                block = by_class[number, :, h * TILE : (h + 1) * TILE]
                turned = jnp.take_along_axis(block, (rows + lanes) % TILE, axis=1)
                forward = jnp.sum(jnp.where(rows + lanes < TILE, turned, 0.0), axis=0, keepdims=True)
                wrapped = jnp.sum(jnp.where(rows + lanes < TILE, 0.0, turned), axis=0, keepdims=True)
                ahead[number, :, h * TILE : (h + 1) * TILE] = forward
                behind[number, :, h * TILE : (h + 1) * TILE] = wrapped
            return carry

        lax.fori_loop(0, CLASSES, reduce, 0)


def attention_backward(info, table, q, k, k_t, v, grad, attended_t, log_total):
    length, columns = q.shape
    heads = columns // HEAD_DIM
    tiles = length // TILE
    width = heads * TILE
    whole = lambda shape: pl.BlockSpec(shape, lambda i, info: (0,) * len(shape))
    rows = pl.BlockSpec((TILE, columns), lambda i, info: (i, 0))
    lanes = pl.BlockSpec((columns, TILE), lambda i, info: (0, i))
    return pl.pallas_call(
        functools.partial(backward_kernel, heads=heads, tiles=tiles),
        grid_spec=pltpu.PrefetchScalarGridSpec(
            num_scalar_prefetch=1,
            grid=(tiles,),
            in_specs=[
                whole(table.shape), rows, whole(k.shape), whole(k_t.shape), whole(v.shape), rows, lanes,
                pl.BlockSpec((1, 1, width), lambda i, info: (i, 0, 0)),
            ],
            out_specs=[
                lanes, whole(k.shape), whole(v.shape),
                whole((CLASSES, 1, width)), whole((CLASSES, 1, width)),
            ],
            scratch_shapes=[
                pltpu.VMEM((CLASSES, TILE, width), jnp.float32),
                pltpu.VMEM((CLASSES, TILE, width), jnp.float32),
                pltpu.VMEM((heads // 2, TILE, 2 * TILE), jnp.float32),
                pltpu.VMEM((length, columns), jnp.float32),
                pltpu.VMEM((length, columns), jnp.float32),
            ],
        ),
        out_shape=[
            jax.ShapeDtypeStruct((columns, length), jnp.bfloat16),
            jax.ShapeDtypeStruct((length, columns), jnp.bfloat16),
            jax.ShapeDtypeStruct((length, columns), jnp.bfloat16),
            jax.ShapeDtypeStruct((CLASSES, 1, width), jnp.float32),
            jax.ShapeDtypeStruct((CLASSES, 1, width), jnp.float32),
        ],
        compiler_params=pltpu.CompilerParams(
            dimension_semantics=("arbitrary",), vmem_limit_bytes=56 << 20
        ),
        cost_estimate=pl.CostEstimate(flops=6 * 10**10, bytes_accessed=10**7, transcendentals=0),
        name="attention_backward",
    )(info, table, q, k, k_t, v, grad, attended_t, log_total)


def bucket_index(distance, bucket_count, max_dist=128):
    half_count = bucket_count // 2
    counted = jnp.zeros_like(distance)
    for number in range(1, bucket_count - half_count):
        border = math.ceil(half_count * (max_dist / half_count) ** (number / (bucket_count - half_count)))
        counted = counted + (distance >= border).astype(jnp.int32)
    return jnp.where(distance < half_count, distance, half_count + counted)


def attention_info(validity):
    trunk = jnp.sum(validity[:TRUNK])
    lengths = jnp.sum(validity[TRUNK:].reshape(NBRANCH, 1 + NLEAF, SEGMENT), axis=2)
    last = (trunk - 1) // TILE
    limits = jnp.concatenate([trunk - TILE * jnp.arange(TRUNK_TILES), lengths.reshape(-1)])
    left = trunk - last * TILE
    branch = lengths[:, 0]
    offsets = jnp.concatenate(
        [
            jnp.array([0, TILE, 4096, 0]),
            jnp.stack([left, left + TILE]),
            left + branch,
            left + branch + TILE,
            branch,
        ]
    )
    info = jnp.zeros((INFO_SIZE,), jnp.int32)
    info = info.at[:20].set(limits).at[20].set(last).at[OFFSET_AT : OFFSET_AT + CLASSES].set(offsets)
    return info


def bias_table(rel_bias):
    places = bucket_index(jnp.arange(TILE, dtype=jnp.int32), rel_bias.shape[0])
    pick = (places[:, None] == jnp.arange(rel_bias.shape[0])[None, :]).astype(jnp.float32)
    shifted = rel_bias - rel_bias[-1:]
    return jnp.einsum("db,bh->hd", pick, shifted, precision=lax.Precision.HIGHEST)


def bias_gradient(ahead, behind, offsets, bucket_count):
    heads = ahead.shape[2] // TILE
    lane = jnp.arange(TILE, dtype=jnp.int32)[None, :]
    distance = jnp.stack([offsets[:, None] + lane, offsets[:, None] + lane - TILE], axis=0)
    bucket = bucket_index(jnp.maximum(distance, 0), bucket_count)
    pick = (bucket[..., None] == jnp.arange(bucket_count)).astype(jnp.float32)
    sums = jnp.stack([ahead, behind], axis=0).reshape(2, CLASSES, heads, TILE)
    return jnp.einsum("sclb,schl->bh", pick, sums, precision=lax.Precision.HIGHEST)


EPSILON = 1e-06
SLOT_TILE = 256


def slot_pick(slots, tile, count, axis):
    shape = (SLOT_TILE, count) if axis == 0 else (count, SLOT_TILE)
    places = lax.broadcasted_iota(jnp.int32, shape, axis)
    return (slots - tile * SLOT_TILE == places).astype(jnp.float32).astype(jnp.bfloat16)


def fill_slots(scalars, block, slots, values, out):
    def one(tile, carry):
        at = pl.ds(pl.multiple_of(tile * SLOT_TILE, SLOT_TILE), SLOT_TILE)
        pick = slot_pick(slots, tile, values.shape[0], 0)
        out[at, :] += jnp.dot(pick, values, preferred_element_type=jnp.float32).astype(jnp.bfloat16)
        return carry

    lax.fori_loop(scalars[block] // SLOT_TILE, pl.cdiv(scalars[block + 1], SLOT_TILE), one, 0)


def compact_rows_kernel(scalars, router, slots, named, *refs, blocks, experts):
    stacks, (out, gate) = refs[:-2], refs[-2:]
    rows = [(stack, number) for stack in stacks for number in range(stack.shape[0])]
    out[...] = jnp.zeros_like(out)
    me = scalars[blocks + 1]
    for b, (stack, number) in enumerate(rows):
        values = stack[number]
        fill_slots(scalars, b, slots[b], values, out)
        products = jnp.dot(values, router[...], preferred_element_type=jnp.float32)
        lane = lax.broadcasted_iota(jnp.int32, products.shape, 1)
        lane = jnp.where(lane < 3 * experts, lane % experts, -1)
        choices = [named[b, :, k : k + 1] for k in range(named.shape[2])]
        logits = [
            jnp.sum(jnp.where(lane == choice, products, 0.0), axis=1, keepdims=True) for choice in choices
        ]
        highest = functools.reduce(jnp.maximum, logits)
        powers = [jnp.exp(logit - highest) for logit in logits]
        mine = sum(jnp.where(choice == me, power, 0.0) for choice, power in zip(choices, powers))
        gate[b] = mine / sum(powers)


def whole_calls(kernel, operands, out_shape, name, limit):
    specs = [pl.BlockSpec(memory_space=pltpu.SMEM)]
    specs += [pl.BlockSpec(memory_space=pltpu.VMEM) for _ in operands[1:]]
    return pl.pallas_call(
        kernel,
        in_specs=specs,
        out_specs=jax.tree.map(lambda _: pl.BlockSpec(memory_space=pltpu.VMEM), out_shape),
        out_shape=out_shape,
        compiler_params=pltpu.CompilerParams(vmem_limit_bytes=limit << 20),
        cost_estimate=pl.CostEstimate(flops=10**10, bytes_accessed=3 * 10**7, transcendentals=0),
        name=name,
    )(*operands)


def slot_room(rows):
    return pl.cdiv(rows, SLOT_TILE) * SLOT_TILE


def compact_rows(scalars, router, slots, named, rows, experts):
    (blocks, count), width = slots.shape, rows[0].shape[2]
    return whole_calls(
        functools.partial(compact_rows_kernel, blocks=blocks, experts=experts),
        (scalars, router, slots.reshape(blocks, 1, count), named, *rows),
        [
            jax.ShapeDtypeStruct((slot_room(blocks * count), width), jnp.bfloat16),
            jax.ShapeDtypeStruct((blocks, count, 1), jnp.float32),
        ],
        "compact_rows",
        48,
    )


def compact_grads_kernel(scalars, slots, gate, produced, *refs, blocks):
    stacks, (out, gate_grad) = refs[:-2], refs[-2:]
    rows = [(stack, number) for stack in stacks for number in range(stack.shape[0])]
    out[...] = jnp.zeros_like(out)
    for b, (stack, number) in enumerate(rows):
        wide = stack[number].astype(jnp.float32)
        gate_grad[b] = jnp.sum(wide * produced[b].astype(jnp.float32), axis=1, keepdims=True)
        fill_slots(scalars, b, slots[b], (gate[b] * wide).astype(jnp.bfloat16), out)


def compact_grads(scalars, slots, gate, produced, rows):
    (blocks, count), width = slots.shape, rows[0].shape[2]
    return whole_calls(
        functools.partial(compact_grads_kernel, blocks=blocks),
        (scalars, slots.reshape(blocks, 1, count), gate, produced, *rows),
        [
            jax.ShapeDtypeStruct((slot_room(blocks * count), width), jnp.bfloat16),
            jax.ShapeDtypeStruct((blocks, count, 1), jnp.float32),
        ],
        "compact_grads",
        56,
    )


def expand_kernel(scalars, slots, *refs, blocks, gated):
    gate = refs[0] if gated else None
    rows, out = refs[1:3] if gated else refs
    count = out.shape[1]
    for b in range(blocks):
        out[b] = jnp.zeros(out.shape[1:], out.dtype)

        def one(tile, carry):
            at = pl.ds(pl.multiple_of(tile * SLOT_TILE, SLOT_TILE), SLOT_TILE)
            pick = slot_pick(slots[b], tile, count, 1)
            part = jnp.dot(pick, rows[at, :].astype(jnp.bfloat16), preferred_element_type=jnp.float32)
            out[b] += part.astype(jnp.bfloat16)
            return carry

        lax.fori_loop(scalars[b] // SLOT_TILE, pl.cdiv(scalars[b + 1], SLOT_TILE), one, 0)
        if gated:
            refs[3][b] = out[b]
            out[b] = (gate[b] * out[b].astype(jnp.float32)).astype(jnp.bfloat16)


def expand(scalars, slots, rows, gate=None):
    blocks, count = slots.shape
    shape = jax.ShapeDtypeStruct((blocks, count, rows.shape[1]), jnp.bfloat16)
    operands = (scalars, slots.reshape(blocks, count, 1)) + (() if gate is None else (gate,)) + (rows,)
    outs = whole_calls(
        functools.partial(expand_kernel, blocks=blocks, gated=gate is not None),
        operands, [shape] * (1 if gate is None else 2), "expand", 56,
    )
    return outs[0] if gate is None else outs


GELU_IN = math.sqrt(2.0 / math.pi)
GELU_CUBE = 0.044715


def gelu_parts(pre):
    square = pre * pre
    bent = jnp.tanh(GELU_IN * pre * (1.0 + GELU_CUBE * square))
    half = 0.5 * (1.0 + bent)
    return pre * half, half, bent, square


LAST = (((1,), (1,)), ((), ()))
FIRST = (((0,), (0,)), ((), ()))


def weight_sources(sources, z):
    theirs, sources = sources[0], sources[1:]
    if len(sources) == 1:
        mine = [[(None, sources[0].at[number])] for number in range(sources[0].shape[0])]
        return mine, [[(None, theirs.at[number])] for number in range(theirs.shape[0])]
    own, up_one, down_one, up_two, down_two = sources[:5]
    low, high = z == 0, z == 3
    mine = [
        [(None, own)],
        [(z < 3, down_one), (high, up_one)],
        [(low, down_two), ((z == 1) | (z == 2), up_one), (high, up_two)],
        [(z == 1, down_two), (z == 2, up_two)],
    ]
    others = [[(None, theirs.at[number])] for number in range(3)]
    others.append([((z == 1) | (z == 2), theirs.at[3])])
    if len(sources) == 7:
        mine[3].append((low | high, sources[5]))
        others[3].append((low | high, sources[6]))
    return mine, others


def weight_copies(step, sources, room, sem, act):
    def copy(slot, half, view):
        rows = view.shape[1]
        for matrix in range(3):
            act(
                pltpu.make_async_copy(
                    view.at[matrix],
                    room.at[slot, matrix, pl.ds(half * rows, rows)],
                    sem.at[slot, half * 3 + matrix],
                )
            )

    for half, places in enumerate(sources):
        for number, choices in enumerate(places):
            for condition, view in choices:
                here = step == number if condition is None else (step == number) & condition
                pl.when(here)(functools.partial(copy, number % 2, half, view))


def next_weights(first, sources, room, sem):
    number, steps = pl.program_id(0), pl.num_programs(0)
    step = first + number

    @pl.when(number == 0)
    def _():
        weight_copies(step, sources, room, sem, lambda copy: copy.start())

    @pl.when(number + 1 < steps)
    def _():
        weight_copies(step + 1, sources, room, sem, lambda copy: copy.start())

    weight_copies(step, sources, room, sem, lambda copy: copy.wait())
    return step % 2


def expert_forward_kernel(scalars, rows, *refs, first, sources, aliased):
    weights, refs = refs[:sources], refs[sources:]
    before, refs = (refs[0], refs[1:]) if aliased else (None, refs)
    total, room, sem = refs
    step = pl.program_id(0)
    slot = next_weights(first, weight_sources(weights, scalars[1]), room, sem)

    def one(tile, carry):
        at = pl.ds(pl.multiple_of(tile * SLOT_TILE, SLOT_TILE), SLOT_TILE)
        values = rows[at, :]
        gate_pre = lax.dot_general(values, room[slot, 0], LAST, preferred_element_type=jnp.float32)
        up_pre = lax.dot_general(values, room[slot, 1], LAST, preferred_element_type=jnp.float32)
        inner = (gelu_parts(gate_pre)[0] * up_pre).astype(jnp.bfloat16)
        part = jnp.dot(inner, room[slot, 2], preferred_element_type=jnp.float32)

        @pl.when(step == 0)
        def _():
            total[at, :] = part if before is None else part + before[at, :]

        @pl.when(step > 0)
        def _():
            total[at, :] += part

        return carry

    lax.fori_loop(0, pl.cdiv(scalars[0], SLOT_TILE), one, 0)


def expert_cost(rows, weights, shards, units):
    return pl.CostEstimate(
        flops=2 * units * rows * shards * weights.shape[-2] * 2 * weights.shape[-1],
        bytes_accessed=4 * weights.size,
        transcendentals=0,
    )


def expert_scratch(weights):
    half, width = weights.shape[-2:]
    return [pltpu.VMEM((2, 3, 2 * half, width), jnp.bfloat16), pltpu.SemaphoreType.DMA((2, 6))]


def expert_forward(scalars, rows, weights, first, steps, before=None):
    padded, width = rows.shape
    theirs = weights[0]
    whole = pl.BlockSpec((padded, width), lambda s, scalars: (0, 0), pipeline_mode=pl.Buffered(1))
    extra = () if before is None else (before,)
    return pl.pallas_call(
        functools.partial(
            expert_forward_kernel, first=first, sources=len(weights), aliased=before is not None
        ),
        grid_spec=pltpu.PrefetchScalarGridSpec(
            num_scalar_prefetch=1,
            grid=(steps,),
            in_specs=[whole] + [pl.BlockSpec(memory_space=pl.ANY)] * len(weights) + [whole] * len(extra),
            out_specs=whole,
            scratch_shapes=expert_scratch(theirs),
        ),
        out_shape=jax.ShapeDtypeStruct((padded, width), jnp.float32),
        compiler_params=pltpu.CompilerParams(vmem_limit_bytes=60 << 20),
        cost_estimate=expert_cost(padded, theirs, steps, 3),
        name="expert_forward",
    )(scalars, rows, *weights, *extra)


def expert_backward_kernel(scalars, rows, grads, *refs):
    weights, rest = refs[:-10], refs[-10:]
    mine_gate, theirs_gate, mine_rest, theirs_rest, total = rest[:5]
    gate_total, up_total, down_total, room, sem = rest[5:]
    step = pl.program_id(0)
    slot = next_weights(0, weight_sources(weights, scalars[1]), room, sem)
    gate_total[...] = jnp.zeros_like(gate_total)
    up_total[...] = jnp.zeros_like(up_total)
    down_total[...] = jnp.zeros_like(down_total)

    def one(tile, carry):
        at = pl.ds(pl.multiple_of(tile * SLOT_TILE, SLOT_TILE), SLOT_TILE)
        values, upstream = rows[at, :], grads[at, :]
        gate_pre = lax.dot_general(values, room[slot, 0], LAST, preferred_element_type=jnp.float32)
        up_pre = lax.dot_general(values, room[slot, 1], LAST, preferred_element_type=jnp.float32)
        grad_inner = lax.dot_general(upstream, room[slot, 2], LAST, preferred_element_type=jnp.float32)
        active, half, bent, square = gelu_parts(gate_pre)
        slope = half + (0.5 * GELU_IN) * gate_pre * (1.0 - bent * bent) * (1.0 + 3.0 * GELU_CUBE * square)
        inner = (active * up_pre).astype(jnp.bfloat16)
        grad_gate = (grad_inner * up_pre * slope).astype(jnp.bfloat16)
        grad_up = (grad_inner * active).astype(jnp.bfloat16)
        down_total[...] += lax.dot_general(inner, upstream, FIRST, preferred_element_type=jnp.float32)
        gate_total[...] += lax.dot_general(grad_gate, values, FIRST, preferred_element_type=jnp.float32)
        up_total[...] += lax.dot_general(grad_up, values, FIRST, preferred_element_type=jnp.float32)
        part = jnp.dot(grad_gate, room[slot, 0], preferred_element_type=jnp.float32)
        part = part + jnp.dot(grad_up, room[slot, 1], preferred_element_type=jnp.float32)

        @pl.when(step == 0)
        def _():
            total[at, :] = part

        @pl.when(step > 0)
        def _():
            total[at, :] += part

        return carry

    lax.fori_loop(0, pl.cdiv(scalars[0], SLOT_TILE), one, 0)
    half = mine_gate.shape[2]
    for sums, mine, theirs, number in (
        (gate_total, mine_gate, theirs_gate, 0),
        (up_total, mine_rest, theirs_rest, 0),
        (down_total, mine_rest, theirs_rest, 1),
    ):
        mine[0, number] = sums[:half].astype(jnp.bfloat16)
        theirs[0, number] = sums[half:].astype(jnp.bfloat16)


def expert_backward(scalars, rows, grads, weights):
    padded, width = rows.shape
    theirs = weights[0]
    shards, _, half, _ = theirs.shape
    whole = pl.BlockSpec((padded, width), lambda s, scalars: (0, 0), pipeline_mode=pl.Buffered(1))
    out = lambda count: pl.BlockSpec(
        (1, count, half, width), lambda s, scalars: (scalars[2 + s], 0, 0, 0)
    )
    shape = lambda count: jax.ShapeDtypeStruct((shards, count, half, width), jnp.bfloat16)
    return pl.pallas_call(
        expert_backward_kernel,
        grid_spec=pltpu.PrefetchScalarGridSpec(
            num_scalar_prefetch=1,
            grid=(shards,),
            in_specs=[whole, whole] + [pl.BlockSpec(memory_space=pl.ANY)] * len(weights),
            out_specs=[out(1), out(1), out(2), out(2), whole],
            scratch_shapes=[pltpu.VMEM((2 * half, width), jnp.float32)] * 3 + expert_scratch(theirs),
        ),
        out_shape=[shape(1), shape(1), shape(2), shape(2), jax.ShapeDtypeStruct((padded, width), jnp.float32)],
        compiler_params=pltpu.CompilerParams(vmem_limit_bytes=60 << 20),
        cost_estimate=expert_cost(padded, theirs, shards, 8),
        name="expert_backward",
    )(scalars, rows, grads, *weights)


def project_kernel(weights, rows, q, k, k_t, v, v_t):
    columns = q.shape[1]
    low = jnp.dot(rows[...], weights[...], preferred_element_type=jnp.float32).astype(jnp.bfloat16)
    q[...] = low[:, :columns]
    k[...] = low[:, columns : 2 * columns]
    v[...] = low[:, 2 * columns :]
    k_t[...] = jnp.transpose(low[:, columns : 2 * columns])
    v_t[...] = jnp.transpose(low[:, 2 * columns :])


def project(weights, rows):
    length, width = rows.shape
    columns = weights.shape[1] // 3
    count = 2 * TILE
    tall = pl.BlockSpec((count, columns), lambda i: (i, 0))
    wide = pl.BlockSpec((columns, count), lambda i: (0, i))
    tall_shape = jax.ShapeDtypeStruct((length, columns), jnp.bfloat16)
    wide_shape = jax.ShapeDtypeStruct((columns, length), jnp.bfloat16)
    return pl.pallas_call(
        project_kernel,
        grid=(length // count,),
        in_specs=[
            pl.BlockSpec(weights.shape, lambda i: (0, 0)),
            pl.BlockSpec((count, width), lambda i: (i, 0)),
        ],
        out_specs=[tall, tall, wide, tall, wide],
        out_shape=[tall_shape, tall_shape, wide_shape, tall_shape, wide_shape],
        compiler_params=pltpu.CompilerParams(vmem_limit_bytes=40 << 20),
        cost_estimate=pl.CostEstimate(flops=10**10, bytes_accessed=2 * 10**7, transcendentals=0),
        name="project",
    )(weights, rows)


def split_float(values):
    high = values.astype(jnp.bfloat16)
    rest = values - high.astype(jnp.float32)
    middle = rest.astype(jnp.bfloat16)
    low = (rest - middle.astype(jnp.float32)).astype(jnp.bfloat16)
    return jnp.concatenate([high, middle, low], axis=1)


def join_float(products, count):
    return products[:, 2 * count :] + products[:, count : 2 * count] + products[:, :count]


def swap(array, axis, bit):
    size = lax.axis_size(axis)
    return lax.ppermute(array, axis, [(i, i ^ bit) for i in range(size)])


def sum_over(array, axes):
    for axis in axes:
        bit = 1
        while bit < lax.axis_size(axis):
            array = array + swap(array, axis, bit)
            bit *= 2
    return array


def ring_layer():
    return lax.axis_size("expert") == 4


def layer_member(number):
    return lax.axis_index("expert") ^ number if ring_layer() else number


def layer_gather(rows):
    columns = lax.axis_size("expert")
    if not ring_layer():
        stacked = lax.all_gather(rows, "expert", axis=0)
        return [stacked[number] for number in range(columns)]
    half = rows.shape[0] // 2
    top, bottom = rows[:half], rows[half:]
    x_top, y_bottom = swap(top, "expert", 1), swap(bottom, "expert", 2)
    x_bottom, y_top = swap(bottom, "expert", 1), swap(top, "expert", 2)
    far_top, far_bottom = swap(x_top, "expert", 2), swap(y_bottom, "expert", 1)
    return [top, bottom, x_top, x_bottom, y_top, y_bottom, far_top, far_bottom]


def layer_scatter(parts):
    if not ring_layer():
        return lax.psum_scatter(parts, "expert", scatter_dimension=0, tiled=False).astype(jnp.float32)
    _, half, width = parts.shape
    block = jax.ShapeDtypeStruct((half, width), jnp.float32)
    low, high = pl.pallas_call(
        scatter_kernel,
        in_specs=[pl.BlockSpec(memory_space=pltpu.VMEM)],
        out_specs=[pl.BlockSpec(memory_space=pltpu.VMEM)] * 2,
        out_shape=[block, block],
        scratch_shapes=[pltpu.VMEM((6, half, width), jnp.bfloat16), pltpu.SemaphoreType.DMA((2, 6))],
        compiler_params=pltpu.CompilerParams(
            collective_id=6, has_side_effects=True, vmem_limit_bytes=40 << 20
        ),
        cost_estimate=pl.CostEstimate(flops=5 * 10**10, bytes_accessed=10**7, transcendentals=0),
        name="layer_scatter",
    )(parts)
    return jnp.concatenate([low, high], axis=0)


def scatter_kernel(parts, low_out, high_out, room, sems):
    column = lax.axis_index("expert")
    greet([{"expert": column ^ 1}, {"expert": column ^ 2}])
    halves = lambda ref, owner, side: ref.at[2 * (owner ^ column) + side]
    onward, terms, finish = ring_scatter(parts, halves, room, sems, 0)
    onward()
    low, high = terms()
    low_out[...] = sum(block[...].astype(jnp.float32) for block in low)
    high_out[...] = sum(block[...].astype(jnp.float32) for block in high)
    finish()


def layer_small(array):
    columns = lax.axis_size("expert")
    if not ring_layer():
        return lax.all_gather(array, "expert", axis=0)
    return jnp.stack([array] + [swap(array, "expert", number) for number in range(1, columns)])


def layer_trade(array):
    if not ring_layer():
        return lax.all_to_all(array, "expert", split_axis=0, concat_axis=0, tiled=True)
    return jnp.stack([array[0]] + [swap(array[n], "expert", n) for n in range(1, array.shape[0])])


def split_trees():
    return lax.axis_size("shard") == 4 and lax.axis_size("dp") == 2 and ring_layer()


def my_place():
    z, core = lax.axis_index("shard"), lax.axis_index("dp")
    return z, core, z // 2, 2 * (z % 2) + core


def rows_to_heads(grads, shards):
    rows, width = grads.shape
    pieces = grads.reshape(rows, shards, width // shards).transpose(1, 0, 2)
    pieces = lax.all_to_all(pieces, "shard", split_axis=0, concat_axis=0, tiled=True)
    return pieces.reshape(shards * rows, width // shards)


def hop(array, pairs):
    return lax.ppermute(array, "shard", pairs)


def weight_hop_one(own):
    if not split_trees():
        return (lax.all_gather(own, "shard", axis=0),)
    return hop(own, [(0, 1), (1, 2), (2, 3)]), hop(own, [(1, 0), (2, 1), (3, 2)])


def weight_last_hop(two):
    z = lax.axis_index("shard")
    return hop(jnp.where(z == 1, two[1], two[0]), [(1, 0), (2, 3)])


def weight_shards():
    z = lax.axis_index("shard")
    if not split_trees():
        return jnp.arange(lax.axis_size("shard"), dtype=jnp.int32)
    places = [
        z,
        jnp.where(z == 3, 2, z + 1),
        jnp.where(z == 0, 2, jnp.where(z == 3, 1, z - 1)),
        jnp.where(z < 2, 3, 0),
    ]
    return jnp.stack(places).astype(jnp.int32)


def greet(devices):
    barrier = pltpu.get_barrier_semaphore()
    for device in devices:
        pl.semaphore_signal(barrier, inc=1, device_id=device, device_id_type=pl.DeviceIdType.MESH)
    pl.semaphore_wait(barrier, len(devices))


def send_to(source, target, sems, number, device):
    return pltpu.make_async_remote_copy(
        src_ref=source,
        dst_ref=target,
        send_sem=sems.at[0, number],
        recv_sem=sems.at[1, number],
        device_id=device,
        device_id_type=pl.DeviceIdType.MESH,
    )


def other_places():
    column, z, core = (lax.axis_index(name) for name in ("expert", "shard", "dp"))
    others = [
        {"shard": z ^ number, "dp": core ^ side} for number in range(4) for side in range(2) if number + side
    ]
    return others + [{"expert": column ^ 1}, {"expert": column ^ 2}]


def chip_role():
    z = lax.axis_index("shard")
    tree = z // 2
    at_end = (z == 0) | (z == 3)
    partner = z ^ 1
    across = 3 - z
    return z, tree, at_end, partner, across, lambda number: jnp.where(tree == 0, number, 3 - number)


PIECES = 2


def gather_kernel(
    own, three, out, pack,
    rows, three_all, out_all, packs, three_mine, out_mine, passing, lent, here, sems,
):
    column, core = lax.axis_index("expert"), lax.axis_index("dp")
    z, tree, at_end, partner, across, seat = chip_role()
    in_middle = jnp.logical_not(at_end)
    beside, above, twin = {"expert": column ^ 1}, {"expert": column ^ 2}, {"dp": core ^ 1}
    to_partner, to_across = {"shard": partner}, {"shard": across}
    greet(near_places())
    keeps = core == tree
    lend = send_to(own.at[core ^ 1], lent, sems, 4, twin)
    lend.start()

    group = 2 * (z % 2) + core
    stays = (group == z) & keeps
    group_place = {"shard": 2 * core + z // 2, "dp": z % 2}
    local_three = pltpu.make_async_copy(three, three_mine, here.at[0])
    sent_three = send_to(three, three_mine, sems, 12, group_place)
    pl.when(stays)(local_three.start)
    pl.when(jnp.logical_not(stays))(sent_three.start)
    local_packs = [pltpu.make_async_copy(pack, packs.at[8 * n], here.at[5 + n]) for n in range(2)]
    pack_on = send_to(pack, packs.at[8], sems, 43, group_place)
    spread = [
        send_to(
            pack, packs.at[2 * n + side], sems, 35 + 2 * n + side,
            {"expert": column ^ n, "dp": core ^ side},
        )
        for n in range(4)
        for side in range(2)
        if n + side
    ]
    for copy in spread:
        copy.start()
    local_packs[0].start()
    pl.when(stays)(local_packs[1].start)
    pl.when(jnp.logical_not(stays))(pack_on.start)

    height = lent.shape[0] // PIECES
    piece = lambda ref, k: ref.at[pl.ds(k * height, height)]
    mine = lambda place, k: rows.at[place, core, pl.ds(k * height, height)]
    each = range(PIECES)

    def along(source, target, number, k, device, arrival=None):
        at = lambda n: 44 + PIECES * n + k
        return pltpu.make_async_remote_copy(
            src_ref=source,
            dst_ref=target,
            send_sem=sems.at[0, at(number)],
            recv_sem=sems.at[1, at(number if arrival is None else arrival)],
            device_id=device,
            device_id_type=pl.DeviceIdType.MESH,
        )

    def start_both(tree_rows, other_rows):
        @pl.when(at_end)
        def _():
            others = [along(piece(other_rows, k), piece(passing, k), 5, k, to_partner) for k in each]
            for copy in others:
                copy.start()
            for copy in others:
                copy.wait_send()
            for k in each:
                along(piece(tree_rows, k), mine(z, k), 0, k, to_partner).start()

        @pl.when(in_middle)
        def _():
            for k in each:
                along(piece(tree_rows, k), mine(z, k), 1, k, to_partner).start()
                along(piece(other_rows, k), mine(z, k), 2, k, to_across).start()

    lend.wait_recv()

    @pl.when(keeps)
    def _():
        start_both(own.at[core], lent)

    @pl.when(jnp.logical_not(keeps))
    def _():
        start_both(lent, own.at[core])

    whole_block = pltpu.make_async_copy(own, rows.at[z], here.at[1])
    block_to_twin = send_to(own, rows.at[z], sems, 11, twin)

    @pl.when(keeps)
    def _():
        whole_block.start()
        block_to_twin.start()

    keep = pltpu.make_async_copy(out, out_mine.at[z], here.at[3])
    keep.start()
    pieces = [send_to(out, out_mine.at[z], sems, 12 + n, {"shard": z ^ n}) for n in range(1, 4)]
    for copy in pieces:
        copy.start()

    pl.when(stays)(local_three.wait)
    pl.when(jnp.logical_not(stays))(sent_three.wait)
    quarter = three_mine.shape[0]
    half = quarter // 2

    def three_half(owner, side):
        return three_all.at[pl.ds(pl.multiple_of(owner * quarter + side * half, half), half)]

    top, bottom = three_mine.at[pl.ds(0, half)], three_mine.at[pl.ds(half, half)]
    first = [
        send_to(top, three_half(column, 0), sems, 16, beside),
        send_to(bottom, three_half(column, 1), sems, 17, above),
        send_to(bottom, three_half(column, 1), sems, 18, beside),
        send_to(top, three_half(column, 0), sems, 19, above),
    ]
    for copy in first:
        copy.start()
    local_all = pltpu.make_async_copy(
        three_mine, three_all.at[pl.ds(pl.multiple_of(column * quarter, quarter), quarter)], here.at[2]
    )
    local_all.start()

    def arrive(number, k):
        block = mine(seat(number), k)
        along(piece(lent, k), block, number, k, to_partner).wait_recv()
        along(block, block, 8 + number, k, twin).start()
        return block

    @pl.when(in_middle)
    def _():
        for k in each:
            along(piece(lent, k), piece(passing, k), 5, k, to_partner).wait_recv()
            along(piece(passing, k), mine(partner, k), 3, k, to_across).start()
            block = arrive(2, k)
            along(block, block, 6, k, to_partner, 2).start()

    @pl.when(at_end)
    def _():
        for k in each:
            arrive(1, k)

    keep.wait()
    for copy in pieces:
        copy.wait()
    halves = [out_mine.at[pl.ds(0, 2)], out_mine.at[pl.ds(2, 2)]]
    place = lambda owner, side, owner_core: out_all.at[pl.ds(2 * side, 2), owner, owner_core]
    third = [
        send_to(halves[0], place(column, 0, core), sems, 20, beside),
        send_to(halves[1], place(column, 1, core), sems, 21, above),
        send_to(halves[1], place(column, 1, core), sems, 22, beside),
        send_to(halves[0], place(column, 0, core), sems, 23, above),
    ]
    for copy in third:
        copy.start()
    whole = lambda owner, owner_core: out_all.at[:, owner, owner_core]
    keep_all = pltpu.make_async_copy(out_mine, whole(column, core), here.at[4])
    keep_all.start()
    to_twin = [send_to(out_mine, whole(column, core), sems, 31, twin)]
    to_twin[0].start()
    first[0].wait_recv()
    first[1].wait_recv()
    second = [
        send_to(three_half(column ^ 1, 0), three_half(column ^ 1, 0), sems, 24, above),
        send_to(three_half(column ^ 2, 1), three_half(column ^ 2, 1), sems, 25, beside),
    ]
    for copy in second:
        copy.start()

    @pl.when(in_middle)
    def _():
        for k in each:
            block = arrive(3, k)
            along(block, block, 7, k, to_partner, 3).start()
        for k in each:
            arrive(0, k)

    third[0].wait_recv()
    third[1].wait_recv()
    fourth = [
        send_to(place(column ^ 1, 0, core), place(column ^ 1, 0, core), sems, 26, above),
        send_to(place(column ^ 2, 1, core), place(column ^ 2, 1, core), sems, 27, beside),
    ]
    for copy in fourth:
        copy.start()

    @pl.when(at_end)
    def _():
        for k in each:
            arrive(2, k)

    third[2].wait_recv()
    third[3].wait_recv()
    for copy in fourth:
        copy.wait_recv()
    for number in range(1, 4):
        block = whole(column ^ number, core)
        to_twin.append(send_to(block, block, sems, 31 + number, twin))
        to_twin[number].start()
    local_all.wait()
    keep_all.wait()
    for copy in (first[2], first[3], second[0], second[1]):
        copy.wait_recv()
    for copy in first + second + third + fourth:
        copy.wait_send()
    for copy in to_twin:
        copy.wait()

    @pl.when(at_end)
    def _():
        for k in each:
            arrive(3, k)

    lend.wait_send()
    for copy in spread:
        copy.wait()
    local_packs[0].wait()
    pl.when(stays)(local_packs[1].wait)
    pl.when(jnp.logical_not(stays))(pack_on.wait)

    def settle(sent, traded):
        for k in each:
            for number in sent:
                along(piece(lent, k), mine(z, k), number, k, to_partner).wait_send()
            for number in traded:
                along(piece(lent, k), mine(z, k), 8 + number, k, twin).wait()

    pl.when(at_end)(functools.partial(settle, (0,), (1, 2, 3)))
    pl.when(in_middle)(functools.partial(settle, (1, 2, 3, 6, 7), (0, 2, 3)))

    @pl.when(keeps)
    def _():
        whole_block.wait()
        block_to_twin.wait_send()

    @pl.when(jnp.logical_not(keeps))
    def _():
        block_to_twin.wait_recv()


def exchange_call(kernel, operands, out_shape, sems, scratch, number, name, cost=5 * 10**10):
    anywhere = pl.BlockSpec(memory_space=pl.ANY)
    return pl.pallas_call(
        kernel,
        in_specs=[anywhere] * len(operands),
        out_specs=[anywhere] * len(out_shape),
        out_shape=[
            shape if hasattr(shape, "dtype") else jax.ShapeDtypeStruct(shape, jnp.bfloat16)
            for shape in out_shape
        ],
        scratch_shapes=list(scratch) + [pltpu.SemaphoreType.DMA((2, sems))],
        compiler_params=pltpu.CompilerParams(
            collective_id=number, has_side_effects=True, vmem_limit_bytes=48 << 20
        ),
        cost_estimate=pl.CostEstimate(flops=cost, bytes_accessed=10**6, transcendentals=0),
        name=name,
    )(*operands)


def gather_tree(own, three, out, pack):
    part, width = out.shape
    half = own.shape[0] // 2
    own = own.reshape(2, half, width)
    rows, three_all, out_all, packs, _, _, _, _ = exchange_call(
        gather_kernel,
        (own, three, out, pack),
        [
            (4, 2, half, width),
            (4 * three.shape[0], three.shape[1]),
            (4, 4, 2, part, width),
            jax.ShapeDtypeStruct((9,) + pack.shape, pack.dtype),
            three.shape,
            (4, part, width),
            (half, width),
            (half, width),
        ],
        44 + 12 * PIECES,
        [pltpu.SemaphoreType.DMA((7,))],
        2,
        "gather_tree",
    )
    return rows.reshape(-1, width), three_all, out_all.reshape(-1, width), packs


SLICES = 4


def heads_kernel(attended, heads, here, sems):
    z, core = lax.axis_index("shard"), lax.axis_index("dp")
    greet(other_places())
    tree, group = z // 2, 2 * (z % 2) + core
    rows = heads.shape[2]

    height = heads.shape[1] // SLICES

    def copies(turn, slice_number):
        place = (group + turn) % 4
        features = pl.ds(slice_number * height, height)
        piece = attended.at[features, pl.ds(pl.multiple_of(place * rows, TILE), rows)]
        target = heads.at[group, features]
        local = pltpu.make_async_copy(piece, target, here.at[slice_number])
        sent = send_to(piece, target, sems, turn * SLICES + slice_number, {"shard": place, "dp": tree})
        return local, sent, (place == z) & (tree == core)

    steps = [(turn, number) for turn in range(4) for number in range(SLICES)]
    for step in steps:
        local, sent, stays = copies(*step)
        pl.when(stays)(local.start)
        pl.when(jnp.logical_not(stays))(sent.start)
    for step in steps:
        local, sent, stays = copies(*step)
        pl.when(stays)(local.wait)
        pl.when(jnp.logical_not(stays))(sent.wait_send)
        from_me = ((z - step[0]) % 4 == group) & (tree == core)
        pl.when(jnp.logical_not(from_me))(sent.wait_recv)


def trade_heads(attended_t):
    columns, length = attended_t.shape
    (heads,) = exchange_call(
        heads_kernel,
        (attended_t,),
        [(4, columns, length // 4)],
        4 * SLICES,
        [pltpu.SemaphoreType.DMA((SLICES,))],
        3,
        "trade_heads",
    )
    return heads.reshape(4 * columns, length // 4)


def add_low(*blocks):
    return sum(block.astype(jnp.float32) for block in blocks).astype(jnp.bfloat16)


def near_places():
    column, core = lax.axis_index("expert"), lax.axis_index("dp")
    layer = [{"expert": column ^ n, "dp": core ^ side} for n in range(1, 4) for side in range(2)]
    return other_places()[:7] + layer


def ring_scatter(sums, halves, room, sems, base):
    column = lax.axis_index("expert")
    beside, above = {"expert": column ^ 1}, {"expert": column ^ 2}
    first = [
        send_to(halves(sums, column ^ 3, 0), room.at[0], sems, base, beside),
        send_to(halves(sums, column ^ 3, 1), room.at[1], sems, base + 1, above),
        send_to(halves(sums, column ^ 1, 0), room.at[2], sems, base + 2, beside),
        send_to(halves(sums, column ^ 2, 1), room.at[3], sems, base + 3, above),
    ]
    for copy in first:
        copy.start()
    second = [
        send_to(room.at[0], room.at[4], sems, base + 4, above),
        send_to(room.at[1], room.at[5], sems, base + 5, beside),
    ]

    def onward():
        for number, (owner, side) in enumerate(((column ^ 2, 0), (column ^ 1, 1))):
            first[number].wait_recv()
            room[number] = add_low(halves(sums, owner, side)[...], room[number])
            second[number].start()

    def terms():
        for copy in (first[2], first[3], second[0], second[1]):
            copy.wait_recv()
        low = (halves(sums, column, 0)[...], room[2], room[4])
        high = (halves(sums, column, 1)[...], room[3], room[5])
        return low, high

    def finish():
        for copy in first + second:
            copy.wait_send()

    return onward, terms, finish


def back_kernel(
    grads, out, heads, out_sum, lent, sums, room, quarter, pieces, total, here, sems
):
    column, core = lax.axis_index("expert"), lax.axis_index("dp")
    z, tree, at_end, partner, across, seat = chip_role()
    twin = {"dp": core ^ 1}
    greet(near_places())
    group = 2 * (z % 2) + core
    columns = heads.shape[2]
    part = lent.shape[2]
    lend = send_to(out.at[:, :, pl.ds((core ^ 1) * part, part)], lent, sems, 4, twin)
    lend.start()

    height = heads.shape[1] // SLICES

    def turn_copies(turn, k):
        to_group = (z - turn) % 4
        rows = pl.ds(k * height, height)
        piece = grads.at[rows, pl.ds(pl.multiple_of(to_group * columns, TILE), columns)]
        place, side = 2 * core + to_group // 2, to_group % 2
        target = heads.at[z, rows]
        local = pltpu.make_async_copy(piece, target, here.at[3 + k])
        sent = send_to(piece, target, sems, 21 + turn * SLICES + k, {"shard": place, "dp": side})
        return local, sent, (place == z) & (side == core)

    steps = [(turn, k) for turn in range(4) for k in range(SLICES)]
    for step in steps:
        local, sent, stays = turn_copies(*step)
        pl.when(stays)(local.start)
        pl.when(jnp.logical_not(stays))(sent.start)

    mine = pltpu.make_async_copy(out.at[:, :, pl.ds(core * part, part)], sums, here.at[1])
    mine.start()
    mine.wait()
    lend.wait_recv()
    sums[...] = add_low(sums[...], lent[...])

    def halves(ref, owner, side):
        return ref.at[pl.ds(2 * side, 2), owner]

    onward, terms, finish = ring_scatter(sums, halves, room, sems, 5)
    onward()
    low, high = terms()
    quarter[:2] = add_low(*low)
    quarter[2:] = add_low(*high)
    copies = [
        send_to(quarter.at[z ^ n], pieces.at[n - 1], sems, 10 + n, {"shard": z ^ n}) for n in range(1, 4)
    ]
    for copy in copies:
        copy.start()
    for copy in copies:
        copy.wait()
    total[...] = add_low(quarter[z], pieces[0], pieces[1], pieces[2])
    spread = [
        send_to(
            total, out_sum.at[column, core], sems, 13 + 2 * n + side,
            {"expert": column ^ n, "dp": core ^ side},
        )
        for n in range(4)
        for side in range(2)
        if n + side
    ]
    for copy in spread:
        copy.start()
    keep = pltpu.make_async_copy(total, out_sum.at[column, core], here.at[2])
    keep.start()
    keep.wait()
    for copy in spread:
        copy.wait()
    finish()
    lend.wait_send()
    for step in steps:
        local, sent, stays = turn_copies(*step)
        pl.when(stays)(local.wait)
        pl.when(jnp.logical_not(stays))(sent.wait_send)
        from_me = ((group + step[0]) % 4 == z) & (tree == core)
        pl.when(jnp.logical_not(from_me))(sent.wait_recv)


def trade_back(grads, out):
    rows, width = grads.shape
    part = width // 32
    low = jnp.bfloat16
    heads, out_sum = exchange_call(
        back_kernel,
        (grads, out.reshape(4, 4, 2 * part, width)),
        [(4, rows, width // 4), (4, 2, part, width)],
        21 + 4 * SLICES,
        [
            pltpu.VMEM((4, 4, part, width), low),
            pltpu.VMEM((4, 4, part, width), low),
            pltpu.VMEM((6, 2, part, width), low),
            pltpu.VMEM((4, part, width), low),
            pltpu.VMEM((3, part, width), low),
            pltpu.VMEM((part, width), low),
            pltpu.SemaphoreType.DMA((3 + SLICES,)),
        ],
        4,
        "trade_back",
        10**6,
    )
    return heads.reshape(4 * rows, width // 4), out_sum.reshape(-1, width)


def last_kernel(
    parts, three, small, total, three_all, small_all,
    lent, forth, arrived, leave, room, quarter, moved, other, mine_half, small_room, here, sems,
):
    column, core = lax.axis_index("expert"), lax.axis_index("dp")
    z, tree, at_end, partner, across, seat = chip_role()
    in_middle = jnp.logical_not(at_end)
    twin, to_partner, to_across = {"dp": core ^ 1}, {"shard": partner}, {"shard": across}
    greet(near_places())
    keeps = core == tree

    def lend(turn):
        block = seat(jnp.where(at_end, 3 - turn, (4 - turn) % 4))
        return block, send_to(parts.at[block, core ^ 1], lent.at[block], sems, turn, twin)

    height = lent.shape[1] // PIECES
    each = range(PIECES)
    piece = lambda ref, k: ref.at[pl.ds(k * height, height)]

    def along(source, target, number, device, arrival=None):
        at = lambda n, k: 33 + PIECES * n + k
        return [
            pltpu.make_async_remote_copy(
                src_ref=piece(source, k),
                dst_ref=piece(target, k),
                send_sem=sems.at[0, at(number, k)],
                recv_sem=sems.at[1, at(number if arrival is None else arrival, k)],
                device_id=device,
                device_id_type=pl.DeviceIdType.MESH,
            )
            for k in each
        ]

    def start_all(copies):
        for copy in copies:
            copy.start()

    for turn in range(4):
        lend(turn)[1].start()
    rows = three.shape[1] // 2

    def halves(ref, owner, side):
        return ref.at[owner, pl.ds(side * rows, rows)]

    onward, terms, finish = ring_scatter(three, halves, room, sems, 4)
    partners = [
        twin, {"expert": column ^ 1}, {"expert": column ^ 2}, {"shard": z ^ 1}, {"shard": z ^ 2}
    ]
    small_all[...] = small[...]

    def small_copy(stage):
        return send_to(small_room.at[stage], small_room.at[5 + stage], sems, 20 + stage, partners[stage])

    def small_start(stage):
        small_room[stage] = small_all[...]
        small_copy(stage).start()

    def small_end(stage):
        small_copy(stage).wait()
        small_all[...] += small_room[5 + stage]

    small_start(0)

    def chip_sum(turn):
        block, copy = lend(turn)
        copy.wait_recv()
        lent[block] = add_low(parts[block, core], lent[block])
        return lent.at[block]

    def end_send(turn):
        start_all(along(chip_sum(turn), forth.at[turn], turn, to_partner))

    pl.when(at_end)(functools.partial(end_send, 0))

    @pl.when(in_middle)
    def _():
        start_all(along(chip_sum(0), forth.at[0], 0, to_partner))

    small_end(0)
    small_start(1)
    onward()
    pl.when(at_end)(functools.partial(end_send, 1))
    small_end(1)
    small_start(2)

    def middle_sum(turn, onwards=None):
        block = chip_sum(turn)
        copies = None if onwards is None else onwards(block)
        for k, arrival in enumerate(along(forth.at[0], forth.at[turn - 1], turn - 1, to_partner)):
            arrival.wait_recv()
            at = pl.ds(k * height, height)
            block[at] = add_low(block[at], forth[turn - 1, at])
            if copies is not None:
                copies[k].start()

    @pl.when(in_middle)
    def _():
        middle_sum(1, lambda block: along(block, arrived, 3, {"shard": across ^ 1}))

    low, high = terms()
    quarter[:rows] = add_low(*low)
    quarter[rows:] = add_low(*high)
    group = 2 * (z % 2) + core
    stays = (group == z) & keeps
    keep = pltpu.make_async_copy(quarter, moved, here.at[0])
    move_on = send_to(quarter, moved, sems, 14, {"shard": group, "dp": tree})
    pl.when(stays)(keep.start)
    pl.when(jnp.logical_not(stays))(move_on.start)
    pl.when(at_end)(functools.partial(end_send, 2))

    small_end(2)
    small_start(3)

    @pl.when(in_middle)
    def _():
        middle_sum(2, lambda block: along(block, arrived, 4, to_across, 3))

    pl.when(stays)(keep.wait)
    pl.when(jnp.logical_not(stays))(move_on.wait)
    swapped = send_to(moved, other, sems, 16, twin)
    swapped.start()
    small_end(3)
    small_start(4)
    swapped.wait()
    at = pl.ds(pl.multiple_of(core * rows, 8), rows)
    mine_half[...] = add_low(moved[at], other[at])
    target = three_all.at[column, core]
    spread = [
        send_to(mine_half, target, sems, 25 + 2 * n + side, {"expert": column ^ n, "dp": core ^ side})
        for n in range(4)
        for side in range(2)
        if n + side
    ]
    for copy in spread:
        copy.start()
    keep_half = pltpu.make_async_copy(mine_half, target, here.at[1])
    keep_half.start()
    small_end(4)

    @pl.when(at_end)
    def _():
        block = chip_sum(3)
        for copy in along(forth.at[0], forth.at[0], 0, to_partner):
            copy.wait_recv()
        block[...] = add_low(block[...], forth[0])

    @pl.when(in_middle)
    def _():
        middle_sum(3)

    mine = lent.at[z]
    for copy in along(forth.at[0], arrived, 3, to_partner):
        copy.wait_recv()

    @pl.when(keeps)
    def _():
        total[core] = mine[...]
        leave[...] = arrived[...]

    @pl.when(jnp.logical_not(keeps))
    def _():
        total[core] = arrived[...]
        leave[...] = mine[...]

    last = send_to(leave, total.at[core], sems, 17, twin)
    last.start()

    keep_half.wait()
    for copy in spread:
        copy.wait()
    finish()
    for turn in range(4):
        lend(turn)[1].wait_send()

    def settle(numbers):
        for number in numbers:
            for copy in along(forth.at[0], forth.at[1], number, to_partner):
                copy.wait_send()

    pl.when(at_end)(functools.partial(settle, (0, 1, 2)))
    pl.when(in_middle)(functools.partial(settle, (0, 3, 4)))
    last.wait()


def reduce_last(parts, three, small):
    blocks, rows, width = parts.shape
    columns = three.shape[1]
    half, quarter = rows // 2, width // 4
    low = jnp.bfloat16
    vmem = pl.BlockSpec(memory_space=pltpu.VMEM)
    block = pltpu.VMEM((half, width), low)
    total, three_all, small_all = pl.pallas_call(
        last_kernel,
        in_specs=[vmem] * 3,
        out_specs=[vmem] * 3,
        out_shape=[
            jax.ShapeDtypeStruct((2, half, width), low),
            jax.ShapeDtypeStruct((4, 2, quarter // 2, columns), low),
            jax.ShapeDtypeStruct(small.shape, jnp.float32),
        ],
        scratch_shapes=[
            pltpu.VMEM((4, half, width), low),
            pltpu.VMEM((3, half, width), low),
            block,
            block,
            pltpu.VMEM((6, quarter // 2, columns), low),
            pltpu.VMEM((quarter, columns), low),
            pltpu.VMEM((quarter, columns), low),
            pltpu.VMEM((quarter, columns), low),
            pltpu.VMEM((quarter // 2, columns), low),
            pltpu.VMEM((10,) + small.shape, jnp.float32),
            pltpu.SemaphoreType.DMA((2,)),
            pltpu.SemaphoreType.DMA((2, 33 + 5 * PIECES)),
        ],
        compiler_params=pltpu.CompilerParams(
            collective_id=5, has_side_effects=True, vmem_limit_bytes=48 << 20
        ),
        cost_estimate=pl.CostEstimate(flops=5 * 10**10, bytes_accessed=10**7, transcendentals=0),
        name="reduce_last",
    )(parts.reshape(blocks, 2, half, width), three.reshape(4, quarter, columns), small)
    return total.reshape(rows, width), three_all.reshape(width, columns), small_all


def meet_kernel(rows, own, up_one, down_one, layer, theirs, up_two, down_two, sems):
    column, z = lax.axis_index("expert"), lax.axis_index("shard")
    beside, above = {"expert": column ^ 1}, {"expert": column ^ 2}
    twin = {"dp": lax.axis_index("dp") ^ 1}
    greet(other_places())
    x_top = send_to(rows.at[0], layer.at[0], sems, 0, beside)
    y_bottom = send_to(rows.at[1], layer.at[3], sems, 1, above)
    x_bottom = send_to(rows.at[1], layer.at[1], sems, 2, beside)
    y_top = send_to(rows.at[0], layer.at[2], sems, 3, above)
    for copy in (x_top, y_bottom, x_bottom, y_top):
        copy.start()

    between = (z == 1) | (z == 2)
    hop_up = [send_to(up_one.at[m], up_two.at[m], sems, 12 + m, {"shard": z + 1}) for m in range(3)]
    hop_down = [send_to(down_one.at[m], down_two.at[m], sems, 15 + m, {"shard": z - 1}) for m in range(3)]

    @pl.when(between)
    def _():
        for copy in hop_up + hop_down:
            copy.start()

    low, high = z == 0, z == 3

    def to_twin(view, place):
        return send_to(view, theirs.at[place], sems, 8 + place, twin)

    to_twin(own, 0).start()
    pl.when(z < 3)(to_twin(down_one, 1).start)
    pl.when(high)(to_twin(up_one, 1).start)
    pl.when(between)(to_twin(up_one, 2).start)

    x_top.wait_recv()
    far_top = send_to(layer.at[0], layer.at[4], sems, 4, above)
    far_top.start()
    y_bottom.wait_recv()
    far_bottom = send_to(layer.at[3], layer.at[5], sems, 5, beside)
    far_bottom.start()

    for copy in (x_top, y_bottom):
        copy.wait_send()
    for copy in (x_bottom, y_top, far_top, far_bottom):
        copy.wait()

    @pl.when(z >= 2)
    def _():
        for copy in hop_up:
            copy.wait_recv()

    @pl.when(z <= 1)
    def _():
        for copy in hop_down:
            copy.wait_recv()

    pl.when(low)(to_twin(down_two, 2).start)
    pl.when(high)(to_twin(up_two, 2).start)
    pl.when(z == 1)(to_twin(down_two, 3).start)
    pl.when(z == 2)(to_twin(up_two, 3).start)

    @pl.when(between)
    def _():
        for copy in hop_up + hop_down:
            copy.wait_send()
        to_twin(own, 3).wait()

    for place in range(3):
        to_twin(own, place).wait()


def meet(rows, own, one):
    half = rows.shape[0] // 2
    halves = rows.reshape(2, half, rows.shape[1])
    layer, theirs, up_two, down_two = exchange_call(
        meet_kernel,
        (halves, own, *one),
        [(6,) + halves.shape[1:], (4,) + own.shape, own.shape, own.shape],
        18,
        [],
        1,
        "meet",
    )
    return [halves, layer], theirs, (up_two, down_two)


def heads_to_rows(attended_t, shards):
    columns, length = attended_t.shape
    pieces = attended_t.reshape(columns, shards, length // shards).transpose(1, 0, 2)
    pieces = lax.all_to_all(pieces, "shard", split_axis=0, concat_axis=0, tiled=True)
    return pieces.reshape(shards * columns, length // shards)


def on_device(
    tokens, teacher, seg_ids, parents, depth, valid, routes, norm1_gain, w_query, w_key, w_value,
    w_out, rel_bias, norm2_gain, router, w_gate, w_up, w_down,
):
    shard_index = lax.axis_index("shard")
    expert_index = lax.axis_index("expert")
    shards = lax.axis_size("shard")
    columns = lax.axis_size("expert")
    experts = columns * w_gate.shape[0]
    token_rows = tokens[0].astype(jnp.float32)
    local_rows, width = token_rows.shape
    length = seg_ids.shape[1]
    bucket_count = rel_bias.shape[0]
    validity = valid[0]
    route_rows = routes[0]

    row_start = shard_index * local_rows
    valid_local = lax.dynamic_slice_in_dim(validity, row_start, local_rows, 0).astype(jnp.float32)
    route_local = lax.dynamic_slice_in_dim(route_rows, row_start, local_rows, 0)

    scale_one = lax.rsqrt(jnp.mean(token_rows * token_rows, axis=1, keepdims=True) + EPSILON)
    base_one = token_rows * scale_one
    normed_one = (base_one * norm1_gain).astype(jnp.bfloat16)
    expert_w = jnp.stack([w_gate[0].T, w_up[0].T, w_down[0]])
    half = expert_w.shape[1] // lax.axis_size("dp")
    expert_w = lax.dynamic_slice_in_dim(expert_w, lax.axis_index("dp") * half, half, 1)
    weights = jnp.concatenate([w_query, w_key, w_value], axis=1)
    info, bias_here = attention_info(validity), rel_bias
    top_count = route_local.shape[1]
    if split_trees():
        quarter, part = width // 4, w_out.shape[0] // 8
        info_row = jnp.pad(info.at[INFO_SIZE - 1].set(jnp.sum(validity)), (0, TILE - INFO_SIZE))
        rows_of = lambda values: values.astype(jnp.float32).reshape(-1, TILE)
        pack = jnp.concatenate([rows_of(info_row), rows_of(rel_bias), rows_of(route_local.T)], axis=0)
        pack = jnp.pad(pack, ((0, -pack.shape[0] % 8), (0, 0)))
        normed_all, weights, out_all, packs = gather_tree(
            normed_one,
            lax.dynamic_slice_in_dim(weights, expert_index * quarter, quarter, 0),
            lax.dynamic_slice_in_dim(
                w_out, (expert_index * 2 + lax.axis_index("dp")) * part, part, 0
            ),
            pack,
        )
        expert_w, packs = lax.optimization_barrier((expert_w, packs))
        tree_rows = packs[:, 0, :INFO_SIZE].astype(jnp.int32)
        z, core, tree, group = my_place()
        info = jnp.where(core == tree, tree_rows[0], tree_rows[1])
        valid_total = jnp.sum(tree_rows[:8, INFO_SIZE - 1]).astype(jnp.float32)
        bias_rows = rel_bias.size // TILE
        bias_here = packs[8, 1 : 1 + bias_rows].reshape(rel_bias.shape)
        route_rows = route_local.size // TILE
        route_layer = packs[0:8:2, 1 + bias_rows : 1 + bias_rows + route_rows]
        route_layer = route_layer.reshape(columns, top_count, local_rows).astype(jnp.int32)
    else:
        normed_all = lax.all_gather(normed_one, "shard", axis=0, tiled=True)
        out_all = lax.all_gather(w_out, "shard", axis=0, tiled=True)
        normed_all, expert_w = lax.optimization_barrier((normed_all, expert_w))
        tree_count = sum_over(jnp.broadcast_to(jnp.sum(validity), (8, 128)), ("dp", "expert"))
        valid_total = tree_count[0, 0].astype(jnp.float32)
        route_layer = layer_small(route_local.T)
    weights_one = weight_hop_one(expert_w)
    query_rows, key_rows, key_t, value_rows, value_t = project(weights, normed_all)

    taken = jnp.any(route_layer == expert_index, axis=1)
    order = jnp.cumsum(taken.reshape(-1).astype(jnp.int32))
    slots = jnp.where(taken, order.reshape(taken.shape) - 1, -1)
    half_blocks = 2 * columns if ring_layer() else columns
    block_rows = columns * local_rows // half_blocks
    slots = slots.reshape(half_blocks, block_rows)
    named = route_layer.transpose(0, 2, 1).reshape(half_blocks, block_rows, top_count)
    scalars = jnp.concatenate(
        [jnp.zeros((1,), jnp.int32), order[block_rows - 1 :: block_rows], expert_index[None].astype(jnp.int32)]
    )

    table = bias_table(bias_here)
    attended_t, log_totals = attention_forward(info, table, query_rows, key_rows, value_t)

    if split_trees():
        attended_here = trade_heads(attended_t)
    else:
        attended_here = heads_to_rows(attended_t, shards)
    update = lax.dot_general(
        attended_here, out_all, (((0,), (0,)), ((), ())), preferred_element_type=jnp.float32
    )
    hidden = token_rows + update

    scale_two = lax.rsqrt(jnp.mean(hidden * hidden, axis=1, keepdims=True) + EPSILON)
    base_two = hidden * scale_two
    normed_two = (base_two * norm2_gain).astype(jnp.bfloat16)

    expert_ids = jnp.arange(experts, dtype=jnp.int32)
    router_pieces = split_float(router)

    def gates_of(rows, named):
        logits = join_float(jnp.dot(rows, router_pieces, preferred_element_type=jnp.float32), experts)
        match = named[:, :, None] == expert_ids[None, None, :]
        chosen = jnp.sum(jnp.where(match, logits[:, None, :], 0.0), axis=2)
        return jax.nn.softmax(chosen, axis=1), match

    gates, route_match = gates_of(normed_two, route_local)
    if split_trees():
        normed_layer, theirs_w, weights_two = meet(normed_two, expert_w, weights_one)
        weights_near = (theirs_w, expert_w, *weights_one, *weights_two)
        far = weight_last_hop(weights_two)
    else:
        normed_layer = [block[None] for block in layer_gather(normed_two)]
        weights_all = (swap(weights_one[0], "dp", 1), weights_one[0])
    expert_scalars = jnp.concatenate(
        [order[-1:], shard_index[None].astype(jnp.int32), weight_shards()]
    )
    router_wide = jnp.pad(router_pieces, ((0, 0), (0, TILE - router_pieces.shape[1])))
    expert_rows, gate_here = compact_rows(scalars, router_wide, slots, named, normed_layer, experts)
    if split_trees():
        produced = expert_forward(expert_scalars, expert_rows, weights_near, 0, 3)
        produced, far = lax.optimization_barrier((produced, far))
        weights_all = weights_near + (far, swap(far, "dp", 1))
        produced = expert_forward(expert_scalars, expert_rows, weights_all, 3, 1, produced)
    else:
        produced = expert_forward(expert_scalars, expert_rows, weights_all, 0, shards)
    shares, produced_layer = expand(scalars, slots, produced, gate_here)
    combined = layer_scatter(shares)

    output_rows = hidden + combined
    factor = length * columns * lax.axis_size("dp") / valid_total
    error = output_rows - teacher[0].astype(jnp.float32)
    error_sum = jnp.sum(valid_local[:, None] * error * error)
    grad_output = valid_local[:, None] * error * factor
    grad_layer = [block[None] for block in layer_gather(grad_output.astype(jnp.bfloat16))]
    grad_rows, gate_grads = compact_grads(scalars, slots, gate_here, produced_layer, grad_layer)
    gate_grads = layer_trade(gate_grads.reshape(columns, local_rows))
    mine_gate, theirs_gate, mine_rest, theirs_rest, rows_grad = expert_backward(
        expert_scalars, expert_rows, grad_rows, weights_all
    )
    theirs_gate = swap(theirs_gate, "dp", 1)
    rows_grad, theirs_gate = lax.optimization_barrier(
        (expand(scalars, slots, rows_grad), theirs_gate)
    )
    rows_grad, gate_part = lax.optimization_barrier((rows_grad, mine_gate + theirs_gate))
    gate_part = lax.psum_scatter(gate_part, "shard", scatter_dimension=0, tiled=False)
    theirs_rest = swap(theirs_rest, "dp", 1)
    expert_back = layer_scatter(rows_grad)

    members = jnp.stack([jnp.asarray(layer_member(number), jnp.int32) for number in range(columns)])
    grad_gates = jnp.sum(
        jnp.where(route_local[:, :, None] == members[None, None, :], gate_grads.T[:, None, :], 0.0), axis=2
    )
    weighted = jnp.sum(gates * grad_gates, axis=1, keepdims=True)
    grad_chosen = gates * (grad_gates - weighted)
    grad_logits = jnp.sum(jnp.where(route_match, grad_chosen[:, :, None], 0.0), axis=1)
    router_grad = join_float(
        lax.dot_general(
            normed_two, split_float(grad_logits), (((0,), (0,)), ((), ())),
            preferred_element_type=jnp.float32,
        ),
        experts,
    )
    grad_normed_two = expert_back
    for number in range(experts):
        grad_normed_two = grad_normed_two + grad_logits[:, number : number + 1] * router[:, number][None]
    grad_base_two = grad_normed_two * norm2_gain
    norm2_grad = jnp.sum(grad_normed_two * base_two, axis=0)
    grad_hidden = grad_output + scale_two * (
        grad_base_two - base_two * jnp.mean(grad_base_two * base_two, axis=1, keepdims=True)
    )
    grad_update = grad_hidden.astype(jnp.bfloat16)
    out_grad = jnp.dot(attended_here, grad_update, preferred_element_type=jnp.float32)
    grad_heads = lax.dot_general(
        grad_update, out_all, (((1,), (1,)), ((), ())), preferred_element_type=jnp.float32
    ).astype(jnp.bfloat16)
    out_grad = out_grad.astype(jnp.bfloat16)
    if split_trees():
        grad_attended, out_grad = trade_back(grad_heads, out_grad)
    else:
        grad_attended = rows_to_heads(grad_heads, shards)
        out_grad = lax.psum_scatter(out_grad, "shard", scatter_dimension=0, tiled=True)
        out_grad = lax.psum(out_grad, ("expert", "dp"))
    out_grad = out_grad.astype(jnp.float32)
    rest_part, grad_attended, gate_part = lax.optimization_barrier(
        (mine_rest + theirs_rest, grad_attended, gate_part)
    )
    rest_part = lax.psum_scatter(rest_part, "shard", scatter_dimension=0, tiled=False)

    grad_queries_t, grad_keys, grad_values, ahead, behind = attention_backward(
        info, table, query_rows, key_rows, key_t, value_rows, grad_attended, attended_t, log_totals
    )
    bias_grad = bias_gradient(ahead, behind, info[OFFSET_AT : OFFSET_AT + CLASSES], bucket_count)
    across = (((0,), (0,)), ((), ()))
    grad_three = jnp.concatenate([grad_queries_t.T, grad_keys, grad_values], axis=1)
    three_wgrad = lax.dot_general(normed_all, grad_three, across, preferred_element_type=jnp.float32)
    norm1_grad = jnp.sum(three_wgrad * weights.astype(jnp.float32), axis=1) / norm1_gain
    grad_normed_all = lax.dot_general(
        grad_three, weights, (((1,), (1,)), ((), ())), preferred_element_type=jnp.float32
    ).astype(jnp.bfloat16)
    three_wgrad = three_wgrad.astype(jnp.bfloat16)

    heads_here = bias_grad.shape[1]
    group = my_place()[3] if split_trees() else shard_index
    bias_all = lax.dynamic_update_slice_in_dim(
        jnp.zeros((bucket_count, heads_here * shards), jnp.float32), bias_grad, group * heads_here, 1
    )
    bias_line = jnp.pad(bias_all.reshape(-1), (0, width - bias_all.size))
    small = jnp.concatenate(
        [router_grad.T, norm2_grad[None], norm1_grad[None], bias_line[None], jnp.full((1, width), error_sum)],
        axis=0,
    )
    if split_trees():
        grad_normed_one, three_wgrad, small = reduce_last(
            grad_normed_all.reshape(shards, local_rows, width), three_wgrad, small
        )
    else:
        grad_normed_one = lax.psum_scatter(grad_normed_all, "shard", scatter_dimension=0, tiled=True)
        three_wgrad = lax.psum(three_wgrad, ("expert", "dp"))
        small = sum_over(small, ("dp", "expert", "shard"))
    three_wgrad = three_wgrad.astype(jnp.float32)
    query_wgrad, key_wgrad, value_wgrad = jnp.split(three_wgrad, 3, axis=1)
    router_grad, norm2_grad, norm1_grad = small[:experts].T, small[experts], small[experts + 1]
    bias_all = small[experts + 2, : bias_all.size].reshape(bias_all.shape)
    bias_grad = lax.dynamic_slice_in_dim(bias_all, shard_index * heads_here, heads_here, 1)
    error_total = small[experts + 3, 0]
    grad_normed_one = grad_normed_one.astype(jnp.float32)
    grad_base_one = grad_normed_one * norm1_gain
    grad_tokens = grad_hidden + scale_one * (
        grad_base_one - base_one * jnp.mean(grad_base_one * base_one, axis=1, keepdims=True)
    )
    loss = error_total / (width * valid_total)

    first_core = lax.axis_index("dp") == 0

    def both_halves(mine):
        other = swap(mine, "dp", 1)
        halves = [jnp.where(first_core, mine, other), jnp.where(first_core, other, mine)]
        return jnp.concatenate(halves, axis=1).astype(jnp.float32)

    gate_grad, rest_grad = both_halves(gate_part)[0].T[None], both_halves(rest_part)
    up_grad, down_grad = rest_grad[0].T[None], rest_grad[1][None]
    return (
        output_rows.astype(jnp.bfloat16)[None],
        loss,
        grad_tokens[None],
        norm1_grad,
        query_wgrad,
        key_wgrad,
        value_wgrad,
        out_grad,
        bias_grad,
        norm2_grad,
        router_grad,
        gate_grad,
        up_grad,
        down_grad,
    )


def solution(mesh):
    in_specs = (
        P(("expert", "dp"), "shard", None),
        P(("expert", "dp"), "shard", None),
        P(("expert", "dp"), None),
        P(("expert", "dp"), None),
        P(("expert", "dp"), None),
        P(("expert", "dp"), None),
        P(("expert", "dp"), None, None),
        P(),
        P(None, "shard"),
        P(None, "shard"),
        P(None, "shard"),
        P("shard", None),
        P(None, "shard"),
        P(),
        P(),
        P("expert", None, "shard"),
        P("expert", None, "shard"),
        P("expert", "shard", None),
    )
    out_specs = (
        P(("expert", "dp"), "shard", None),
        P(),
        P(("expert", "dp"), "shard", None),
        P(),
        P(None, "shard"),
        P(None, "shard"),
        P(None, "shard"),
        P("shard", None),
        P(None, "shard"),
        P(),
        P(),
        P("expert", None, "shard"),
        P("expert", None, "shard"),
        P("expert", "shard", None),
    )
    return jax.shard_map(
        on_device, mesh=mesh, in_specs=in_specs, out_specs=out_specs, check_vma=False
    )
```

```python
import functools
import math

import jax
import jax.numpy as jnp
from jax import lax
from jax.experimental import pallas as pl
from jax.experimental.pallas import tpu as pltpu
from jax.sharding import PartitionSpec as P

TRUNK, SEGMENT, NBRANCH, NLEAF = 1024, 128, 4, 2
TILE = 128
TRUNK_TILES = TRUNK // TILE
HEAD_DIM = 64
MASKED = -1e30
DIAG, SUB, FAR, NONE, BRANCH_NEAR, LEAF_NEAR, LEAF_BRANCH = 0, 1, 2, 3, 4, 6, 14
CLASSES = 18
LIMIT_AT, OFFSET_AT, INFO_SIZE = 0, 32, 64


def head_rows(block, heads):
    lane = lax.broadcasted_iota(jnp.int32, block.shape, 1) // HEAD_DIM
    return jnp.concatenate(
        [jnp.where(lane == h, block, jnp.zeros((), block.dtype)) for h in range(heads)], axis=0
    )


def fill_bias(info, table, bias, heads):
    rows = lax.broadcasted_iota(jnp.int32, (TILE, TILE), 0)
    lanes = lax.broadcasted_iota(jnp.int32, (TILE, TILE), 1)

    def one(number, carry):
        place = jnp.clip(info[OFFSET_AT + number] + lanes - rows, 0, TILE - 1)
        hidden = ((number == DIAG) & (rows > lanes)) | (number == NONE)
        for h in range(heads):
            line = jnp.broadcast_to(table[h : h + 1, :], (TILE, TILE))
            values = jnp.take_along_axis(line, place, axis=1)
            bias[number, :, h * TILE : (h + 1) * TILE] = jnp.where(hidden, MASKED, values)
        return carry

    lax.fori_loop(0, CLASSES, one, 0)


def tile_plan(i, info):
    last = info[LIMIT_AT + 20]
    trunk = i < TRUNK_TILES
    place = jnp.maximum(i - TRUNK_TILES, 0)
    branch = place // (1 + NLEAF)
    leaf = (place % (1 + NLEAF)) > 0
    branch_tile = TRUNK_TILES + branch * (1 + NLEAF)
    near = jnp.where(trunk, i, last)
    near_class = jnp.where(trunk, DIAG, jnp.where(leaf, LEAF_NEAR + branch, BRANCH_NEAR))
    next_class = jnp.where(trunk, SUB, jnp.where(leaf, LEAF_NEAR + NBRANCH + branch, BRANCH_NEAR + 1))
    trunk_steps = TRUNK_TILES // 2
    tail = (
        (jnp.where(leaf, branch_tile, i), jnp.where(leaf, LEAF_BRANCH + branch, DIAG)),
        (i, jnp.where(leaf, DIAG, NONE)),
    )

    def tile_of(step, half):
        kt = step * 2 + half
        in_trunk = trunk | (step < trunk_steps)
        kind = jnp.where(
            kt == near, near_class, jnp.where(kt == near - 1, next_class, jnp.where(kt < near, FAR, NONE))
        )
        return jnp.where(in_trunk, kt, tail[half][0]), jnp.where(in_trunk, kind, tail[half][1])

    return tile_of


def by_steps(i, run):
    for count in range(1, TRUNK_TILES // 2 + 1):

        @pl.when((i < TRUNK_TILES) & (i // 2 == count - 1))
        def _(count=count):
            run(count)

    @pl.when(i >= TRUNK_TILES)
    def _():
        run(TRUNK_TILES // 2 + 1)


def masked_scores(scores, half, tile, kind, info, bias, heads):
    rows = lax.broadcasted_iota(jnp.int32, (TILE, TILE), 0)
    shade = jnp.where(rows < info[LIMIT_AT + tile], 0.0, MASKED)
    shade = jnp.concatenate([shade] * heads, axis=1)
    return scores[half * TILE : (half + 1) * TILE] + bias[kind] + shade


def rows_at(ref, tile):
    return ref[pl.ds(pl.multiple_of(tile * TILE, TILE), TILE), :]


def lanes_at(ref, first, count, tile):
    return ref[first : first + count, pl.ds(pl.multiple_of(tile * TILE, TILE), TILE)]


def forward_kernel(info, table, q, k, v_t, out, log_total, bias, score, total_out, *, heads):
    i = pl.program_id(0)

    @pl.when(i == 0)
    def _():
        fill_bias(info, table, bias, heads)

    tile_of = tile_plan(i, info)
    queries = head_rows(q[...] * jnp.bfloat16(0.125), heads)
    width = heads * TILE

    def first(step, highest):
        (ta, ka), (tb, kb) = tile_of(step, 0), tile_of(step, 1)
        keys = jnp.concatenate([rows_at(k, ta), rows_at(k, tb)], axis=0)
        raw = lax.dot_general(keys, queries, (((1,), (1,)), ((), ())), preferred_element_type=jnp.float32)
        both = jnp.concatenate(
            [masked_scores(raw, 0, ta, ka, info, bias, heads), masked_scores(raw, 1, tb, kb, info, bias, heads)],
            axis=0,
        )
        score[step * 2 * TILE : (step + 1) * 2 * TILE, :] = both
        return jnp.maximum(highest, jnp.max(both.reshape(2 * TILE // 8, 8, width), axis=0))

    pairs = heads // 2

    def run(steps):
        highest = jnp.full((8, width), MASKED, jnp.float32)
        for step in range(steps):
            highest = first(step, highest)
        highest = jnp.max(highest, axis=0, keepdims=True)
        total = jnp.zeros((8, width), jnp.float32)
        for step in range(steps):
            (ta, _), (tb, _) = tile_of(step, 0), tile_of(step, 1)
            part = jnp.exp(score[step * 2 * TILE : (step + 1) * 2 * TILE, :] - highest)
            low = part.astype(jnp.bfloat16)
            for p in range(pairs):
                values = jnp.concatenate(
                    [lanes_at(v_t, p * TILE, TILE, ta), lanes_at(v_t, p * TILE, TILE, tb)], axis=1
                )
                product = jnp.dot(
                    values, low[:, p * 2 * TILE : (p + 1) * 2 * TILE], preferred_element_type=jnp.float32
                )
                if step == 0:
                    total_out[p] = product
                else:
                    total_out[p] += product
            total = total + jnp.sum(part.reshape(2 * TILE // 8, 8, width), axis=0)
        total = jnp.sum(total, axis=0, keepdims=True)
        inverse = 1.0 / total
        for h in range(heads):
            p, odd = h // 2, h % 2
            block = total_out[p, odd * HEAD_DIM : (odd + 1) * HEAD_DIM, odd * TILE : (odd + 1) * TILE]
            out[h * HEAD_DIM : (h + 1) * HEAD_DIM, :] = (
                block * inverse[:, h * TILE : (h + 1) * TILE]
            ).astype(jnp.bfloat16)
        log_total[0] = highest + jnp.log(total)

    by_steps(i, run)


def attention_forward(info, table, q, k, v_t):
    length, columns = q.shape
    heads = columns // HEAD_DIM
    tiles = length // TILE
    width = heads * TILE
    whole = lambda shape: pl.BlockSpec(shape, lambda i, info: (0,) * len(shape))
    return pl.pallas_call(
        functools.partial(forward_kernel, heads=heads),
        grid_spec=pltpu.PrefetchScalarGridSpec(
            num_scalar_prefetch=1,
            grid=(tiles,),
            in_specs=[
                whole(table.shape),
                pl.BlockSpec((TILE, columns), lambda i, info: (i, 0)),
                whole(k.shape),
                whole(v_t.shape),
            ],
            out_specs=[
                pl.BlockSpec((columns, TILE), lambda i, info: (0, i)),
                pl.BlockSpec((1, 1, width), lambda i, info: (i, 0, 0)),
            ],
            scratch_shapes=[
                pltpu.VMEM((CLASSES, TILE, width), jnp.float32),
                pltpu.VMEM((10 * TILE, width), jnp.float32),
                pltpu.VMEM((heads // 2, TILE, 2 * TILE), jnp.float32),
            ],
        ),
        out_shape=[
            jax.ShapeDtypeStruct((columns, length), jnp.bfloat16),
            jax.ShapeDtypeStruct((tiles, 1, width), jnp.float32),
        ],
        compiler_params=pltpu.CompilerParams(
            dimension_semantics=("arbitrary",), vmem_limit_bytes=50 << 20
        ),
        cost_estimate=pl.CostEstimate(flops=4 * 10**10, bytes_accessed=10**7, transcendentals=0),
        name="attention_forward",
    )(info, table, q, k, v_t)


def backward_kernel(
    info, table, q, k, k_t, v, grad, attended_t, log_total,
    grad_q, grad_k, grad_v, ahead, behind,
    bias, by_class, total_q, total_k, total_v, *, heads, tiles,
):
    i = pl.program_id(0)
    width = heads * TILE

    @pl.when(i == 0)
    def _():
        fill_bias(info, table, bias, heads)
        by_class[...] = jnp.zeros_like(by_class)
        total_k[...] = jnp.zeros_like(total_k)
        total_v[...] = jnp.zeros_like(total_v)

    tile_of = tile_plan(i, info)
    queries = head_rows(q[...] * jnp.bfloat16(0.125), heads)
    grads = head_rows(grad[...], heads)
    product = jnp.transpose(grad[...].astype(jnp.float32)) * attended_t[...].astype(jnp.float32)
    centre = jnp.concatenate(
        [
            jnp.sum(product[h * HEAD_DIM : (h + 1) * HEAD_DIM], axis=0, keepdims=True)
            for h in range(heads)
        ],
        axis=1,
    )
    logs = log_total[0]
    total_q[...] = jnp.zeros_like(total_q)
    pairs = heads // 2

    def one(step):
        (ta, ka), (tb, kb) = tile_of(step, 0), tile_of(step, 1)
        keys = jnp.concatenate([rows_at(k, ta), rows_at(k, tb)], axis=0)
        values = jnp.concatenate([rows_at(v, ta), rows_at(v, tb)], axis=0)
        raw = lax.dot_general(keys, queries, (((1,), (1,)), ((), ())), preferred_element_type=jnp.float32)
        both = jnp.concatenate(
            [masked_scores(raw, 0, ta, ka, info, bias, heads), masked_scores(raw, 1, tb, kb, info, bias, heads)],
            axis=0,
        )
        probs = jnp.exp(both - logs)
        grad_probs = lax.dot_general(
            values, grads, (((1,), (1,)), ((), ())), preferred_element_type=jnp.float32
        )
        grad_scores = probs * (grad_probs - centre)
        by_class[ka] += grad_scores[:TILE]
        by_class[kb] += grad_scores[TILE:]
        low = grad_scores.astype(jnp.bfloat16)
        value_part = jnp.dot(probs.astype(jnp.bfloat16), grads, preferred_element_type=jnp.float32)
        key_part = jnp.dot(low, queries, preferred_element_type=jnp.float32)
        for half, tile in ((0, ta), (1, tb)):
            at = pl.ds(pl.multiple_of(tile * TILE, TILE), TILE)
            total_v[at, :] += value_part[half * TILE : (half + 1) * TILE]
            total_k[at, :] += key_part[half * TILE : (half + 1) * TILE]
        for p in range(pairs):
            keys_t = jnp.concatenate(
                [lanes_at(k_t, p * TILE, TILE, ta), lanes_at(k_t, p * TILE, TILE, tb)], axis=1
            )
            total_q[p] += jnp.dot(
                keys_t, low[:, p * 2 * TILE : (p + 1) * 2 * TILE], preferred_element_type=jnp.float32
            )

    def run(steps):
        for step in range(steps):
            one(step)

    by_steps(i, run)
    for h in range(heads):
        p, odd = h // 2, h % 2
        block = total_q[p, odd * HEAD_DIM : (odd + 1) * HEAD_DIM, odd * TILE : (odd + 1) * TILE]
        grad_q[h * HEAD_DIM : (h + 1) * HEAD_DIM, :] = (block * 0.125).astype(jnp.bfloat16)

    @pl.when(i == tiles - 1)
    def _():
        grad_k[...] = total_k[...].astype(jnp.bfloat16)
        grad_v[...] = total_v[...].astype(jnp.bfloat16)
        rows = lax.broadcasted_iota(jnp.int32, (TILE, TILE), 0)
        lanes = lax.broadcasted_iota(jnp.int32, (TILE, TILE), 1)

        def reduce(number, carry):
            for h in range(heads):
                block = by_class[number, :, h * TILE : (h + 1) * TILE]
                turned = jnp.take_along_axis(block, (rows + lanes) % TILE, axis=1)
                forward = jnp.sum(jnp.where(rows + lanes < TILE, turned, 0.0), axis=0, keepdims=True)
                wrapped = jnp.sum(jnp.where(rows + lanes < TILE, 0.0, turned), axis=0, keepdims=True)
                ahead[number, :, h * TILE : (h + 1) * TILE] = forward
                behind[number, :, h * TILE : (h + 1) * TILE] = wrapped
            return carry

        lax.fori_loop(0, CLASSES, reduce, 0)


def attention_backward(info, table, q, k, k_t, v, grad, attended_t, log_total):
    length, columns = q.shape
    heads = columns // HEAD_DIM
    tiles = length // TILE
    width = heads * TILE
    whole = lambda shape: pl.BlockSpec(shape, lambda i, info: (0,) * len(shape))
    rows = pl.BlockSpec((TILE, columns), lambda i, info: (i, 0))
    lanes = pl.BlockSpec((columns, TILE), lambda i, info: (0, i))
    return pl.pallas_call(
        functools.partial(backward_kernel, heads=heads, tiles=tiles),
        grid_spec=pltpu.PrefetchScalarGridSpec(
            num_scalar_prefetch=1,
            grid=(tiles,),
            in_specs=[
                whole(table.shape), rows, whole(k.shape), whole(k_t.shape), whole(v.shape), rows, lanes,
                pl.BlockSpec((1, 1, width), lambda i, info: (i, 0, 0)),
            ],
            out_specs=[
                lanes, whole(k.shape), whole(v.shape),
                whole((CLASSES, 1, width)), whole((CLASSES, 1, width)),
            ],
            scratch_shapes=[
                pltpu.VMEM((CLASSES, TILE, width), jnp.float32),
                pltpu.VMEM((CLASSES, TILE, width), jnp.float32),
                pltpu.VMEM((heads // 2, TILE, 2 * TILE), jnp.float32),
                pltpu.VMEM((length, columns), jnp.float32),
                pltpu.VMEM((length, columns), jnp.float32),
            ],
        ),
        out_shape=[
            jax.ShapeDtypeStruct((columns, length), jnp.bfloat16),
            jax.ShapeDtypeStruct((length, columns), jnp.bfloat16),
            jax.ShapeDtypeStruct((length, columns), jnp.bfloat16),
            jax.ShapeDtypeStruct((CLASSES, 1, width), jnp.float32),
            jax.ShapeDtypeStruct((CLASSES, 1, width), jnp.float32),
        ],
        compiler_params=pltpu.CompilerParams(
            dimension_semantics=("arbitrary",), vmem_limit_bytes=56 << 20
        ),
        cost_estimate=pl.CostEstimate(flops=6 * 10**10, bytes_accessed=10**7, transcendentals=0),
        name="attention_backward",
    )(info, table, q, k, k_t, v, grad, attended_t, log_total)


def bucket_index(distance, bucket_count, max_dist=128):
    half_count = bucket_count // 2
    counted = jnp.zeros_like(distance)
    for number in range(1, bucket_count - half_count):
        border = math.ceil(half_count * (max_dist / half_count) ** (number / (bucket_count - half_count)))
        counted = counted + (distance >= border).astype(jnp.int32)
    return jnp.where(distance < half_count, distance, half_count + counted)


def attention_info(validity):
    trunk = jnp.sum(validity[:TRUNK])
    lengths = jnp.sum(validity[TRUNK:].reshape(NBRANCH, 1 + NLEAF, SEGMENT), axis=2)
    last = (trunk - 1) // TILE
    limits = jnp.concatenate([trunk - TILE * jnp.arange(TRUNK_TILES), lengths.reshape(-1)])
    left = trunk - last * TILE
    branch = lengths[:, 0]
    offsets = jnp.concatenate(
        [
            jnp.array([0, TILE, 4096, 0]),
            jnp.stack([left, left + TILE]),
            left + branch,
            left + branch + TILE,
            branch,
        ]
    )
    gap = lambda count: jnp.zeros((count,), jnp.int32)
    info = jnp.concatenate(
        [
            limits, last[None], gap(OFFSET_AT - 21), offsets,
            gap(INFO_SIZE - 1 - OFFSET_AT - CLASSES), (trunk + jnp.sum(lengths))[None],
        ]
    )
    return info


def bias_table(rel_bias):
    places = bucket_index(jnp.arange(TILE, dtype=jnp.int32), rel_bias.shape[0])
    pick = (places[:, None] == jnp.arange(rel_bias.shape[0])[None, :]).astype(jnp.float32)
    shifted = rel_bias - rel_bias[-1:]
    return jnp.einsum("db,bh->hd", pick, shifted, precision=lax.Precision.HIGHEST)


def bias_gradient(ahead, behind, offsets, bucket_count):
    heads = ahead.shape[2] // TILE
    lane = jnp.arange(TILE, dtype=jnp.int32)[None, :]
    distance = jnp.stack([offsets[:, None] + lane, offsets[:, None] + lane - TILE], axis=0)
    bucket = bucket_index(jnp.maximum(distance, 0), bucket_count)
    pick = (bucket[..., None] == jnp.arange(bucket_count)).astype(jnp.float32)
    sums = jnp.stack([ahead, behind], axis=0).reshape(2, CLASSES, heads, TILE)
    return jnp.einsum("sclb,schl->bh", pick, sums, precision=lax.Precision.HIGHEST)


EPSILON = 1e-06
SLOT_TILE = 256


def slot_pick(slots, tile, count, axis):
    shape = (SLOT_TILE, count) if axis == 0 else (count, SLOT_TILE)
    places = lax.broadcasted_iota(jnp.int32, shape, axis)
    return (slots - tile * SLOT_TILE == places).astype(jnp.float32).astype(jnp.bfloat16)


def fill_slots(scalars, block, slots, values, out):
    def one(tile, carry):
        at = pl.ds(pl.multiple_of(tile * SLOT_TILE, SLOT_TILE), SLOT_TILE)
        pick = slot_pick(slots, tile, values.shape[0], 0)
        out[at, :] += jnp.dot(pick, values, preferred_element_type=jnp.float32).astype(jnp.bfloat16)
        return carry

    lax.fori_loop(scalars[block] // SLOT_TILE, pl.cdiv(scalars[block + 1], SLOT_TILE), one, 0)


def compact_rows_kernel(scalars, router, slots, named, *refs, blocks, experts):
    stacks, (out, gate) = refs[:-2], refs[-2:]
    rows = [(stack, number) for stack in stacks for number in range(stack.shape[0])]
    out[...] = jnp.zeros_like(out)
    me = scalars[blocks + 1]
    for b, (stack, number) in enumerate(rows):
        values = stack[number]
        fill_slots(scalars, b, slots[b], values, out)
        products = jnp.dot(values, router[...], preferred_element_type=jnp.float32)
        lane = lax.broadcasted_iota(jnp.int32, products.shape, 1)
        lane = jnp.where(lane < 3 * experts, lane % experts, -1)
        choices = [named[b, :, k : k + 1] for k in range(named.shape[2])]
        logits = [
            jnp.sum(jnp.where(lane == choice, products, 0.0), axis=1, keepdims=True) for choice in choices
        ]
        highest = functools.reduce(jnp.maximum, logits)
        powers = [jnp.exp(logit - highest) for logit in logits]
        mine = sum(jnp.where(choice == me, power, 0.0) for choice, power in zip(choices, powers))
        gate[b] = mine / sum(powers)


def whole_calls(kernel, operands, out_shape, name, limit):
    specs = [pl.BlockSpec(memory_space=pltpu.SMEM)]
    specs += [pl.BlockSpec(memory_space=pltpu.VMEM) for _ in operands[1:]]
    return pl.pallas_call(
        kernel,
        in_specs=specs,
        out_specs=jax.tree.map(lambda _: pl.BlockSpec(memory_space=pltpu.VMEM), out_shape),
        out_shape=out_shape,
        compiler_params=pltpu.CompilerParams(vmem_limit_bytes=limit << 20),
        cost_estimate=pl.CostEstimate(flops=10**10, bytes_accessed=3 * 10**7, transcendentals=0),
        name=name,
    )(*operands)


def slot_room(rows):
    return pl.cdiv(rows, SLOT_TILE) * SLOT_TILE


def compact_rows(scalars, router, slots, named, rows, experts):
    (blocks, count), width = slots.shape, rows[0].shape[2]
    return whole_calls(
        functools.partial(compact_rows_kernel, blocks=blocks, experts=experts),
        (scalars, router, slots.reshape(blocks, 1, count), named, *rows),
        [
            jax.ShapeDtypeStruct((slot_room(blocks * count), width), jnp.bfloat16),
            jax.ShapeDtypeStruct((blocks, count, 1), jnp.float32),
        ],
        "compact_rows",
        48,
    )


def compact_grads_kernel(scalars, slots, gate, produced, *refs, blocks):
    stacks, (out, gate_grad) = refs[:-2], refs[-2:]
    rows = [(stack, number) for stack in stacks for number in range(stack.shape[0])]
    out[...] = jnp.zeros_like(out)
    for b, (stack, number) in enumerate(rows):
        wide = stack[number].astype(jnp.float32)
        gate_grad[b] = jnp.sum(wide * produced[b].astype(jnp.float32), axis=1, keepdims=True)
        fill_slots(scalars, b, slots[b], (gate[b] * wide).astype(jnp.bfloat16), out)


def compact_grads(scalars, slots, gate, produced, rows):
    (blocks, count), width = slots.shape, rows[0].shape[2]
    return whole_calls(
        functools.partial(compact_grads_kernel, blocks=blocks),
        (scalars, slots.reshape(blocks, 1, count), gate, produced, *rows),
        [
            jax.ShapeDtypeStruct((slot_room(blocks * count), width), jnp.bfloat16),
            jax.ShapeDtypeStruct((blocks, count, 1), jnp.float32),
        ],
        "compact_grads",
        56,
    )


def expand_kernel(scalars, slots, *refs, gated):
    gate, (rows, *outs) = (refs[0], refs[1:]) if gated else (None, refs)
    expand_blocks(scalars, 0, slots, rows, outs, gate)


def expand_blocks(scalars, first, slots, rows, outs, gate=None):
    out = outs[0]
    blocks, count = out.shape[:2]
    for b in range(blocks):
        out[b] = jnp.zeros(out.shape[1:], out.dtype)

        def one(tile, carry):
            at = pl.ds(pl.multiple_of(tile * SLOT_TILE, SLOT_TILE), SLOT_TILE)
            pick = slot_pick(slots[b], tile, count, 1)
            part = jnp.dot(pick, rows[at, :].astype(jnp.bfloat16), preferred_element_type=jnp.float32)
            out[b] += part.astype(jnp.bfloat16)
            return carry

        start, stop = scalars[first + b], scalars[first + b + 1]
        lax.fori_loop(start // SLOT_TILE, pl.cdiv(stop, SLOT_TILE), one, 0)
        if gate is not None:
            outs[1][b] = out[b]
            out[b] = (gate[b] * out[b].astype(jnp.float32)).astype(jnp.bfloat16)


def expand(scalars, slots, rows, gate=None):
    blocks, count = slots.shape
    shape = jax.ShapeDtypeStruct((blocks, count, rows.shape[1]), jnp.bfloat16)
    operands = (scalars, slots.reshape(blocks, count, 1)) + (() if gate is None else (gate,)) + (rows,)
    outs = whole_calls(
        functools.partial(expand_kernel, gated=gate is not None),
        operands, [shape] * (1 if gate is None else 2), "expand", 56,
    )
    return outs[0] if gate is None else outs


GELU_IN = math.sqrt(2.0 / math.pi)
GELU_CUBE = 0.044715


def gelu_parts(pre):
    square = pre * pre
    bent = jnp.tanh(GELU_IN * pre * (1.0 + GELU_CUBE * square))
    half = 0.5 * (1.0 + bent)
    return pre * half, half, bent, square


LAST = (((1,), (1,)), ((), ()))
FIRST = (((0,), (0,)), ((), ()))


def weight_sources(sources, z):
    theirs, sources = sources[0], sources[1:]
    if len(sources) == 1:
        mine = [[(None, sources[0].at[number])] for number in range(sources[0].shape[0])]
        return mine, [[(None, theirs.at[number])] for number in range(theirs.shape[0])]
    own, up_one, down_one, up_two, down_two = sources[:5]
    low, high = z == 0, z == 3
    mine = [
        [(None, own)],
        [(z < 3, down_one), (high, up_one)],
        [(low, down_two), ((z == 1) | (z == 2), up_one), (high, up_two)],
        [(z == 1, down_two), (z == 2, up_two)],
    ]
    others = [[(None, theirs.at[number])] for number in range(3)]
    others.append([((z == 1) | (z == 2), theirs.at[3])])
    if len(sources) == 7:
        mine[3].append((low | high, sources[5]))
        others[3].append((low | high, sources[6]))
    return mine, others


def weight_copies(step, sources, room, sem, act):
    def copy(slot, half, view):
        rows = view.shape[1]
        for matrix in range(3):
            act(
                pltpu.make_async_copy(
                    view.at[matrix],
                    room.at[slot, matrix, pl.ds(half * rows, rows)],
                    sem.at[slot, half * 3 + matrix],
                )
            )

    for half, places in enumerate(sources):
        for number, choices in enumerate(places):
            for condition, view in choices:
                here = step == number if condition is None else (step == number) & condition
                pl.when(here)(functools.partial(copy, number % 2, half, view))


def next_weights(first, sources, room, sem):
    number, steps = pl.program_id(0), pl.num_programs(0)
    step = first + number

    @pl.when(number == 0)
    def _():
        weight_copies(step, sources, room, sem, lambda copy: copy.start())

    @pl.when(number + 1 < steps)
    def _():
        weight_copies(step + 1, sources, room, sem, lambda copy: copy.start())

    weight_copies(step, sources, room, sem, lambda copy: copy.wait())
    return step % 2


def over_tiles(count, room, body):
    large = 2 * SLOT_TILE if room <= 10 * SLOT_TILE else SLOT_TILE
    rest = count % large
    tiles = count // large + jnp.where(rest > SLOT_TILE if large > SLOT_TILE else rest > 0, 1, 0)

    def one(tile, carry):
        body(pl.multiple_of(tile * large, large), large)
        return carry

    lax.fori_loop(0, tiles, one, 0)
    if large > SLOT_TILE:

        @pl.when((rest > 0) & (rest <= SLOT_TILE))
        def _():
            body(pl.multiple_of(tiles * large, large), SLOT_TILE)


def expert_forward_kernel(scalars, rows, *refs, first, sources, aliased, blocks):
    weights, refs = refs[:sources], refs[sources:]
    before, refs = (refs[0], refs[1:]) if aliased else (None, refs)
    if blocks:
        slots, gate, out, plain, total, room, sem = refs
    else:
        total, room, sem = refs
    step = pl.program_id(0)
    slot = next_weights(first, weight_sources(weights, scalars[1]), room, sem)

    def body(start, size):
        at = pl.ds(start, size)
        values = rows[at, :]
        gate_pre = lax.dot_general(values, room[slot, 0], LAST, preferred_element_type=jnp.float32)
        up_pre = lax.dot_general(values, room[slot, 1], LAST, preferred_element_type=jnp.float32)
        inner = (gelu_parts(gate_pre)[0] * up_pre).astype(jnp.bfloat16)
        part = jnp.dot(inner, room[slot, 2], preferred_element_type=jnp.float32)

        @pl.when(step == 0)
        def _():
            total[at, :] = part if before is None else part + before[at, :]

        @pl.when(step > 0)
        def _():
            total[at, :] += part

    over_tiles(scalars[0], rows.shape[0], body)
    if blocks:
        expand_blocks(scalars, scalars.shape[0] - blocks - 1, slots, total, (out, plain), gate)


def expert_cost(rows, weights, shards, units):
    return pl.CostEstimate(
        flops=2 * units * rows * shards * weights.shape[-2] * 2 * weights.shape[-1],
        bytes_accessed=4 * weights.size,
        transcendentals=0,
    )


def expert_scratch(weights):
    half, width = weights.shape[-2:]
    return [pltpu.VMEM((2, 3, 2 * half, width), jnp.bfloat16), pltpu.SemaphoreType.DMA((2, 6))]


def expert_forward(scalars, rows, weights, first, steps, before=None, bounds=None, slots=None, gate=None):
    padded, width = rows.shape
    theirs = weights[0]
    whole = pl.BlockSpec((padded, width), lambda s, scalars: (0, 0), pipeline_mode=pl.Buffered(1))
    extra = () if before is None else (before,)
    extra_specs = [whole] * len(extra)
    blocks = 0
    out_specs, scratch = whole, []
    out_shape = jax.ShapeDtypeStruct((padded, width), jnp.float32)
    if slots is not None:
        blocks, count = slots.shape
        scalars = jnp.concatenate([scalars, bounds[: blocks + 1]])
        extra += (slots.reshape(blocks, count, 1), gate)
        extra_specs += [block_spec((blocks, count, 1))] * 2
        out_specs = [block_spec((blocks, count, width))] * 2
        out_shape = [jax.ShapeDtypeStruct((blocks, count, width), jnp.bfloat16)] * 2
        scratch = [pltpu.VMEM((padded, width), jnp.float32)]
    return pl.pallas_call(
        functools.partial(
            expert_forward_kernel,
            first=first, sources=len(weights), aliased=before is not None, blocks=blocks,
        ),
        grid_spec=pltpu.PrefetchScalarGridSpec(
            num_scalar_prefetch=1,
            grid=(steps,),
            in_specs=[whole] + [pl.BlockSpec(memory_space=pl.ANY)] * len(weights) + extra_specs,
            out_specs=out_specs,
            scratch_shapes=scratch + expert_scratch(theirs),
        ),
        out_shape=out_shape,
        compiler_params=pltpu.CompilerParams(vmem_limit_bytes=60 << 20),
        cost_estimate=expert_cost(padded, theirs, steps, 3),
        name="expert_forward",
    )(scalars, rows, *weights, *extra)


def block_spec(shape):
    return pl.BlockSpec(shape, lambda s, scalars: (0,) * len(shape), pipeline_mode=pl.Buffered(1))


def expert_backward_kernel(scalars, rows, grads, *refs, sources):
    weights, rest = refs[:sources], refs[sources:]
    mine_gate, theirs_gate, mine_rest, theirs_rest, total = rest[:5]
    gate_total, up_total, down_total, room, sem = rest[-5:]
    step = pl.program_id(0)
    slot = next_weights(0, weight_sources(weights, scalars[1]), room, sem)
    gate_total[...] = jnp.zeros_like(gate_total)
    up_total[...] = jnp.zeros_like(up_total)
    down_total[...] = jnp.zeros_like(down_total)

    def body(start, size):
        at = pl.ds(start, size)
        values, upstream = rows[at, :], grads[at, :]
        gate_pre = lax.dot_general(room[slot, 0], values, LAST, preferred_element_type=jnp.float32)
        up_pre = lax.dot_general(room[slot, 1], values, LAST, preferred_element_type=jnp.float32)
        grad_inner = lax.dot_general(room[slot, 2], upstream, LAST, preferred_element_type=jnp.float32)
        active, half, bent, square = gelu_parts(gate_pre)
        slope = half + (0.5 * GELU_IN) * gate_pre * (1.0 - bent * bent) * (1.0 + 3.0 * GELU_CUBE * square)
        inner = (active * up_pre).astype(jnp.bfloat16)
        grad_gate = (grad_inner * up_pre * slope).astype(jnp.bfloat16)
        grad_up = (grad_inner * active).astype(jnp.bfloat16)
        down_total[...] += jnp.dot(inner, upstream, preferred_element_type=jnp.float32)
        gate_total[...] += jnp.dot(grad_gate, values, preferred_element_type=jnp.float32)
        up_total[...] += jnp.dot(grad_up, values, preferred_element_type=jnp.float32)
        part = lax.dot_general(grad_gate, room[slot, 0], FIRST, preferred_element_type=jnp.float32)
        part = part + lax.dot_general(grad_up, room[slot, 1], FIRST, preferred_element_type=jnp.float32)

        @pl.when(step == 0)
        def _():
            total[at, :] = part

        @pl.when(step > 0)
        def _():
            total[at, :] += part

    over_tiles(scalars[0], rows.shape[0], body)
    half = mine_gate.shape[2]
    for sums, mine, theirs, number in (
        (gate_total, mine_gate, theirs_gate, 0),
        (up_total, mine_rest, theirs_rest, 0),
        (down_total, mine_rest, theirs_rest, 1),
    ):
        mine[0, number] = sums[:half].astype(jnp.bfloat16)
        theirs[0, number] = sums[half:].astype(jnp.bfloat16)


def expert_backward(scalars, rows, grads, weights):
    padded, width = rows.shape
    theirs = weights[0]
    shards, _, half, _ = theirs.shape
    whole = pl.BlockSpec((padded, width), lambda s, scalars: (0, 0), pipeline_mode=pl.Buffered(1))
    out = lambda count: pl.BlockSpec(
        (1, count, half, width), lambda s, scalars: (scalars[2 + s], 0, 0, 0)
    )
    shape = lambda count: jax.ShapeDtypeStruct((shards, count, half, width), jnp.bfloat16)
    return pl.pallas_call(
        functools.partial(expert_backward_kernel, sources=len(weights)),
        grid_spec=pltpu.PrefetchScalarGridSpec(
            num_scalar_prefetch=1,
            grid=(shards,),
            in_specs=[whole, whole] + [pl.BlockSpec(memory_space=pl.ANY)] * len(weights),
            out_specs=[out(1), out(1), out(2), out(2), whole],
            scratch_shapes=[pltpu.VMEM((2 * half, width), jnp.float32)] * 3 + expert_scratch(theirs),
        ),
        out_shape=[shape(1), shape(1), shape(2), shape(2), jax.ShapeDtypeStruct((padded, width), jnp.float32)],
        compiler_params=pltpu.CompilerParams(vmem_limit_bytes=63 << 20),
        cost_estimate=expert_cost(padded, theirs, shards, 8),
        name="expert_backward",
    )(scalars, rows, grads, *weights)


def project_kernel(weights, rows, q, k, k_t, v, v_t):
    columns = q.shape[1]
    low = jnp.dot(rows[...], weights[...], preferred_element_type=jnp.float32).astype(jnp.bfloat16)
    q[...] = low[:, :columns]
    k[...] = low[:, columns : 2 * columns]
    v[...] = low[:, 2 * columns :]
    k_t[...] = jnp.transpose(low[:, columns : 2 * columns])
    v_t[...] = jnp.transpose(low[:, 2 * columns :])


def project(weights, rows):
    length, width = rows.shape
    columns = weights.shape[1] // 3
    count = 2 * TILE
    tall = pl.BlockSpec((count, columns), lambda i: (i, 0))
    wide = pl.BlockSpec((columns, count), lambda i: (0, i))
    tall_shape = jax.ShapeDtypeStruct((length, columns), jnp.bfloat16)
    wide_shape = jax.ShapeDtypeStruct((columns, length), jnp.bfloat16)
    return pl.pallas_call(
        project_kernel,
        grid=(length // count,),
        in_specs=[
            pl.BlockSpec(weights.shape, lambda i: (0, 0)),
            pl.BlockSpec((count, width), lambda i: (i, 0)),
        ],
        out_specs=[tall, tall, wide, tall, wide],
        out_shape=[tall_shape, tall_shape, wide_shape, tall_shape, wide_shape],
        compiler_params=pltpu.CompilerParams(vmem_limit_bytes=40 << 20),
        cost_estimate=pl.CostEstimate(flops=10**10, bytes_accessed=2 * 10**7, transcendentals=0),
        name="project",
    )(weights, rows)


def products_kernel(rows, weights, q_t, k, v, parts, three, norm, total):
    step = pl.program_id(0)
    grads = jnp.concatenate([jnp.transpose(q_t[...]), k[...], v[...]], axis=1)
    values = rows[...]
    part = lax.dot_general(grads, weights[...], LAST, preferred_element_type=jnp.float32)
    parts[...] = part.astype(jnp.bfloat16)
    product = lax.dot_general(values, grads, FIRST, preferred_element_type=jnp.float32)
    column = jnp.sum(part * values.astype(jnp.float32), axis=0, keepdims=True)

    @pl.when(step == 0)
    def _():
        total[...] = product
        norm[...] = column

    @pl.when(step > 0)
    def _():
        total[...] += product
        norm[...] += column

    @pl.when(step == pl.num_programs(0) - 1)
    def _():
        three[...] = total[...].astype(jnp.bfloat16)


def last_products(rows, weights, q_t, k, v):
    length, width = rows.shape
    columns = k.shape[1]
    count = 4 * TILE
    whole = lambda shape: pl.BlockSpec(shape, lambda i: (0, 0))
    tall = pl.BlockSpec((count, columns), lambda i: (i, 0))
    wide = pl.BlockSpec((count, width), lambda i: (i, 0))
    return pl.pallas_call(
        products_kernel,
        grid=(length // count,),
        in_specs=[wide, whole(weights.shape), pl.BlockSpec((columns, count), lambda i: (0, i)), tall, tall],
        out_specs=[wide, whole(weights.shape), whole((1, width))],
        out_shape=[
            jax.ShapeDtypeStruct((length, width), jnp.bfloat16),
            jax.ShapeDtypeStruct(weights.shape, jnp.bfloat16),
            jax.ShapeDtypeStruct((1, width), jnp.float32),
        ],
        scratch_shapes=[pltpu.VMEM(weights.shape, jnp.float32)],
        compiler_params=pltpu.CompilerParams(vmem_limit_bytes=48 << 20),
        cost_estimate=pl.CostEstimate(flops=10**10, bytes_accessed=2 * 10**7, transcendentals=0),
        name="last_products",
    )(rows, weights, q_t, k, v)


def split_float(values):
    high = values.astype(jnp.bfloat16)
    rest = values - high.astype(jnp.float32)
    middle = rest.astype(jnp.bfloat16)
    low = (rest - middle.astype(jnp.float32)).astype(jnp.bfloat16)
    return jnp.concatenate([high, middle, low], axis=1)


def join_float(products, count):
    return products[:, 2 * count :] + products[:, count : 2 * count] + products[:, :count]


def swap(array, axis, bit):
    size = lax.axis_size(axis)
    return lax.ppermute(array, axis, [(i, i ^ bit) for i in range(size)])


def sum_over(array, axes):
    for axis in axes:
        bit = 1
        while bit < lax.axis_size(axis):
            array = array + swap(array, axis, bit)
            bit *= 2
    return array


def ring_layer():
    return lax.axis_size("expert") == 4


def layer_member(number):
    return lax.axis_index("expert") ^ number if ring_layer() else number


def layer_gather(rows):
    columns = lax.axis_size("expert")
    if not ring_layer():
        stacked = lax.all_gather(rows, "expert", axis=0)
        return [stacked[number] for number in range(columns)]
    half = rows.shape[0] // 2
    top, bottom = rows[:half], rows[half:]
    x_top, y_bottom = swap(top, "expert", 1), swap(bottom, "expert", 2)
    x_bottom, y_top = swap(bottom, "expert", 1), swap(top, "expert", 2)
    far_top, far_bottom = swap(x_top, "expert", 2), swap(y_bottom, "expert", 1)
    return [top, bottom, x_top, x_bottom, y_top, y_bottom, far_top, far_bottom]


def layer_scatter(parts):
    if not ring_layer():
        return lax.psum_scatter(parts, "expert", scatter_dimension=0, tiled=False).astype(jnp.float32)
    _, half, width = parts.shape
    block = jax.ShapeDtypeStruct((half, width), jnp.float32)
    low, high = pl.pallas_call(
        scatter_kernel,
        in_specs=[pl.BlockSpec(memory_space=pltpu.VMEM)],
        out_specs=[pl.BlockSpec(memory_space=pltpu.VMEM)] * 2,
        out_shape=[block, block],
        scratch_shapes=[pltpu.VMEM((6, half, width), jnp.bfloat16), pltpu.SemaphoreType.DMA((2, 6))],
        compiler_params=pltpu.CompilerParams(
            collective_id=6, has_side_effects=True, vmem_limit_bytes=40 << 20
        ),
        cost_estimate=pl.CostEstimate(flops=5 * 10**10, bytes_accessed=10**7, transcendentals=0),
        name="layer_scatter",
    )(parts)
    return jnp.concatenate([low, high], axis=0)


def scatter_kernel(parts, low_out, high_out, room, sems):
    column = lax.axis_index("expert")
    greet([{"expert": column ^ 1}, {"expert": column ^ 2}])
    halves = lambda ref, owner, side: ref.at[2 * (owner ^ column) + side]
    onward, terms, finish = ring_scatter(parts, halves, room, sems, 0)
    onward()
    low, high = terms()
    low_out[...] = sum(block[...].astype(jnp.float32) for block in low)
    high_out[...] = sum(block[...].astype(jnp.float32) for block in high)
    finish()


def layer_small(array):
    columns = lax.axis_size("expert")
    if not ring_layer():
        return lax.all_gather(array, "expert", axis=0)
    return jnp.stack([array] + [swap(array, "expert", number) for number in range(1, columns)])


def layer_trade(array):
    if not ring_layer():
        return lax.all_to_all(array, "expert", split_axis=0, concat_axis=0, tiled=True)
    return jnp.stack([array[0]] + [swap(array[n], "expert", n) for n in range(1, array.shape[0])])


def split_trees():
    return lax.axis_size("shard") == 4 and lax.axis_size("dp") == 2 and ring_layer()


def my_place():
    z, core = lax.axis_index("shard"), lax.axis_index("dp")
    return z, core, z // 2, 2 * (z % 2) + core


def rows_to_heads(grads, shards):
    rows, width = grads.shape
    pieces = grads.reshape(rows, shards, width // shards).transpose(1, 0, 2)
    pieces = lax.all_to_all(pieces, "shard", split_axis=0, concat_axis=0, tiled=True)
    return pieces.reshape(shards * rows, width // shards)


def hop(array, pairs):
    return lax.ppermute(array, "shard", pairs)


def weight_hop_one(own):
    if not split_trees():
        return (lax.all_gather(own, "shard", axis=0),)
    return hop(own, [(0, 1), (1, 2), (2, 3)]), hop(own, [(1, 0), (2, 1), (3, 2)])


def weight_last_hop(two):
    z = lax.axis_index("shard")
    return hop(jnp.where(z == 1, two[1], two[0]), [(1, 0), (2, 3)])


def weight_shards():
    z = lax.axis_index("shard")
    if not split_trees():
        return jnp.arange(lax.axis_size("shard"), dtype=jnp.int32)
    places = [
        z,
        jnp.where(z == 3, 2, z + 1),
        jnp.where(z == 0, 2, jnp.where(z == 3, 1, z - 1)),
        jnp.where(z < 2, 3, 0),
    ]
    return jnp.stack(places).astype(jnp.int32)


def greet(devices):
    barrier = pltpu.get_barrier_semaphore()
    for device in devices:
        pl.semaphore_signal(barrier, inc=1, device_id=device, device_id_type=pl.DeviceIdType.MESH)
    pl.semaphore_wait(barrier, len(devices))


def send_to(source, target, sems, number, device):
    return pltpu.make_async_remote_copy(
        src_ref=source,
        dst_ref=target,
        send_sem=sems.at[0, number],
        recv_sem=sems.at[1, number],
        device_id=device,
        device_id_type=pl.DeviceIdType.MESH,
    )


def other_places():
    column, z, core = (lax.axis_index(name) for name in ("expert", "shard", "dp"))
    others = [
        {"shard": z ^ number, "dp": core ^ side} for number in range(4) for side in range(2) if number + side
    ]
    return others + [{"expert": column ^ 1}, {"expert": column ^ 2}]


def chip_role():
    z = lax.axis_index("shard")
    tree = z // 2
    at_end = (z == 0) | (z == 3)
    partner = z ^ 1
    across = 3 - z
    return z, tree, at_end, partner, across, lambda number: jnp.where(tree == 0, number, 3 - number)


PIECES = 2


def gather_kernel(
    own, three, out, pack,
    rows, three_all, out_all, packs, three_mine, out_mine, passing, lent, here, sems,
):
    column, core = lax.axis_index("expert"), lax.axis_index("dp")
    z, tree, at_end, partner, across, seat = chip_role()
    in_middle = jnp.logical_not(at_end)
    beside, above, twin = {"expert": column ^ 1}, {"expert": column ^ 2}, {"dp": core ^ 1}
    to_partner, to_across = {"shard": partner}, {"shard": across}
    greet(near_places())
    keeps = core == tree
    lend = send_to(own.at[core ^ 1], lent, sems, 4, twin)
    lend.start()

    group = 2 * (z % 2) + core
    stays = (group == z) & keeps
    group_place = {"shard": 2 * core + z // 2, "dp": z % 2}
    local_three = pltpu.make_async_copy(three, three_mine, here.at[0])
    sent_three = send_to(three, three_mine, sems, 12, group_place)
    pl.when(stays)(local_three.start)
    pl.when(jnp.logical_not(stays))(sent_three.start)
    local_packs = [pltpu.make_async_copy(pack, packs.at[8 * n], here.at[5 + n]) for n in range(2)]
    pack_on = send_to(pack, packs.at[8], sems, 43, group_place)
    spread = [
        send_to(
            pack, packs.at[2 * n + side], sems, 35 + 2 * n + side,
            {"expert": column ^ n, "dp": core ^ side},
        )
        for n in range(4)
        for side in range(2)
        if n + side
    ]
    for copy in spread:
        copy.start()
    local_packs[0].start()
    pl.when(stays)(local_packs[1].start)
    pl.when(jnp.logical_not(stays))(pack_on.start)

    height = lent.shape[0] // PIECES
    piece = lambda ref, k: ref.at[pl.ds(k * height, height)]
    mine = lambda place, k: rows.at[place, core, pl.ds(k * height, height)]
    each = range(PIECES)

    def along(source, target, number, k, device, arrival=None):
        at = lambda n: 44 + PIECES * n + k
        return pltpu.make_async_remote_copy(
            src_ref=source,
            dst_ref=target,
            send_sem=sems.at[0, at(number)],
            recv_sem=sems.at[1, at(number if arrival is None else arrival)],
            device_id=device,
            device_id_type=pl.DeviceIdType.MESH,
        )

    def start_both(tree_rows, other_rows):
        @pl.when(at_end)
        def _():
            others = [along(piece(other_rows, k), piece(passing, k), 5, k, to_partner) for k in each]
            for copy in others:
                copy.start()
            for copy in others:
                copy.wait_send()
            for k in each:
                along(piece(tree_rows, k), mine(z, k), 0, k, to_partner).start()

        @pl.when(in_middle)
        def _():
            for k in each:
                along(piece(tree_rows, k), mine(z, k), 1, k, to_partner).start()
                along(piece(other_rows, k), mine(z, k), 2, k, to_across).start()

    lend.wait_recv()

    @pl.when(keeps)
    def _():
        start_both(own.at[core], lent)

    @pl.when(jnp.logical_not(keeps))
    def _():
        start_both(lent, own.at[core])

    whole_block = pltpu.make_async_copy(own, rows.at[z], here.at[1])
    block_to_twin = send_to(own, rows.at[z], sems, 11, twin)

    @pl.when(keeps)
    def _():
        whole_block.start()
        block_to_twin.start()

    keep = pltpu.make_async_copy(out, out_mine.at[z], here.at[3])
    keep.start()
    pieces = [send_to(out, out_mine.at[z], sems, 12 + n, {"shard": z ^ n}) for n in range(1, 4)]
    for copy in pieces:
        copy.start()

    pl.when(stays)(local_three.wait)
    pl.when(jnp.logical_not(stays))(sent_three.wait)
    quarter = three_mine.shape[0]
    half = quarter // 2

    def three_half(owner, side):
        return three_all.at[pl.ds(pl.multiple_of(owner * quarter + side * half, half), half)]

    top, bottom = three_mine.at[pl.ds(0, half)], three_mine.at[pl.ds(half, half)]
    first = [
        send_to(top, three_half(column, 0), sems, 16, beside),
        send_to(bottom, three_half(column, 1), sems, 17, above),
        send_to(bottom, three_half(column, 1), sems, 18, beside),
        send_to(top, three_half(column, 0), sems, 19, above),
    ]
    for copy in first:
        copy.start()
    local_all = pltpu.make_async_copy(
        three_mine, three_all.at[pl.ds(pl.multiple_of(column * quarter, quarter), quarter)], here.at[2]
    )
    local_all.start()

    def arrive(number, k):
        block = mine(seat(number), k)
        along(piece(lent, k), block, number, k, to_partner).wait_recv()
        along(block, block, 8 + number, k, twin).start()
        return block

    @pl.when(in_middle)
    def _():
        for k in each:
            along(piece(lent, k), piece(passing, k), 5, k, to_partner).wait_recv()
            along(piece(passing, k), mine(partner, k), 3, k, to_across).start()
            block = arrive(2, k)
            along(block, block, 6, k, to_partner, 2).start()

    @pl.when(at_end)
    def _():
        for k in each:
            arrive(1, k)

    keep.wait()
    for copy in pieces:
        copy.wait()
    halves = [out_mine.at[pl.ds(0, 2)], out_mine.at[pl.ds(2, 2)]]
    place = lambda owner, side, owner_core: out_all.at[pl.ds(2 * side, 2), owner, owner_core]
    third = [
        send_to(halves[0], place(column, 0, core), sems, 20, beside),
        send_to(halves[1], place(column, 1, core), sems, 21, above),
        send_to(halves[1], place(column, 1, core), sems, 22, beside),
        send_to(halves[0], place(column, 0, core), sems, 23, above),
    ]
    for copy in third:
        copy.start()
    whole = lambda owner, owner_core: out_all.at[:, owner, owner_core]
    keep_all = pltpu.make_async_copy(out_mine, whole(column, core), here.at[4])
    keep_all.start()
    to_twin = [send_to(out_mine, whole(column, core), sems, 31, twin)]
    to_twin[0].start()
    first[0].wait_recv()
    first[1].wait_recv()
    second = [
        send_to(three_half(column ^ 1, 0), three_half(column ^ 1, 0), sems, 24, above),
        send_to(three_half(column ^ 2, 1), three_half(column ^ 2, 1), sems, 25, beside),
    ]
    for copy in second:
        copy.start()

    @pl.when(in_middle)
    def _():
        for k in each:
            block = arrive(3, k)
            along(block, block, 7, k, to_partner, 3).start()
        for k in each:
            arrive(0, k)

    third[0].wait_recv()
    third[1].wait_recv()
    fourth = [
        send_to(place(column ^ 1, 0, core), place(column ^ 1, 0, core), sems, 26, above),
        send_to(place(column ^ 2, 1, core), place(column ^ 2, 1, core), sems, 27, beside),
    ]
    for copy in fourth:
        copy.start()

    @pl.when(at_end)
    def _():
        for k in each:
            arrive(2, k)

    third[2].wait_recv()
    third[3].wait_recv()
    for copy in fourth:
        copy.wait_recv()
    for number in range(1, 4):
        block = whole(column ^ number, core)
        to_twin.append(send_to(block, block, sems, 31 + number, twin))
        to_twin[number].start()
    local_all.wait()
    keep_all.wait()
    for copy in (first[2], first[3], second[0], second[1]):
        copy.wait_recv()
    for copy in first + second + third + fourth:
        copy.wait_send()
    for copy in to_twin:
        copy.wait()

    @pl.when(at_end)
    def _():
        for k in each:
            arrive(3, k)

    lend.wait_send()
    for copy in spread:
        copy.wait()
    local_packs[0].wait()
    pl.when(stays)(local_packs[1].wait)
    pl.when(jnp.logical_not(stays))(pack_on.wait)

    def settle(sent, traded):
        for k in each:
            for number in sent:
                along(piece(lent, k), mine(z, k), number, k, to_partner).wait_send()
            for number in traded:
                along(piece(lent, k), mine(z, k), 8 + number, k, twin).wait()

    pl.when(at_end)(functools.partial(settle, (0,), (1, 2, 3)))
    pl.when(in_middle)(functools.partial(settle, (1, 2, 3, 6, 7), (0, 2, 3)))

    @pl.when(keeps)
    def _():
        whole_block.wait()
        block_to_twin.wait_send()

    @pl.when(jnp.logical_not(keeps))
    def _():
        block_to_twin.wait_recv()


def exchange_call(kernel, operands, out_shape, sems, scratch, number, name, cost=5 * 10**10):
    anywhere = pl.BlockSpec(memory_space=pl.ANY)
    return pl.pallas_call(
        kernel,
        in_specs=[anywhere] * len(operands),
        out_specs=[anywhere] * len(out_shape),
        out_shape=[
            shape if hasattr(shape, "dtype") else jax.ShapeDtypeStruct(shape, jnp.bfloat16)
            for shape in out_shape
        ],
        scratch_shapes=list(scratch) + [pltpu.SemaphoreType.DMA((2, sems))],
        compiler_params=pltpu.CompilerParams(
            collective_id=number, has_side_effects=True, vmem_limit_bytes=48 << 20
        ),
        cost_estimate=pl.CostEstimate(flops=cost, bytes_accessed=10**6, transcendentals=0),
        name=name,
    )(*operands)


def gather_tree(own, three, out, pack):
    part, width = out.shape
    half = own.shape[0] // 2
    own = own.reshape(2, half, width)
    rows, three_all, out_all, packs, _, _, _, _ = exchange_call(
        gather_kernel,
        (own, three, out, pack),
        [
            (4, 2, half, width),
            (4 * three.shape[0], three.shape[1]),
            (4, 4, 2, part, width),
            jax.ShapeDtypeStruct((9,) + pack.shape, pack.dtype),
            three.shape,
            (4, part, width),
            (half, width),
            (half, width),
        ],
        44 + 12 * PIECES,
        [pltpu.SemaphoreType.DMA((7,))],
        2,
        "gather_tree",
    )
    return rows.reshape(-1, width), three_all, out_all.reshape(-1, width), packs


SLICES = 4


def heads_kernel(attended, heads, here, sems):
    z, core = lax.axis_index("shard"), lax.axis_index("dp")
    greet(other_places())
    tree, group = z // 2, 2 * (z % 2) + core
    rows = heads.shape[2]

    height = heads.shape[1] // SLICES

    def copies(turn, slice_number):
        place = (group + turn) % 4
        features = pl.ds(slice_number * height, height)
        piece = attended.at[features, pl.ds(pl.multiple_of(place * rows, TILE), rows)]
        target = heads.at[group, features]
        local = pltpu.make_async_copy(piece, target, here.at[slice_number])
        sent = send_to(piece, target, sems, turn * SLICES + slice_number, {"shard": place, "dp": tree})
        return local, sent, (place == z) & (tree == core)

    steps = [(turn, number) for turn in range(4) for number in range(SLICES)]
    for step in steps:
        local, sent, stays = copies(*step)
        pl.when(stays)(local.start)
        pl.when(jnp.logical_not(stays))(sent.start)
    for step in steps:
        local, sent, stays = copies(*step)
        pl.when(stays)(local.wait)
        pl.when(jnp.logical_not(stays))(sent.wait_send)
        from_me = ((z - step[0]) % 4 == group) & (tree == core)
        pl.when(jnp.logical_not(from_me))(sent.wait_recv)


def trade_heads(attended_t):
    columns, length = attended_t.shape
    (heads,) = exchange_call(
        heads_kernel,
        (attended_t,),
        [(4, columns, length // 4)],
        4 * SLICES,
        [pltpu.SemaphoreType.DMA((SLICES,))],
        3,
        "trade_heads",
    )
    return heads.reshape(4 * columns, length // 4)


def add_low(*blocks):
    return sum(block.astype(jnp.float32) for block in blocks).astype(jnp.bfloat16)


def near_places():
    column, core = lax.axis_index("expert"), lax.axis_index("dp")
    layer = [{"expert": column ^ n, "dp": core ^ side} for n in range(1, 4) for side in range(2)]
    return other_places()[:7] + layer


def ring_scatter(sums, halves, room, sems, base):
    column = lax.axis_index("expert")
    beside, above = {"expert": column ^ 1}, {"expert": column ^ 2}
    first = [
        send_to(halves(sums, column ^ 3, 0), room.at[0], sems, base, beside),
        send_to(halves(sums, column ^ 3, 1), room.at[1], sems, base + 1, above),
        send_to(halves(sums, column ^ 1, 0), room.at[2], sems, base + 2, beside),
        send_to(halves(sums, column ^ 2, 1), room.at[3], sems, base + 3, above),
    ]
    for copy in first:
        copy.start()
    second = [
        send_to(room.at[0], room.at[4], sems, base + 4, above),
        send_to(room.at[1], room.at[5], sems, base + 5, beside),
    ]

    def onward():
        for number, (owner, side) in enumerate(((column ^ 2, 0), (column ^ 1, 1))):
            first[number].wait_recv()
            room[number] = add_low(halves(sums, owner, side)[...], room[number])
            second[number].start()

    def terms():
        for copy in (first[2], first[3], second[0], second[1]):
            copy.wait_recv()
        low = (halves(sums, column, 0)[...], room[2], room[4])
        high = (halves(sums, column, 1)[...], room[3], room[5])
        return low, high

    def finish():
        for copy in first + second:
            copy.wait_send()

    return onward, terms, finish


def back_kernel(
    grads, out, heads, out_sum, lent, sums, room, quarter, pieces, total, here, sems
):
    column, core = lax.axis_index("expert"), lax.axis_index("dp")
    z, tree, at_end, partner, across, seat = chip_role()
    twin = {"dp": core ^ 1}
    greet(near_places())
    group = 2 * (z % 2) + core
    columns = heads.shape[2]
    part = lent.shape[2]
    lend = send_to(out.at[:, :, pl.ds((core ^ 1) * part, part)], lent, sems, 4, twin)
    lend.start()

    height = heads.shape[1] // SLICES

    def turn_copies(turn, k):
        to_group = (z - turn) % 4
        rows = pl.ds(k * height, height)
        piece = grads.at[rows, pl.ds(pl.multiple_of(to_group * columns, TILE), columns)]
        place, side = 2 * core + to_group // 2, to_group % 2
        target = heads.at[z, rows]
        local = pltpu.make_async_copy(piece, target, here.at[3 + k])
        sent = send_to(piece, target, sems, 21 + turn * SLICES + k, {"shard": place, "dp": side})
        return local, sent, (place == z) & (side == core)

    steps = [(turn, k) for turn in range(4) for k in range(SLICES)]
    for step in steps:
        local, sent, stays = turn_copies(*step)
        pl.when(stays)(local.start)
        pl.when(jnp.logical_not(stays))(sent.start)

    mine = pltpu.make_async_copy(out.at[:, :, pl.ds(core * part, part)], sums, here.at[1])
    mine.start()
    mine.wait()
    lend.wait_recv()
    sums[...] = add_low(sums[...], lent[...])

    def halves(ref, owner, side):
        return ref.at[pl.ds(2 * side, 2), owner]

    onward, terms, finish = ring_scatter(sums, halves, room, sems, 5)
    onward()
    low, high = terms()
    quarter[:2] = add_low(*low)
    quarter[2:] = add_low(*high)
    copies = [
        send_to(quarter.at[z ^ n], pieces.at[n - 1], sems, 10 + n, {"shard": z ^ n}) for n in range(1, 4)
    ]
    for copy in copies:
        copy.start()
    for copy in copies:
        copy.wait()
    total[...] = add_low(quarter[z], pieces[0], pieces[1], pieces[2])
    spread = [
        send_to(
            total, out_sum.at[column, core], sems, 13 + 2 * n + side,
            {"expert": column ^ n, "dp": core ^ side},
        )
        for n in range(4)
        for side in range(2)
        if n + side
    ]
    for copy in spread:
        copy.start()
    keep = pltpu.make_async_copy(total, out_sum.at[column, core], here.at[2])
    keep.start()
    keep.wait()
    for copy in spread:
        copy.wait()
    finish()
    lend.wait_send()
    for step in steps:
        local, sent, stays = turn_copies(*step)
        pl.when(stays)(local.wait)
        pl.when(jnp.logical_not(stays))(sent.wait_send)
        from_me = ((group + step[0]) % 4 == z) & (tree == core)
        pl.when(jnp.logical_not(from_me))(sent.wait_recv)


def trade_back(grads, out):
    rows, width = grads.shape
    part = width // 32
    low = jnp.bfloat16
    heads, out_sum = exchange_call(
        back_kernel,
        (grads, out.reshape(4, 4, 2 * part, width)),
        [(4, rows, width // 4), (4, 2, part, width)],
        21 + 4 * SLICES,
        [
            pltpu.VMEM((4, 4, part, width), low),
            pltpu.VMEM((4, 4, part, width), low),
            pltpu.VMEM((6, 2, part, width), low),
            pltpu.VMEM((4, part, width), low),
            pltpu.VMEM((3, part, width), low),
            pltpu.VMEM((part, width), low),
            pltpu.SemaphoreType.DMA((3 + SLICES,)),
        ],
        4,
        "trade_back",
        10**6,
    )
    return heads.reshape(4 * rows, width // 4), out_sum.reshape(-1, width)


def last_kernel(
    parts, three, small, total, three_all, small_all,
    lent, forth, arrived, leave, room, quarter, moved, other, mine_half, small_room, here, sems,
):
    column, core = lax.axis_index("expert"), lax.axis_index("dp")
    z, tree, at_end, partner, across, seat = chip_role()
    in_middle = jnp.logical_not(at_end)
    twin, to_partner, to_across = {"dp": core ^ 1}, {"shard": partner}, {"shard": across}
    greet(near_places())
    keeps = core == tree

    def lend(turn):
        block = seat(jnp.where(at_end, 3 - turn, (4 - turn) % 4))
        return block, send_to(parts.at[block, core ^ 1], lent.at[block], sems, turn, twin)

    height = lent.shape[1] // PIECES
    each = range(PIECES)
    piece = lambda ref, k: ref.at[pl.ds(k * height, height)]

    def along(source, target, number, device, arrival=None):
        at = lambda n, k: 33 + PIECES * n + k
        return [
            pltpu.make_async_remote_copy(
                src_ref=piece(source, k),
                dst_ref=piece(target, k),
                send_sem=sems.at[0, at(number, k)],
                recv_sem=sems.at[1, at(number if arrival is None else arrival, k)],
                device_id=device,
                device_id_type=pl.DeviceIdType.MESH,
            )
            for k in each
        ]

    def start_all(copies):
        for copy in copies:
            copy.start()

    for turn in range(4):
        lend(turn)[1].start()
    rows = three.shape[1] // 2

    def halves(ref, owner, side):
        return ref.at[owner, pl.ds(side * rows, rows)]

    onward, terms, finish = ring_scatter(three, halves, room, sems, 4)
    partners = [
        twin, {"expert": column ^ 1}, {"expert": column ^ 2}, {"shard": z ^ 1}, {"shard": z ^ 2}
    ]
    small_all[...] = small[...]

    def small_copy(stage):
        return send_to(small_room.at[stage], small_room.at[5 + stage], sems, 20 + stage, partners[stage])

    def small_start(stage):
        small_room[stage] = small_all[...]
        small_copy(stage).start()

    def small_end(stage):
        small_copy(stage).wait()
        small_all[...] += small_room[5 + stage]

    small_start(0)

    def chip_sum(turn):
        block, copy = lend(turn)
        copy.wait_recv()
        lent[block] = add_low(parts[block, core], lent[block])
        return lent.at[block]

    def end_send(turn):
        start_all(along(chip_sum(turn), forth.at[turn], turn, to_partner))

    pl.when(at_end)(functools.partial(end_send, 0))

    @pl.when(in_middle)
    def _():
        start_all(along(chip_sum(0), forth.at[0], 0, to_partner))

    small_end(0)
    small_start(1)
    onward()
    pl.when(at_end)(functools.partial(end_send, 1))
    small_end(1)
    small_start(2)

    def middle_sum(turn, onwards=None):
        block = chip_sum(turn)
        copies = None if onwards is None else onwards(block)
        for k, arrival in enumerate(along(forth.at[0], forth.at[turn - 1], turn - 1, to_partner)):
            arrival.wait_recv()
            at = pl.ds(k * height, height)
            block[at] = add_low(block[at], forth[turn - 1, at])
            if copies is not None:
                copies[k].start()

    @pl.when(in_middle)
    def _():
        middle_sum(1, lambda block: along(block, arrived, 3, {"shard": across ^ 1}))

    low, high = terms()
    quarter[:rows] = add_low(*low)
    quarter[rows:] = add_low(*high)
    group = 2 * (z % 2) + core
    stays = (group == z) & keeps
    keep = pltpu.make_async_copy(quarter, moved, here.at[0])
    move_on = send_to(quarter, moved, sems, 14, {"shard": group, "dp": tree})
    pl.when(stays)(keep.start)
    pl.when(jnp.logical_not(stays))(move_on.start)
    pl.when(at_end)(functools.partial(end_send, 2))

    small_end(2)
    small_start(3)

    @pl.when(in_middle)
    def _():
        middle_sum(2, lambda block: along(block, arrived, 4, to_across, 3))

    pl.when(stays)(keep.wait)
    pl.when(jnp.logical_not(stays))(move_on.wait)
    swapped = send_to(moved, other, sems, 16, twin)
    swapped.start()
    small_end(3)
    small_start(4)
    swapped.wait()
    at = pl.ds(pl.multiple_of(core * rows, 8), rows)
    mine_half[...] = add_low(moved[at], other[at])
    target = three_all.at[column, core]
    spread = [
        send_to(mine_half, target, sems, 25 + 2 * n + side, {"expert": column ^ n, "dp": core ^ side})
        for n in range(4)
        for side in range(2)
        if n + side
    ]
    for copy in spread:
        copy.start()
    keep_half = pltpu.make_async_copy(mine_half, target, here.at[1])
    keep_half.start()
    small_end(4)

    @pl.when(at_end)
    def _():
        block = chip_sum(3)
        for copy in along(forth.at[0], forth.at[0], 0, to_partner):
            copy.wait_recv()
        block[...] = add_low(block[...], forth[0])

    @pl.when(in_middle)
    def _():
        middle_sum(3)

    mine = lent.at[z]
    for copy in along(forth.at[0], arrived, 3, to_partner):
        copy.wait_recv()

    @pl.when(keeps)
    def _():
        total[core] = mine[...]
        leave[...] = arrived[...]

    @pl.when(jnp.logical_not(keeps))
    def _():
        total[core] = arrived[...]
        leave[...] = mine[...]

    last = send_to(leave, total.at[core], sems, 17, twin)
    last.start()

    keep_half.wait()
    for copy in spread:
        copy.wait()
    finish()
    for turn in range(4):
        lend(turn)[1].wait_send()

    def settle(numbers):
        for number in numbers:
            for copy in along(forth.at[0], forth.at[1], number, to_partner):
                copy.wait_send()

    pl.when(at_end)(functools.partial(settle, (0, 1, 2)))
    pl.when(in_middle)(functools.partial(settle, (0, 3, 4)))
    last.wait()


def reduce_last(parts, three, small):
    blocks, rows, width = parts.shape
    columns = three.shape[1]
    half, quarter = rows // 2, width // 4
    low = jnp.bfloat16
    vmem = pl.BlockSpec(memory_space=pltpu.VMEM)
    block = pltpu.VMEM((half, width), low)
    total, three_all, small_all = pl.pallas_call(
        last_kernel,
        in_specs=[vmem] * 3,
        out_specs=[vmem] * 3,
        out_shape=[
            jax.ShapeDtypeStruct((2, half, width), low),
            jax.ShapeDtypeStruct((4, 2, quarter // 2, columns), low),
            jax.ShapeDtypeStruct(small.shape, jnp.float32),
        ],
        scratch_shapes=[
            pltpu.VMEM((4, half, width), low),
            pltpu.VMEM((3, half, width), low),
            block,
            block,
            pltpu.VMEM((6, quarter // 2, columns), low),
            pltpu.VMEM((quarter, columns), low),
            pltpu.VMEM((quarter, columns), low),
            pltpu.VMEM((quarter, columns), low),
            pltpu.VMEM((quarter // 2, columns), low),
            pltpu.VMEM((10,) + small.shape, jnp.float32),
            pltpu.SemaphoreType.DMA((2,)),
            pltpu.SemaphoreType.DMA((2, 33 + 5 * PIECES)),
        ],
        compiler_params=pltpu.CompilerParams(
            collective_id=5, has_side_effects=True, vmem_limit_bytes=48 << 20
        ),
        cost_estimate=pl.CostEstimate(flops=5 * 10**10, bytes_accessed=10**7, transcendentals=0),
        name="reduce_last",
    )(parts.reshape(blocks, 2, half, width), three.reshape(4, quarter, columns), small)
    return total.reshape(rows, width), three_all.reshape(width, columns), small_all


def meet_kernel(rows, own, up_one, down_one, layer, theirs, up_two, down_two, sems):
    column, z = lax.axis_index("expert"), lax.axis_index("shard")
    beside, above = {"expert": column ^ 1}, {"expert": column ^ 2}
    twin = {"dp": lax.axis_index("dp") ^ 1}
    greet(other_places())
    x_top = send_to(rows.at[0], layer.at[0], sems, 0, beside)
    y_bottom = send_to(rows.at[1], layer.at[3], sems, 1, above)
    x_bottom = send_to(rows.at[1], layer.at[1], sems, 2, beside)
    y_top = send_to(rows.at[0], layer.at[2], sems, 3, above)
    for copy in (x_top, y_bottom, x_bottom, y_top):
        copy.start()

    between = (z == 1) | (z == 2)
    hop_up = [send_to(up_one.at[m], up_two.at[m], sems, 12 + m, {"shard": z + 1}) for m in range(3)]
    hop_down = [send_to(down_one.at[m], down_two.at[m], sems, 15 + m, {"shard": z - 1}) for m in range(3)]

    @pl.when(between)
    def _():
        for copy in hop_up + hop_down:
            copy.start()

    low, high = z == 0, z == 3

    def to_twin(view, place):
        return send_to(view, theirs.at[place], sems, 8 + place, twin)

    to_twin(own, 0).start()
    pl.when(z < 3)(to_twin(down_one, 1).start)
    pl.when(high)(to_twin(up_one, 1).start)
    pl.when(between)(to_twin(up_one, 2).start)

    x_top.wait_recv()
    far_top = send_to(layer.at[0], layer.at[4], sems, 4, above)
    far_top.start()
    y_bottom.wait_recv()
    far_bottom = send_to(layer.at[3], layer.at[5], sems, 5, beside)
    far_bottom.start()

    for copy in (x_top, y_bottom):
        copy.wait_send()
    for copy in (x_bottom, y_top, far_top, far_bottom):
        copy.wait()

    @pl.when(z >= 2)
    def _():
        for copy in hop_up:
            copy.wait_recv()

    @pl.when(z <= 1)
    def _():
        for copy in hop_down:
            copy.wait_recv()

    pl.when(low)(to_twin(down_two, 2).start)
    pl.when(high)(to_twin(up_two, 2).start)
    pl.when(z == 1)(to_twin(down_two, 3).start)
    pl.when(z == 2)(to_twin(up_two, 3).start)

    @pl.when(between)
    def _():
        for copy in hop_up + hop_down:
            copy.wait_send()
        to_twin(own, 3).wait()

    for place in range(3):
        to_twin(own, place).wait()


def meet(rows, own, one):
    half = rows.shape[0] // 2
    halves = rows.reshape(2, half, rows.shape[1])
    layer, theirs, up_two, down_two = exchange_call(
        meet_kernel,
        (halves, own, *one),
        [(6,) + halves.shape[1:], (4,) + own.shape, own.shape, own.shape],
        18,
        [],
        1,
        "meet",
    )
    return [halves, layer], theirs, (up_two, down_two)


def heads_to_rows(attended_t, shards):
    columns, length = attended_t.shape
    pieces = attended_t.reshape(columns, shards, length // shards).transpose(1, 0, 2)
    pieces = lax.all_to_all(pieces, "shard", split_axis=0, concat_axis=0, tiled=True)
    return pieces.reshape(shards * columns, length // shards)


def on_device(
    tokens, teacher, seg_ids, parents, depth, valid, routes, norm1_gain, w_query, w_key, w_value,
    w_out, rel_bias, norm2_gain, router, w_gate, w_up, w_down,
):
    shard_index = lax.axis_index("shard")
    expert_index = lax.axis_index("expert")
    shards = lax.axis_size("shard")
    columns = lax.axis_size("expert")
    experts = columns * w_gate.shape[0]
    token_rows = tokens[0].astype(jnp.float32)
    local_rows, width = token_rows.shape
    length = seg_ids.shape[1]
    bucket_count = rel_bias.shape[0]
    validity = valid[0]
    route_rows = routes[0]

    row_start = shard_index * local_rows
    valid_local = lax.dynamic_slice_in_dim(validity, row_start, local_rows, 0).astype(jnp.float32)
    route_local = lax.dynamic_slice_in_dim(route_rows, row_start, local_rows, 0)

    scale_one = lax.rsqrt(jnp.mean(token_rows * token_rows, axis=1, keepdims=True) + EPSILON)
    base_one = token_rows * scale_one
    normed_one = (base_one * norm1_gain).astype(jnp.bfloat16)
    expert_w = jnp.stack([w_gate[0].T, w_up[0].T, w_down[0]])
    half = expert_w.shape[1] // lax.axis_size("dp")
    expert_w = lax.dynamic_slice_in_dim(expert_w, lax.axis_index("dp") * half, half, 1)
    weights = jnp.concatenate([w_query, w_key, w_value], axis=1)
    info, bias_here = attention_info(validity), rel_bias
    top_count = route_local.shape[1]
    if split_trees():
        quarter, part = width // 4, w_out.shape[0] // 8
        info_row = jnp.pad(info, (0, TILE - INFO_SIZE))
        rows_of = lambda values: values.astype(jnp.float32).reshape(-1, TILE)
        pack = jnp.concatenate([rows_of(info_row), rows_of(rel_bias), rows_of(route_local.T)], axis=0)
        pack = jnp.pad(pack, ((0, -pack.shape[0] % 8), (0, 0)))
        normed_all, weights, out_all, packs = gather_tree(
            normed_one,
            lax.dynamic_slice_in_dim(weights, expert_index * quarter, quarter, 0),
            lax.dynamic_slice_in_dim(
                w_out, (expert_index * 2 + lax.axis_index("dp")) * part, part, 0
            ),
            pack,
        )
        expert_w, packs = lax.optimization_barrier((expert_w, packs))
        tree_rows = packs[:, 0, :INFO_SIZE].astype(jnp.int32)
        z, core, tree, group = my_place()
        info = jnp.where(core == tree, tree_rows[0], tree_rows[1])
        valid_total = jnp.sum(tree_rows[:8, INFO_SIZE - 1]).astype(jnp.float32)
        bias_rows = rel_bias.size // TILE
        bias_here = packs[8, 1 : 1 + bias_rows].reshape(rel_bias.shape)
        route_rows = route_local.size // TILE
        route_layer = packs[0:8:2, 1 + bias_rows : 1 + bias_rows + route_rows]
        route_layer = route_layer.reshape(columns, top_count, local_rows).astype(jnp.int32)
    else:
        normed_all = lax.all_gather(normed_one, "shard", axis=0, tiled=True)
        out_all = lax.all_gather(w_out, "shard", axis=0, tiled=True)
        normed_all, expert_w = lax.optimization_barrier((normed_all, expert_w))
        tree_count = sum_over(jnp.broadcast_to(jnp.sum(validity), (8, 128)), ("dp", "expert"))
        valid_total = tree_count[0, 0].astype(jnp.float32)
        route_layer = layer_small(route_local.T)
    weights_one = weight_hop_one(expert_w)
    query_rows, key_rows, key_t, value_rows, value_t = project(weights, normed_all)

    taken = jnp.any(route_layer == expert_index, axis=1)
    order = jnp.cumsum(taken.reshape(-1).astype(jnp.int32))
    slots = jnp.where(taken, order.reshape(taken.shape) - 1, -1)
    half_blocks = 2 * columns if ring_layer() else columns
    block_rows = columns * local_rows // half_blocks
    slots = slots.reshape(half_blocks, block_rows)
    named = route_layer.transpose(0, 2, 1).reshape(half_blocks, block_rows, top_count)
    scalars = jnp.concatenate(
        [jnp.zeros((1,), jnp.int32), order[block_rows - 1 :: block_rows], expert_index[None].astype(jnp.int32)]
    )

    table = bias_table(bias_here)
    attended_t, log_totals = attention_forward(info, table, query_rows, key_rows, value_t)

    if split_trees():
        attended_here = trade_heads(attended_t)
    else:
        attended_here = heads_to_rows(attended_t, shards)
    update = lax.dot_general(
        attended_here, out_all, (((0,), (0,)), ((), ())), preferred_element_type=jnp.float32
    )
    hidden = token_rows + update

    scale_two = lax.rsqrt(jnp.mean(hidden * hidden, axis=1, keepdims=True) + EPSILON)
    base_two = hidden * scale_two
    normed_two = (base_two * norm2_gain).astype(jnp.bfloat16)

    expert_ids = jnp.arange(experts, dtype=jnp.int32)
    router_pieces = split_float(router)

    def gates_of(rows, named):
        logits = join_float(jnp.dot(rows, router_pieces, preferred_element_type=jnp.float32), experts)
        match = named[:, :, None] == expert_ids[None, None, :]
        chosen = jnp.sum(jnp.where(match, logits[:, None, :], 0.0), axis=2)
        return jax.nn.softmax(chosen, axis=1), match

    gates, route_match = gates_of(normed_two, route_local)
    if split_trees():
        normed_layer, theirs_w, weights_two = meet(normed_two, expert_w, weights_one)
        weights_near = (theirs_w, expert_w, *weights_one, *weights_two)
        far = weight_last_hop(weights_two)
    else:
        normed_layer = [block[None] for block in layer_gather(normed_two)]
        weights_all = (swap(weights_one[0], "dp", 1), weights_one[0])
    expert_scalars = jnp.concatenate(
        [order[-1:], shard_index[None].astype(jnp.int32), weight_shards()]
    )
    router_wide = jnp.pad(router_pieces, ((0, 0), (0, TILE - router_pieces.shape[1])))
    expert_rows, gate_here = compact_rows(scalars, router_wide, slots, named, normed_layer, experts)
    if split_trees():
        produced = expert_forward(expert_scalars, expert_rows, weights_near, 0, 3)
        produced, far = lax.optimization_barrier((produced, far))
        weights_all = weights_near + (far, swap(far, "dp", 1))
        shares, produced_layer = expert_forward(
            expert_scalars, expert_rows, weights_all, 3, 1, produced, scalars, slots, gate_here
        )
    else:
        produced = expert_forward(expert_scalars, expert_rows, weights_all, 0, shards)
        shares, produced_layer = expand(scalars, slots, produced, gate_here)
    combined = layer_scatter(shares)

    output_rows = hidden + combined
    factor = length * columns * lax.axis_size("dp") / valid_total
    error = output_rows - teacher[0].astype(jnp.float32)
    error_sum = jnp.sum(valid_local[:, None] * error * error)
    grad_output = valid_local[:, None] * error * factor
    grad_layer = [block[None] for block in layer_gather(grad_output.astype(jnp.bfloat16))]
    grad_rows, gate_grads = compact_grads(scalars, slots, gate_here, produced_layer, grad_layer)
    gate_grads = layer_trade(gate_grads.reshape(columns, local_rows))
    mine_gate, theirs_gate, mine_rest, theirs_rest, rows_grad = expert_backward(
        expert_scalars, expert_rows, grad_rows, weights_all
    )
    theirs_gate = swap(theirs_gate, "dp", 1)
    rows_grad, theirs_gate = lax.optimization_barrier(
        (expand(scalars, slots, rows_grad), theirs_gate)
    )
    rows_grad, gate_part = lax.optimization_barrier((rows_grad, mine_gate + theirs_gate))
    gate_part = lax.psum_scatter(gate_part, "shard", scatter_dimension=0, tiled=False)
    theirs_rest = swap(theirs_rest, "dp", 1)
    expert_back = layer_scatter(rows_grad)

    members = jnp.stack([jnp.asarray(layer_member(number), jnp.int32) for number in range(columns)])
    grad_gates = jnp.sum(
        jnp.where(route_local[:, :, None] == members[None, None, :], gate_grads.T[:, None, :], 0.0), axis=2
    )
    weighted = jnp.sum(gates * grad_gates, axis=1, keepdims=True)
    grad_chosen = gates * (grad_gates - weighted)
    grad_logits = jnp.sum(jnp.where(route_match, grad_chosen[:, :, None], 0.0), axis=1)
    router_grad = join_float(
        lax.dot_general(
            normed_two, split_float(grad_logits), (((0,), (0,)), ((), ())),
            preferred_element_type=jnp.float32,
        ),
        experts,
    )
    grad_normed_two = expert_back
    for number in range(experts):
        grad_normed_two = grad_normed_two + grad_logits[:, number : number + 1] * router[:, number][None]
    grad_base_two = grad_normed_two * norm2_gain
    norm2_grad = jnp.sum(grad_normed_two * base_two, axis=0)
    grad_hidden = grad_output + scale_two * (
        grad_base_two - base_two * jnp.mean(grad_base_two * base_two, axis=1, keepdims=True)
    )
    grad_update = grad_hidden.astype(jnp.bfloat16)
    out_grad = jnp.dot(attended_here, grad_update, preferred_element_type=jnp.float32)
    grad_heads = lax.dot_general(
        grad_update, out_all, (((1,), (1,)), ((), ())), preferred_element_type=jnp.float32
    ).astype(jnp.bfloat16)
    out_grad = out_grad.astype(jnp.bfloat16)
    if split_trees():
        grad_attended, out_grad = trade_back(grad_heads, out_grad)
    else:
        grad_attended = rows_to_heads(grad_heads, shards)
        out_grad = lax.psum_scatter(out_grad, "shard", scatter_dimension=0, tiled=True)
        out_grad = lax.psum(out_grad, ("expert", "dp"))
    out_grad = out_grad.astype(jnp.float32)
    rest_part, grad_attended, gate_part = lax.optimization_barrier(
        (mine_rest + theirs_rest, grad_attended, gate_part)
    )
    rest_part = lax.psum_scatter(rest_part, "shard", scatter_dimension=0, tiled=False)

    grad_queries_t, grad_keys, grad_values, ahead, behind = attention_backward(
        info, table, query_rows, key_rows, key_t, value_rows, grad_attended, attended_t, log_totals
    )
    bias_grad = bias_gradient(ahead, behind, info[OFFSET_AT : OFFSET_AT + CLASSES], bucket_count)
    grad_normed_all, three_wgrad, norm1_grad = last_products(
        normed_all, weights, grad_queries_t, grad_keys, grad_values
    )
    norm1_grad = norm1_grad[0] / norm1_gain

    heads_here = bias_grad.shape[1]
    group = my_place()[3] if split_trees() else shard_index
    bias_all = lax.dynamic_update_slice_in_dim(
        jnp.zeros((bucket_count, heads_here * shards), jnp.float32), bias_grad, group * heads_here, 1
    )
    bias_line = jnp.pad(bias_all.reshape(-1), (0, width - bias_all.size))
    small = jnp.concatenate(
        [router_grad.T, norm2_grad[None], norm1_grad[None], bias_line[None], jnp.full((1, width), error_sum)],
        axis=0,
    )
    if split_trees():
        grad_normed_one, three_wgrad, small = reduce_last(
            grad_normed_all.reshape(shards, local_rows, width), three_wgrad, small
        )
    else:
        grad_normed_one = lax.psum_scatter(grad_normed_all, "shard", scatter_dimension=0, tiled=True)
        three_wgrad = lax.psum(three_wgrad, ("expert", "dp"))
        small = sum_over(small, ("dp", "expert", "shard"))
    three_wgrad = three_wgrad.astype(jnp.float32)
    query_wgrad, key_wgrad, value_wgrad = jnp.split(three_wgrad, 3, axis=1)
    router_grad, norm2_grad, norm1_grad = small[:experts].T, small[experts], small[experts + 1]
    bias_all = small[experts + 2, : bias_all.size].reshape(bias_all.shape)
    bias_grad = lax.dynamic_slice_in_dim(bias_all, shard_index * heads_here, heads_here, 1)
    error_total = small[experts + 3, 0]
    grad_normed_one = grad_normed_one.astype(jnp.float32)
    grad_base_one = grad_normed_one * norm1_gain
    grad_tokens = grad_hidden + scale_one * (
        grad_base_one - base_one * jnp.mean(grad_base_one * base_one, axis=1, keepdims=True)
    )
    loss = error_total / (width * valid_total)

    first_core = lax.axis_index("dp") == 0

    def both_halves(mine):
        other = swap(mine, "dp", 1)
        halves = [jnp.where(first_core, mine, other), jnp.where(first_core, other, mine)]
        return jnp.concatenate(halves, axis=1).astype(jnp.float32)

    gate_grad, rest_grad = both_halves(gate_part)[0].T[None], both_halves(rest_part)
    up_grad, down_grad = rest_grad[0].T[None], rest_grad[1][None]
    return (
        output_rows.astype(jnp.bfloat16)[None],
        loss,
        grad_tokens[None],
        norm1_grad,
        query_wgrad,
        key_wgrad,
        value_wgrad,
        out_grad,
        bias_grad,
        norm2_grad,
        router_grad,
        gate_grad,
        up_grad,
        down_grad,
    )


def solution(mesh):
    in_specs = (
        P(("expert", "dp"), "shard", None),
        P(("expert", "dp"), "shard", None),
        P(("expert", "dp"), None),
        P(("expert", "dp"), None),
        P(("expert", "dp"), None),
        P(("expert", "dp"), None),
        P(("expert", "dp"), None, None),
        P(),
        P(None, "shard"),
        P(None, "shard"),
        P(None, "shard"),
        P("shard", None),
        P(None, "shard"),
        P(),
        P(),
        P("expert", None, "shard"),
        P("expert", None, "shard"),
        P("expert", "shard", None),
    )
    out_specs = (
        P(("expert", "dp"), "shard", None),
        P(),
        P(("expert", "dp"), "shard", None),
        P(),
        P(None, "shard"),
        P(None, "shard"),
        P(None, "shard"),
        P("shard", None),
        P(None, "shard"),
        P(),
        P(),
        P("expert", None, "shard"),
        P("expert", None, "shard"),
        P("expert", "shard", None),
    )
    return jax.shard_map(
        on_device, mesh=mesh, in_specs=in_specs, out_specs=out_specs, check_vma=False
    )
```
